32 devices in a mesh: row: 4 (over z), col: 8 (over y, x, core).
Axes of the slice: x: 2, y: 2, z: 4, core: 2. Of those that a mesh axis runs over, the one named last changes fastest.
Arguments:
- image_feats: bfloat16 [18432, 6144], P(('row', 'col')), may hold values from -6 to 6
- text_feats: bfloat16 [18432, 4096], P(('row', 'col')), may hold values from -6 to 6
- probe_image: bfloat16 [6144, 128], P('row'), may hold values from -0.078125 to 0.078125
- probe_text: bfloat16 [4096, 128], P('col'), may hold values from -0.09375 to 0.09375
Outputs:
- image_basis: float32 [6144, 128], P('row')
- text_basis: float32 [4096, 128], P('col')
The draws below stay inside these ranges and needn't reach their ends.
All inputs are finite; a program needn't handle non-finite values.
Results may differ from the reference program's by a relative error of at most 0.0031.
Values may be sent and summed in bfloat16 or wider, within the bound.
No kernel may reach another device: no remote copies, remote signals or barrier semaphores. Data moves between devices by JAX's collectives and lax.ppermute only.
A program may use at most 64 MiB of HBM per device.

```python
import math
import jax
import jax.numpy as jnp
from jax import lax

DX = 6144
DY = 4096
RANK = 128
PAIRS = 18432


def raised(array, rng, source, target, parts, factor):
    def block_of(dim):
        return (jnp.arange(array.shape[dim]) // (array.shape[dim] // parts)).reshape((-1,) + (1,) * (array.ndim - 1 - dim))

    one_side = jax.random.permutation(rng, parts)[block_of(target)]
    second = (block_of(target) + parts // 2) % parts
    return jnp.where((block_of(source) == one_side) | (block_of(source) == second), factor * array, array)


def steps_of(own_key, shape, split, low, top_value):
    def one(dim, shards_of):
        steps = jax.random.uniform(jax.random.fold_in(jax.random.fold_in(own_key, 6), dim), (shards_of,), jnp.float32, low / len(split), top_value / len(split))
        return jnp.repeat(jnp.exp(steps), shape[dim] // shards_of).reshape((-1,) + (1,) * (len(shape) - dim - 1))

    factor_of = one(*split[0])
    for cut in split[1:]:
        factor_of = factor_of * one(*cut)
    return factor_of


def normal_values(own_key, shape, scale, bound, split=(), kind=jnp.bfloat16):
    drawn = scale * jax.random.normal(own_key, shape, jnp.float32)
    if split:
        drawn = drawn * steps_of(own_key, shape, split, -0.22, 0.18)
    return jnp.clip(drawn, -bound, bound).astype(kind)


def gaussian_with(rng, extent, deviation, most, split, heavy, held_as=jnp.bfloat16):
    values = deviation * jax.random.normal(rng, extent, jnp.float32)
    if split:
        values = values * steps_of(rng, extent, split, -0.22, 0.18)
    return jnp.clip(raised(values, jax.random.fold_in(rng, 3), *heavy), -most, most).astype(held_as)


def setup_inputs(seed: int = 0) -> dict:
    key_list = jax.random.split(jax.random.key(seed), 5)
    return {
        "image_feats": gaussian_with(key_list[0], (PAIRS, DX), 1.0, 6.0, ((0, 32),), (0, 1, 32, 2.75)),
        "text_feats": gaussian_with(key_list[1], (PAIRS, DY), 1.0, 6.0, ((0, 32),), (0, 1, 32, 2.75)),
        "probe_image": normal_values(key_list[2], (DX, RANK), DX ** -0.5, 0.078125, ((0, 4),)),
        "probe_text": normal_values(key_list[3], (DY, RANK), DY ** -0.5, 0.09375, ((0, 8),)),
    }


def orthonormal(panel, width):
    gram = jnp.dot(panel.T.astype(jnp.float32), panel.astype(jnp.float32), precision=lax.Precision.HIGHEST, preferred_element_type=jnp.float32)
    factor = jnp.linalg.cholesky(gram)
    basis = lax.linalg.triangular_solve(factor, panel, left_side=False, lower=True, transpose_a=True)
    return basis * math.sqrt(width)

def reference(image_feats, text_feats, probe_image, probe_text):
    sketch_text = jnp.dot(text_feats.astype(jnp.float32), probe_text.astype(jnp.float32), preferred_element_type=jnp.float32).astype(jnp.bfloat16)
    sketch_image = jnp.dot(image_feats.astype(jnp.float32), probe_image.astype(jnp.float32), preferred_element_type=jnp.float32).astype(jnp.bfloat16)
    dims = (((0,), (0,)), ((), ()))
    image_panel = lax.dot_general(image_feats.astype(jnp.float32), sketch_text.astype(jnp.float32), dims, preferred_element_type=jnp.float32)
    text_panel = lax.dot_general(text_feats.astype(jnp.float32), sketch_image.astype(jnp.float32), dims, preferred_element_type=jnp.float32)
    return (orthonormal(image_panel, DX), orthonormal(text_panel, DY))
```

```python
import functools
import math

import jax
import jax.numpy as jnp
from jax import lax
from jax.experimental import pallas as pl
from jax.experimental.pallas import tpu as pltpu
from jax.sharding import PartitionSpec as P

F32 = jnp.float32
BF16 = jnp.bfloat16
VMEM = pl.BlockSpec(memory_space=pltpu.VMEM)
SMEM = pl.BlockSpec(memory_space=pltpu.SMEM)
LIMIT = 48 * 1024 * 1024


def sds(shape, dtype):
    return jax.ShapeDtypeStruct(shape, dtype)


def params(**kw):
    return pltpu.CompilerParams(vmem_limit_bytes=LIMIT, **kw)


def cost(flops, nbytes):
    return pl.CostEstimate(flops=int(flops), bytes_accessed=int(nbytes), transcendentals=0)


def swap(x, axis, n, s):
    return lax.ppermute(x, axis, [(i, i ^ s) for i in range(n)])


def panel_kernel(n_in, me_ref, probe_ref, a_ref, b_ref, keep_ref, send_ref, acc, sketch, tile):
    step = pl.program_id(0)
    depth = a_ref.shape[1]

    @pl.when(step < n_in)
    def _():
        rows = pl.ds(pl.multiple_of(step * depth, depth), depth)
        part = jnp.dot(a_ref[...], probe_ref[rows, :], preferred_element_type=F32)

        @pl.when(step == 0)
        def _():
            acc[...] = part

        @pl.when(step > 0)
        def _():
            acc[...] += part

    @pl.when(step == n_in - 1)
    def _():
        sketch[...] = acc[...].T.astype(BF16)

    @pl.when(step >= n_in)
    def _():
        core = me_ref[0] % 2
        _, groups, rows, _ = keep_ref.shape
        out = jnp.dot(sketch[...], b_ref[...], preferred_element_type=F32)
        tile[...] = out.T.reshape(tile.shape)
        for g in range(groups):
            keep_ref[0, g] = tile[2 * g + core]
            send_ref[0, g] = tile[2 * g + 1 - core]


def panel_call(me, probe, a, b, n_in, n_out, groups):
    pairs, width_a = a.shape
    width_b = b.shape[1]
    rank = probe.shape[1]
    depth = width_a // n_in
    cols = width_b // n_out
    rows = cols // groups // 2
    out = sds((n_out, groups, rows, rank), F32)
    spec = pl.BlockSpec((1, groups, rows, rank), lambda i: (jnp.maximum(i - n_in, 0), 0, 0, 0))
    return pl.pallas_call(
        functools.partial(panel_kernel, n_in),
        grid=(n_in + n_out,),
        in_specs=[
            SMEM,
            VMEM,
            pl.BlockSpec((pairs, depth), lambda i: (0, jnp.minimum(i, n_in - 1))),
            pl.BlockSpec((pairs, cols), lambda i: (0, jnp.maximum(i - n_in, 0))),
        ],
        out_specs=[spec, spec],
        out_shape=[out, out],
        scratch_shapes=[
            pltpu.VMEM((pairs, rank), F32),
            pltpu.VMEM((rank, pairs), BF16),
            pltpu.VMEM((2 * groups, rows, rank), F32),
        ],
        compiler_params=params(),
        cost_estimate=cost(2 * pairs * rank * (width_a + width_b), 2 * pairs * (width_a + width_b)),
        name="panel",
    )(me, probe, a, b)


def place_kernel(order, me_ref, *refs):
    *parts, out_ref = refs
    for part, spot in zip(parts, order):
        for i, (r, c) in enumerate(spot):
            row, col = me_ref[1] ^ r, me_ref[0] ^ c
            out_ref[row, col] = part[i]


def plane_kernel(axis, shifts, me_ref, keep_ref, recv_ref, own_ref, *send_refs):
    spot = me_ref[0] // 2

    def total(i):
        if axis == 1:
            return keep_ref[:, i] + recv_ref[:, i]
        return keep_ref[i] + recv_ref[i]

    own_ref[...] = total(spot)
    for s, ref in zip(shifts, send_refs):
        ref[...] = total(spot ^ (s // 2)).astype(BF16)


def plane_call(axis, shifts, me, keep, recv):
    shape = list(keep.shape)
    del shape[axis]
    return pl.pallas_call(
        functools.partial(plane_kernel, axis, shifts),
        in_specs=[SMEM, VMEM, VMEM],
        out_specs=[VMEM] * (1 + len(shifts)),
        out_shape=[sds(shape, F32)] + [sds(shape, BF16)] * len(shifts),
        compiler_params=params(),
        cost_estimate=cost(keep.size, 3 * 4 * keep.size),
        name="plane",
    )(me, keep, recv)


def depth_kernel(shifts, n, me_ref, own_ref, *refs):
    recv, (keep_ref, *send) = refs[:n], refs[n:]

    def total(r):
        value = own_ref[r]
        for ref in recv:
            value = value + ref[r].astype(F32)
        return value

    keep_ref[...] = total(me_ref[1])
    for s, ref in zip(shifts, send):
        ref[...] = total(me_ref[1] ^ s).astype(BF16)


def depth_call(shifts, me, own, recv):
    shape = own.shape[1:]
    return pl.pallas_call(
        functools.partial(depth_kernel, shifts, len(recv)),
        in_specs=[SMEM] + [VMEM] * (1 + len(recv)),
        out_specs=[VMEM] * (1 + len(shifts)),
        out_shape=[sds(shape, F32)] + [sds(shape, BF16)] * len(shifts),
        compiler_params=params(),
        cost_estimate=cost(own.size, 12 * own.size),
        name="depth",
    )(me, own, *recv)


def last_kernel(own_ref, *refs):
    *recv, out_ref = refs
    value = own_ref[...]
    for ref in recv:
        value = value + ref[...].astype(F32)
    out_ref[...] = value.astype(BF16)


def last_call(own, recv):
    return pl.pallas_call(
        last_kernel,
        in_specs=[VMEM] * (1 + len(recv)),
        out_specs=VMEM,
        out_shape=sds(own.shape, BF16),
        compiler_params=params(),
        cost_estimate=cost(own.size, 12 * own.size),
        name="last",
    )(own, *recv)


def gram_kernel(which, n, me_ref, *refs):
    parts, (panel_ref, gram_ref) = refs[:n], refs[n:]
    me = me_ref[which]
    for s, part in enumerate(parts):
        panel_ref[me ^ s] = part[...]
    rank = gram_ref.shape[0]
    panel = panel_ref[...].reshape(-1, rank)
    gram_ref[...] = lax.dot_general(
        panel, panel, (((0,), (0,)), ((), ())), preferred_element_type=F32
    )


def gram_call(which, me, parts):
    n = len(parts)
    rows, rank = parts[0].shape
    return pl.pallas_call(
        functools.partial(gram_kernel, which, n),
        in_specs=[SMEM] + [VMEM] * n,
        out_specs=[VMEM, VMEM],
        out_shape=[sds((n, rows, rank), BF16), sds((rank, rank), F32)],
        compiler_params=params(),
        cost_estimate=cost(2 * n * rows * rank * rank, 4 * n * rows * rank),
        name="gram",
    )(me, *parts)


def inverse_factor(gram):
    n = gram.shape[0]
    lane = lax.broadcasted_iota(jnp.int32, (8, n), 1)
    sub = lax.broadcasted_iota(jnp.int32, (8, n), 0)
    rows = [gram[8 * i : 8 * i + 8, :] for i in range(n // 8)]
    for b in range(n // 8):
        cols = [
            [jnp.broadcast_to(rows[i][:, 8 * b + j : 8 * b + j + 1], (8, n)) for i in range(b, n // 8)]
            for j in range(8)
        ]
        scale = jnp.ones((8, n), F32)
        for j in range(8):
            k = 8 * b + j
            pivot = jnp.broadcast_to(cols[j][0][j : j + 1, :], (8, n))
            inv = 1.0 / pivot
            scale = jnp.where(sub == j, pivot, scale)
            pivot_row = jnp.where(lane == k, 1.0, jnp.broadcast_to(rows[b][j : j + 1, :], (8, n)))
            below = sub > j
            mult = [c * inv for c in cols[j]]
            mult[0] = jnp.where(below, mult[0], 0.0)
            for jj in range(j + 1, 8):
                entry = jnp.broadcast_to(cols[jj][0][j : j + 1, :], (8, n))
                cols[jj] = [c - m * entry for c, m in zip(cols[jj], mult)]
            for i in range(b, n // 8):
                here = lane == k
                if i == b:
                    here = jnp.logical_and(here, below)
                rows[i] = jnp.where(here, 0.0, rows[i]) - mult[i - b] * pivot_row
        unit = jnp.where(lane == sub + 8 * b, 1.0, jnp.where(lane < sub + 8 * b, rows[b], 0.0))
        rows[b] = unit * lax.rsqrt(scale)
    return jnp.concatenate(rows, axis=0)


def finish_kernel(width, panel_ref, own_ref, *refs):
    *recv, out_ref = refs
    gram = own_ref[...]
    for ref in recv:
        gram = gram + ref[...]
    inverse = inverse_factor(gram) * math.sqrt(width)
    high = inverse.astype(BF16)
    low = (inverse - high.astype(F32)).astype(BF16)
    dims = (((1,), (1,)), ((), ()))
    panel = panel_ref[...].reshape(out_ref.shape)
    out_ref[...] = lax.dot_general(panel, high, dims, preferred_element_type=F32) + lax.dot_general(
        panel, low, dims, preferred_element_type=F32
    )


def finish_call(width, panel, own, recv):
    n, rows, rank = panel.shape
    return pl.pallas_call(
        functools.partial(finish_kernel, width),
        in_specs=[VMEM] * (2 + len(recv)),
        out_specs=VMEM,
        out_shape=sds((n * rows, rank), F32),
        compiler_params=params(),
        cost_estimate=cost(10**10, 6 * n * rows * rank),
        name="finish",
    )(panel, own, *recv)


def per_device(n_row, n_col, image_feats, text_feats, probe_image, probe_text):
    col_swap = lambda x, s: swap(x, "col", n_col, s)
    row_swap = lambda x, s: swap(x, "row", n_row, s)
    me = jnp.stack([lax.axis_index("col"), lax.axis_index("row")]).astype(jnp.int32)
    chips = list(range(2, n_col, 2))
    depths = list(range(1, n_row))
    rank = probe_text.shape[1]
    groups = n_col // 2

    parts = {0: probe_text}
    for s in chips:
        parts[s] = col_swap(probe_text, s)
    for s in list(parts):
        parts[s ^ 1] = col_swap(parts[s], 1)
    order = sorted(parts)
    text_whole = pl.pallas_call(
        functools.partial(place_kernel, [[(0, s)] for s in order]),
        in_specs=[SMEM] + [VMEM] * n_col,
        out_specs=VMEM,
        out_shape=sds((1, n_col) + probe_text.shape, BF16),
        compiler_params=params(),
        name="place_text",
    )(me * jnp.array([1, 0], jnp.int32), *[parts[s][None] for s in order]).reshape(-1, rank)

    depth_rows, _ = probe_image.shape
    piece = depth_rows // n_col
    if piece % 16 == 0:
        mine = lax.dynamic_slice_in_dim(probe_image, me[0] * piece, piece, 0)
        got = jnp.stack([row_swap(mine, t) for t in depths])
        sets = {0: got}
        for s in chips:
            sets[s] = col_swap(got, s)
        for s in list(sets):
            sets[s ^ 1] = col_swap(sets[s], 1)
        order = sorted(sets)
        spots = [[(0, c) for c in range(n_col)]] + [[(t, s) for t in depths] for s in order]

        def image_place(me_ref, own_ref, *refs):
            *parts, out_ref = refs
            for c in range(n_col):
                out_ref[me_ref[1], c] = own_ref[c]
            for part, s in zip(parts, order):
                for i, t in enumerate(depths):
                    out_ref[me_ref[1] ^ t, me_ref[0] ^ s] = part[i]

        image_whole = pl.pallas_call(
            image_place,
            in_specs=[SMEM] + [VMEM] * (1 + n_col),
            out_specs=VMEM,
            out_shape=sds((n_row, n_col, piece, rank), BF16),
            compiler_params=params(),
            name="place_image",
        )(me, probe_image.reshape(n_col, piece, rank), *[sets[s] for s in order]).reshape(-1, rank)
    else:
        image_whole = lax.all_gather(probe_image, "row", axis=0, tiled=True)

    n_text = max(1, text_feats.shape[1] // 1024)
    n_image = max(1, image_feats.shape[1] // 1536)
    keep, send = panel_call(me, text_whole, text_feats, image_feats, n_text, n_row, groups)
    recv = col_swap(send, 1)
    own, *sends = plane_call(1, chips, me, keep, recv)
    recv = [col_swap(x, s) for x, s in zip(sends, chips)]
    own, *sends = depth_call(depths, me, own, recv)
    recv = [row_swap(x, s) for x, s in zip(sends, depths)]
    mine = last_call(own, recv)
    image_parts = [mine] + [col_swap(mine, s) for s in range(1, n_col)]
    image_panel, image_local = gram_call(0, me, image_parts)
    image_grams = [row_swap(image_local, s) for s in depths]
    image_basis = finish_call(image_feats.shape[1], image_panel, image_local, image_grams)

    keep, send = panel_call(me, image_whole, image_feats, text_feats, n_image, groups, 1)
    split = (groups, n_row, keep.shape[2] // n_row, rank)
    keep, send = keep.reshape(split), send.reshape(split)
    recv = col_swap(send, 1)
    own, *sends = plane_call(0, chips, me, keep, recv)
    recv = [col_swap(x, s) for x, s in zip(sends, chips)]
    own, *sends = depth_call(depths, me, own, recv)
    recv = [row_swap(x, s) for x, s in zip(sends, depths)]
    mine = last_call(own, recv)
    text_parts = [mine] + [row_swap(mine, s) for s in depths]
    text_panel, text_local = gram_call(1, me, text_parts)
    text_grams = [col_swap(text_local, s) for s in range(1, n_col)]
    text_basis = finish_call(text_feats.shape[1], text_panel, text_local, text_grams)
    return image_basis, text_basis


def solution(mesh):
    in_specs = (P(("row", "col"), None), P(("row", "col"), None), P("row", None), P("col", None))
    out_specs = (P("row", None), P("col", None))
    body = functools.partial(per_device, mesh.shape["row"], mesh.shape["col"])
    return jax.shard_map(body, mesh=mesh, in_specs=in_specs, out_specs=out_specs, check_vma=False)
```

```python
import functools
import math

import jax
import jax.numpy as jnp
from jax import lax
from jax.experimental import pallas as pl
from jax.experimental.pallas import tpu as pltpu
from jax.sharding import PartitionSpec as P

F32 = jnp.float32
BF16 = jnp.bfloat16
VMEM = pl.BlockSpec(memory_space=pltpu.VMEM)
SMEM = pl.BlockSpec(memory_space=pltpu.SMEM)
LIMIT = 24 * 1024 * 1024


def sds(shape, dtype):
    return jax.ShapeDtypeStruct(shape, dtype)


def params(**kw):
    return pltpu.CompilerParams(vmem_limit_bytes=LIMIT, **kw)


def cost(flops, nbytes):
    return pl.CostEstimate(flops=int(flops), bytes_accessed=int(nbytes), transcendentals=0)


def chunks_of(width):
    return width // max(1, width // 1024)


def sketch_of(feats_ref, weights, out_ref):
    width = feats_ref.shape[1]
    step = chunks_of(width)
    total = None
    for at in range(0, width, step):
        part = jnp.dot(
            feats_ref[:, at : at + step], weights(at, step), preferred_element_type=F32
        )
        total = part if total is None else total + part
    out_ref[...] = total.T.astype(BF16)


def text_sketch_kernel(order, me_ref, feats_ref, *refs):
    *parts, out_ref, probe = refs
    n = parts[0].shape[0]
    rows = parts[0].shape[1]
    for part, s in zip(parts, order):
        for i in range(n):
            col = 2 * i + (me_ref[0] % 2 ^ s)
            probe[pl.ds(pl.multiple_of(col * rows, rows), rows), :] = part[i]
    sketch_of(feats_ref, lambda at, step: probe[at : at + step, :], out_ref)


def image_sketch_kernel(me_ref, feats_ref, *refs):
    *parts, out_ref, probe = refs
    groups, n_row, rows, _ = parts[0].shape
    for s, part in enumerate(parts):
        core = me_ref[0] % 2 ^ s
        for g in range(groups):
            for r in range(n_row):
                at = (r * 2 * groups + 2 * g + core) * rows
                probe[pl.ds(pl.multiple_of(at, rows), rows), :] = part[g, r]
    sketch_of(feats_ref, lambda at, step: probe[at : at + step, :], out_ref)


def plain_sketch_kernel(me_ref, feats_ref, probe, out_ref):
    sketch_of(feats_ref, lambda at, step: probe[at : at + step, :], out_ref)


def sketch_call(kernel, me, feats, parts, scratch, name):
    pairs, width = feats.shape
    rank = parts[0].shape[-1]
    return pl.pallas_call(
        kernel,
        in_specs=[SMEM] + [VMEM] * (1 + len(parts)),
        out_specs=VMEM,
        out_shape=sds((rank, pairs), BF16),
        scratch_shapes=[pltpu.VMEM((width, rank), BF16)] * scratch,
        compiler_params=params(),
        cost_estimate=cost(2 * pairs * rank * width, 2 * pairs * width),
        name=name,
    )(me, feats, *parts)


def product_kernel(me_ref, sketch_ref, feats_ref, keep_ref, send_ref):
    core = me_ref[0] % 2
    blocks = keep_ref.shape[0]
    cols = feats_ref.shape[1] // blocks // 2

    @pl.loop(0, blocks)
    def _(i):
        for rel, ref in ((0, keep_ref), (1, send_ref)):
            at = pl.multiple_of((2 * i + (core ^ rel)) * cols, cols)
            out = jnp.dot(sketch_ref[...], feats_ref[:, pl.ds(at, cols)], preferred_element_type=F32)
            ref[i] = out.T.reshape(ref.shape[1:])


def product_call(me, sketch, feats, blocks, parts, name):
    pairs, width = feats.shape
    rank = sketch.shape[0]
    out = sds((blocks, parts, width // blocks // parts // 2, rank), F32)
    return pl.pallas_call(
        product_kernel,
        in_specs=[SMEM, VMEM, VMEM],
        out_specs=[VMEM, VMEM],
        out_shape=[out, out],
        compiler_params=params(),
        cost_estimate=cost(2 * pairs * rank * width, 2 * pairs * width),
        name=name,
    )(me, sketch, feats)


def plane_kernel(me_ref, ikeep, irecv, tkeep, trecv, iown, town, send):
    groups, n_row = send.shape[:2]
    rows = iown.shape[1]
    spot = me_ref[0] // 2
    for r in range(n_row):
        iown[r] = ikeep[r, spot] + irecv[r, spot]
        town[r] = tkeep[spot, r] + trecv[spot, r]
        for g in range(groups):
            send[g, r, :rows] = (ikeep[r, g] + irecv[r, g]).astype(BF16)
            send[g, r, rows:] = (tkeep[g, r] + trecv[g, r]).astype(BF16)


def plane_call(me, ikeep, irecv, tkeep, trecv):
    n_row, groups, irows, rank = ikeep.shape
    trows = tkeep.shape[2]
    return pl.pallas_call(
        plane_kernel,
        in_specs=[SMEM] + [VMEM] * 4,
        out_specs=[VMEM] * 3,
        out_shape=[
            sds((n_row, irows, rank), F32),
            sds((n_row, trows, rank), F32),
            sds((groups, n_row, irows + trows, rank), BF16),
        ],
        compiler_params=params(),
        cost_estimate=cost(ikeep.size, 12 * (ikeep.size + tkeep.size)),
        name="plane",
    )(me, ikeep, irecv, tkeep, trecv)


def depth_kernel(me_ref, iown, town, recv, ikeep, tkeep, send):
    groups, n_row = recv.shape[:2]
    rows = ikeep.shape[0]
    spot = me_ref[0] // 2

    def sums(r):
        image, text = iown[r], town[r]
        for s in range(1, groups):
            image = image + recv[spot ^ s, r, :rows].astype(F32)
            text = text + recv[spot ^ s, r, rows:].astype(F32)
        return image, text

    ikeep[...], tkeep[...] = sums(me_ref[1])
    for r in range(n_row):
        image, text = sums(r)
        send[r, :rows] = image.astype(BF16)
        send[r, rows:] = text.astype(BF16)


def depth_call(me, iown, town, recv):
    n_row, irows, rank = iown.shape
    trows = town.shape[1]
    return pl.pallas_call(
        depth_kernel,
        in_specs=[SMEM] + [VMEM] * 3,
        out_specs=[VMEM] * 3,
        out_shape=[
            sds((irows, rank), F32),
            sds((trows, rank), F32),
            sds((n_row, irows + trows, rank), BF16),
        ],
        compiler_params=params(),
        cost_estimate=cost(iown.size, 12 * (iown.size + town.size)),
        name="depth",
    )(me, iown, town, recv)


def last_kernel(me_ref, iown, town, recv, iout, tout):
    rows = iown.shape[0]
    image, text = iown[...], town[...]
    for s in range(1, recv.shape[0]):
        image = image + recv[me_ref[1] ^ s, :rows].astype(F32)
        text = text + recv[me_ref[1] ^ s, rows:].astype(F32)
    image, text = image.astype(BF16), text.astype(BF16)
    for i in range(iout.shape[0]):
        iout[i] = image
    for i in range(tout.shape[0]):
        tout[i] = text


def last_call(me, n_col, iown, town, recv):
    n_row = recv.shape[0]
    return pl.pallas_call(
        last_kernel,
        in_specs=[SMEM] + [VMEM] * 3,
        out_specs=[VMEM] * 2,
        out_shape=[sds((n_col,) + iown.shape, BF16), sds((n_row,) + town.shape, BF16)],
        compiler_params=params(),
        cost_estimate=cost(iown.size, 4 * n_col * iown.size),
        name="last",
    )(me, iown, town, recv)


def gram_kernel(panel_ref, out_ref):
    rank = out_ref.shape[-1]
    panel = panel_ref[...].reshape(-1, rank)
    gram = lax.dot_general(panel, panel, (((0,), (0,)), ((), ())), preferred_element_type=F32)
    for i in range(out_ref.shape[0]):
        out_ref[i] = gram


def gram_call(panel, copies):
    n, rows, rank = panel.shape
    return pl.pallas_call(
        gram_kernel,
        in_specs=[VMEM],
        out_specs=VMEM,
        out_shape=sds((copies, rank, rank), F32),
        compiler_params=params(),
        cost_estimate=cost(2 * n * rows * rank * rank, 4 * n * rows * rank),
        name="gram",
    )(panel)


def inverse_factor(gram):
    n = gram.shape[0]
    lane = lax.broadcasted_iota(jnp.int32, (8, n), 1)
    sub = lax.broadcasted_iota(jnp.int32, (8, n), 0)
    rows = [gram[8 * i : 8 * i + 8, :] for i in range(n // 8)]
    for b in range(n // 8):
        cols = [
            [jnp.broadcast_to(rows[i][:, 8 * b + j : 8 * b + j + 1], (8, n)) for i in range(b, n // 8)]
            for j in range(8)
        ]
        scale = jnp.ones((8, n), F32)
        for j in range(8):
            k = 8 * b + j
            pivot = jnp.broadcast_to(cols[j][0][j : j + 1, :], (8, n))
            inv = 1.0 / pivot
            scale = jnp.where(sub == j, pivot, scale)
            pivot_row = jnp.where(lane == k, 1.0, jnp.broadcast_to(rows[b][j : j + 1, :], (8, n)))
            below = sub > j
            mult = [c * inv for c in cols[j]]
            mult[0] = jnp.where(below, mult[0], 0.0)
            for jj in range(j + 1, 8):
                entry = jnp.broadcast_to(cols[jj][0][j : j + 1, :], (8, n))
                cols[jj] = [c - m * entry for c, m in zip(cols[jj], mult)]
            for i in range(b, n // 8):
                here = lane == k
                if i == b:
                    here = jnp.logical_and(here, below)
                rows[i] = jnp.where(here, 0.0, rows[i]) - mult[i - b] * pivot_row
            yield None
        unit = jnp.where(lane == sub + 8 * b, 1.0, jnp.where(lane < sub + 8 * b, rows[b], 0.0))
        rows[b] = unit * lax.rsqrt(scale)
        yield None
    yield jnp.concatenate(rows, axis=0)


def finish_kernel(widths, ipanel, igrams, tpanel, tgrams, iout, tout):
    def total(ref):
        value = ref[0]
        for i in range(1, ref.shape[0]):
            value = value + ref[i]
        return value

    inverses = None
    for inverses in zip(inverse_factor(total(igrams)), inverse_factor(total(tgrams))):
        pass
    dims = (((1,), (1,)), ((), ()))
    for inverse, width, panel_ref, out_ref in zip(inverses, widths, (ipanel, tpanel), (iout, tout)):
        inverse = inverse * math.sqrt(width)
        high = inverse.astype(BF16)
        low = (inverse - high.astype(F32)).astype(BF16)
        panel = panel_ref[...].reshape(out_ref.shape)
        out_ref[...] = lax.dot_general(panel, high, dims, preferred_element_type=F32) + lax.dot_general(
            panel, low, dims, preferred_element_type=F32
        )


def finish_call(widths, ipanel, igrams, tpanel, tgrams):
    rank = ipanel.shape[-1]
    outs = [sds((math.prod(p.shape[:-1]), rank), F32) for p in (ipanel, tpanel)]
    return pl.pallas_call(
        functools.partial(finish_kernel, widths),
        in_specs=[VMEM] * 4,
        out_specs=[VMEM] * 2,
        out_shape=outs,
        compiler_params=params(),
        cost_estimate=cost(10**10, 6 * ipanel.size),
        name="finish",
    )(ipanel, igrams, tpanel, tgrams)


def per_device(n_row, n_col, image_feats, text_feats, probe_image, probe_text):
    groups = n_col // 2
    rank = probe_text.shape[1]
    me = jnp.stack([lax.axis_index("col"), lax.axis_index("row")]).astype(jnp.int32)
    core_swap = lambda x: lax.ppermute(x, "col", [(i, i ^ 1) for i in range(n_col)])
    chips = [list(range(core, n_col, 2)) for core in range(2)]
    over_chips = lambda x: lax.all_to_all(x, "col", 0, 0, axis_index_groups=chips)
    over_col = lambda x: lax.all_to_all(x, "col", 0, 0)
    over_row = lambda x: lax.all_to_all(x, "row", 0, 0)
    copies = lambda x, n: jnp.broadcast_to(x[None], (n,) + x.shape)

    piece = probe_image.shape[0] // n_col
    text_part = over_chips(copies(probe_text, groups))
    text_parts = [text_part, core_swap(text_part)]
    if piece % 16 == 0:
        mine = lax.dynamic_slice_in_dim(probe_image, me[0] * piece, piece, 0)
        image_part = over_chips(copies(over_row(copies(mine, n_row)), groups))
        image_parts = [image_part, core_swap(image_part)]
        image_kernel, scratch = image_sketch_kernel, 1
    else:
        image_parts = [lax.all_gather(probe_image, "row", axis=0, tiled=True)]
        image_kernel, scratch = plain_sketch_kernel, 0

    text_kernel = functools.partial(text_sketch_kernel, (0, 1))
    sketch_text = sketch_call(text_kernel, me, text_feats, text_parts, 1, "sketch_text")
    ikeep, isend = product_call(me, sketch_text, image_feats, n_row, groups, "product_image")
    irecv = core_swap(isend)
    sketch_image = sketch_call(image_kernel, me, image_feats, image_parts, scratch, "sketch_image")
    tkeep, tsend = product_call(me, sketch_image, text_feats, groups, n_row, "product_text")
    trecv = core_swap(tsend)

    iown, town, send = plane_call(me, ikeep, irecv, tkeep, trecv)
    iown, town, send = depth_call(me, iown, town, over_chips(send))
    icopies, tcopies = last_call(me, n_col, iown, town, over_row(send))
    ipanel, tpanel = over_col(icopies), over_row(tcopies)
    ipanel = ipanel.reshape(groups, 2, -1, rank).transpose(1, 0, 2, 3).reshape(ipanel.shape)
    igrams = over_row(gram_call(ipanel, n_row))
    tgrams = over_col(gram_call(tpanel, n_col))
    widths = (image_feats.shape[1], text_feats.shape[1])
    return finish_call(widths, ipanel, igrams, tpanel, tgrams)


def solution(mesh):
    in_specs = (P(("row", "col"), None), P(("row", "col"), None), P("row", None), P("col", None))
    out_specs = (P("row", None), P("col", None))
    body = functools.partial(per_device, mesh.shape["row"], mesh.shape["col"])
    return jax.shard_map(body, mesh=mesh, in_specs=in_specs, out_specs=out_specs, check_vma=False)
```

```python
import functools
import math

import jax
import jax.numpy as jnp
from jax import lax
from jax.experimental import pallas as pl
from jax.experimental.pallas import tpu as pltpu
from jax.sharding import PartitionSpec as P

F32 = jnp.float32
BF16 = jnp.bfloat16
VMEM = pl.BlockSpec(memory_space=pltpu.VMEM)
SMEM = pl.BlockSpec(memory_space=pltpu.SMEM)
LIMIT = 24 * 1024 * 1024


def sds(shape, dtype):
    return jax.ShapeDtypeStruct(shape, dtype)


def params(**kw):
    return pltpu.CompilerParams(vmem_limit_bytes=LIMIT, **kw)


def cost(flops, nbytes):
    return pl.CostEstimate(flops=int(flops), bytes_accessed=int(nbytes), transcendentals=0)


def text_sketch_kernel(order, me_ref, feats_ref, *refs):
    *parts, out_ref = refs
    total = None
    for part, s in zip(parts, order):
        rows = part.shape[0]
        at = pl.multiple_of((me_ref[0] ^ s) * rows, rows)
        term = jnp.dot(feats_ref[:, pl.ds(at, rows)], part[...], preferred_element_type=F32)
        total = term if total is None else total + term
    out_ref[...] = total.T.astype(BF16)


def image_sketch_kernel(order, me_ref, feats_ref, own_ref, *refs):
    *parts, out_ref = refs
    rows = own_ref.shape[0]
    half = rows // 2
    at = pl.multiple_of(me_ref[1] * rows, rows)
    total = jnp.dot(feats_ref[:, pl.ds(at, rows)], own_ref[...], preferred_element_type=F32)
    for part, (t, c) in zip(parts, order):
        at = (me_ref[1] ^ t) * rows + (me_ref[0] % 2 ^ c) * half
        at = pl.multiple_of(at, half)
        total = total + jnp.dot(feats_ref[:, pl.ds(at, half)], part[...], preferred_element_type=F32)
    out_ref[...] = total.T.astype(BF16)


def sketch_call(kernel, order, me, feats, parts, name):
    pairs, width = feats.shape
    rank = parts[0].shape[-1]
    return pl.pallas_call(
        functools.partial(kernel, order),
        in_specs=[SMEM] + [VMEM] * (1 + len(parts)),
        out_specs=VMEM,
        out_shape=sds((rank, pairs), BF16),
        compiler_params=params(),
        cost_estimate=cost(2 * pairs * rank * width, 2 * pairs * width),
        name=name,
    )(me, feats, *parts)


def product_kernel(me_ref, sketch_ref, feats_ref, keep_ref, send_ref):
    core = me_ref[0] % 2
    blocks = keep_ref.shape[0]
    cols = feats_ref.shape[1] // blocks // 2

    @pl.loop(0, blocks)
    def _(i):
        for rel, ref in ((0, keep_ref), (1, send_ref)):
            at = pl.multiple_of((2 * i + (core ^ rel)) * cols, cols)
            out = jnp.dot(sketch_ref[...], feats_ref[:, pl.ds(at, cols)], preferred_element_type=F32)
            ref[i] = out.T.reshape(ref.shape[1:])


def product_call(me, sketch, feats, blocks, parts, name):
    pairs, width = feats.shape
    rank = sketch.shape[0]
    out = sds((blocks, parts, width // blocks // parts // 2, rank), F32)
    return pl.pallas_call(
        product_kernel,
        in_specs=[SMEM, VMEM, VMEM],
        out_specs=[VMEM, VMEM],
        out_shape=[out, out],
        compiler_params=params(),
        cost_estimate=cost(2 * pairs * rank * width, 2 * pairs * width),
        name=name,
    )(me, sketch, feats)


def sums_kernel(which, axis, shifts, n, me_ref, *refs):
    terms, (own_ref, *sends) = refs[:n], refs[n:]
    spot = me_ref[1] if which == "row" else me_ref[0] // 2

    def total(i):
        at = (slice(None),) * axis + (i,)
        value = terms[0][at]
        for term in terms[1:]:
            value = value + term[at].astype(F32)
        return value

    own_ref[...] = total(spot)
    for s, ref in zip(shifts, sends):
        ref[...] = total(spot ^ s).astype(BF16)


def sums_call(which, axis, shifts, me, terms, name):
    shape = list(terms[0].shape)
    size = terms[0].size
    del shape[axis]
    return pl.pallas_call(
        functools.partial(sums_kernel, which, axis, shifts, len(terms)),
        in_specs=[SMEM] + [VMEM] * len(terms),
        out_specs=[VMEM] * (1 + len(shifts)),
        out_shape=[sds(shape, F32)] + [sds(shape, BF16)] * len(shifts),
        compiler_params=params(),
        cost_estimate=cost(size, 4 * size * len(terms)),
        name=name,
    )(me, *terms)


def last_kernel(own_ref, *refs):
    *recv, out_ref = refs
    value = own_ref[...]
    for ref in recv:
        value = value + ref[...].astype(F32)
    out_ref[...] = value.astype(out_ref.dtype)


def last_call(own, recv, dtype, name):
    return pl.pallas_call(
        last_kernel,
        in_specs=[VMEM] * (1 + len(recv)),
        out_specs=VMEM,
        out_shape=sds(own.shape, dtype),
        compiler_params=params(),
        cost_estimate=cost(own.size, 12 * own.size),
        name=name,
    )(own, *recv)


def gram_kernel(which, order, me_ref, *refs):
    parts, (panel_ref, gram_ref) = refs[: len(order)], refs[len(order) :]
    for s, part in zip(order, parts):
        if which == "row":
            panel_ref[me_ref[1] ^ s] = part[...]
        else:
            spot = me_ref[0] ^ s
            panel_ref[spot % 2 * (len(order) // 2) + spot // 2] = part[...]
    panel = panel_ref[...].reshape(-1, gram_ref.shape[0])
    gram_ref[...] = lax.dot_general(
        panel, panel, (((0,), (0,)), ((), ())), preferred_element_type=F32
    )


def gram_call(which, order, me, parts, name):
    n = len(parts)
    rows, rank = parts[0].shape
    return pl.pallas_call(
        functools.partial(gram_kernel, which, order),
        in_specs=[SMEM] + [VMEM] * n,
        out_specs=[VMEM, VMEM],
        out_shape=[sds((n, rows, rank), BF16), sds((rank, rank), F32)],
        compiler_params=params(),
        cost_estimate=cost(2 * n * rows * rank * rank, 4 * n * rows * rank),
        name=name,
    )(me, *parts)


def inverse_factor(gram):
    n = gram.shape[0]
    lane = lax.broadcasted_iota(jnp.int32, (8, n), 1)
    sub = lax.broadcasted_iota(jnp.int32, (8, n), 0)
    rows = [gram[8 * i : 8 * i + 8, :] for i in range(n // 8)]
    for b in range(n // 8):
        cols = [
            [jnp.broadcast_to(rows[i][:, 8 * b + j : 8 * b + j + 1], (8, n)) for i in range(b, n // 8)]
            for j in range(8)
        ]
        scale = jnp.ones((8, n), F32)
        for j in range(8):
            k = 8 * b + j
            pivot = jnp.broadcast_to(cols[j][0][j : j + 1, :], (8, n))
            inv = 1.0 / pivot
            scale = jnp.where(sub == j, pivot, scale)
            pivot_row = jnp.where(lane == k, 1.0, jnp.broadcast_to(rows[b][j : j + 1, :], (8, n)))
            below = sub > j
            mult = [c * inv for c in cols[j]]
            mult[0] = jnp.where(below, mult[0], 0.0)
            for jj in range(j + 1, 8):
                entry = jnp.broadcast_to(cols[jj][0][j : j + 1, :], (8, n))
                cols[jj] = [c - m * entry for c, m in zip(cols[jj], mult)]
            for i in range(b, n // 8):
                here = lane == k
                if i == b:
                    here = jnp.logical_and(here, below)
                rows[i] = jnp.where(here, 0.0, rows[i]) - mult[i - b] * pivot_row
            yield None
        unit = jnp.where(lane == sub + 8 * b, 1.0, jnp.where(lane < sub + 8 * b, rows[b], 0.0))
        rows[b] = unit * lax.rsqrt(scale)
        yield None
    yield jnp.concatenate(rows, axis=0)


def finish_kernel(widths, n_image, ipanel, tpanel, *refs):
    *grams, iout, tout = refs

    def total(refs):
        value = refs[0][...]
        for ref in refs[1:]:
            value = value + ref[...]
        return value

    inverses = None
    for inverses in zip(inverse_factor(total(grams[:n_image])), inverse_factor(total(grams[n_image:]))):
        pass
    dims = (((1,), (1,)), ((), ()))
    for inverse, width, panel_ref, out_ref in zip(inverses, widths, (ipanel, tpanel), (iout, tout)):
        inverse = inverse * math.sqrt(width)
        high = inverse.astype(BF16)
        low = (inverse - high.astype(F32)).astype(BF16)
        panel = panel_ref[...].reshape(out_ref.shape)
        out_ref[...] = lax.dot_general(panel, high, dims, preferred_element_type=F32) + lax.dot_general(
            panel, low, dims, preferred_element_type=F32
        )


def finish_call(widths, ipanel, igrams, tpanel, tgrams):
    rank = ipanel.shape[-1]
    outs = [sds((math.prod(p.shape[:-1]), rank), F32) for p in (ipanel, tpanel)]
    return pl.pallas_call(
        functools.partial(finish_kernel, widths, len(igrams)),
        in_specs=[VMEM] * (2 + len(igrams) + len(tgrams)),
        out_specs=[VMEM] * 2,
        out_shape=outs,
        compiler_params=params(),
        cost_estimate=cost(10**10, 6 * ipanel.size),
        name="finish",
    )(ipanel, tpanel, *igrams, *tgrams)


def per_device(n_row, n_col, image_feats, text_feats, probe_image, probe_text):
    groups = n_col // 2
    me = jnp.stack([lax.axis_index("col"), lax.axis_index("row")]).astype(jnp.int32)
    col_swap = lambda x, s: lax.ppermute(x, "col", [(i, i ^ s) for i in range(n_col)])
    row_swap = lambda x, s: lax.ppermute(x, "row", [(i, i ^ s) for i in range(n_row)])
    chips, depths = list(range(1, groups)), list(range(1, n_row))
    over_chips = lambda xs: [col_swap(x, 2 * s) for x, s in zip(xs, chips)]
    over_depth = lambda xs: [row_swap(x, t) for x, t in zip(xs, depths)]

    def over_plane(x):
        got = {0: x}
        for s, block in zip(chips, over_chips([x] * len(chips))):
            got[2 * s] = block
        for s in list(got):
            got[s ^ 1] = col_swap(got[s], 1)
        return got

    half = probe_image.shape[0] // 2
    mine = lax.dynamic_slice_in_dim(probe_image, me[0] % 2 * half, half, 0)
    text_parts = over_plane(probe_text)
    image_parts = {}
    for t, block in zip(depths, over_depth([mine] * len(depths))):
        image_parts[t, 0] = block
        image_parts[t, 1] = col_swap(block, 1)

    sketch_text = sketch_call(
        text_sketch_kernel, list(text_parts), me, text_feats, list(text_parts.values()), "sketch_text"
    )
    keep, send = product_call(me, sketch_text, image_feats, n_row, groups, "product_image")
    own, *sends = sums_call("col", 1, chips, me, [keep, col_swap(send, 1)], "image_cores")
    own, *sends = sums_call("row", 0, depths, me, [own] + over_chips(sends), "image_plane")
    mine = last_call(own, over_depth(sends), BF16, "image_depth")
    parts = over_plane(mine)
    ipanel, gram = gram_call("col", list(parts), me, list(parts.values()), "image_gram")
    igrams = [gram] + over_depth([gram] * len(depths))

    sketch_image = sketch_call(
        image_sketch_kernel,
        list(image_parts),
        me,
        image_feats,
        [probe_image] + list(image_parts.values()),
        "sketch_image",
    )
    keep, send = product_call(me, sketch_image, text_feats, groups, n_row, "product_text")
    own, *sends = sums_call("row", 1, depths, me, [keep, col_swap(send, 1)], "text_cores")
    own, *sends = sums_call("col", 0, chips, me, [own] + over_depth(sends), "text_depth")
    mine = last_call(own, over_chips(sends), BF16, "text_plane")
    parts = [mine] + over_depth([mine] * len(depths))
    tpanel, gram = gram_call("row", [0] + depths, me, parts, "text_gram")
    gram = last_call(gram, [col_swap(gram, 1)], F32, "text_gram_cores")
    tgrams = [gram] + over_chips([gram] * len(chips))

    widths = (image_feats.shape[1], text_feats.shape[1])
    return finish_call(widths, ipanel, igrams, tpanel, tgrams)


def solution(mesh):
    in_specs = (P(("row", "col"), None), P(("row", "col"), None), P("row", None), P("col", None))
    out_specs = (P("row", None), P("col", None))
    body = functools.partial(per_device, mesh.shape["row"], mesh.shape["col"])
    return jax.shard_map(body, mesh=mesh, in_specs=in_specs, out_specs=out_specs, check_vma=False)
```

```python
import functools
import math

import jax
import jax.numpy as jnp
from jax import lax
from jax.experimental import pallas as pl
from jax.experimental.pallas import tpu as pltpu
from jax.sharding import PartitionSpec as P

F32 = jnp.float32
BF16 = jnp.bfloat16
VMEM = pl.BlockSpec(memory_space=pltpu.VMEM)
SMEM = pl.BlockSpec(memory_space=pltpu.SMEM)
LIMIT = 32 * 1024 * 1024


def sds(shape, dtype):
    return jax.ShapeDtypeStruct(shape, dtype)


def params(**kw):
    return pltpu.CompilerParams(vmem_limit_bytes=LIMIT, **kw)


def cost(flops, nbytes):
    return pl.CostEstimate(flops=int(flops), bytes_accessed=int(nbytes), transcendentals=0)


def panel_kernel(shifts, n_out, me_ref, a_hbm, b_hbm, *refs):
    n = len(shifts)
    parts, (keep_ref, send_ref, a_ref, b_ref, a_sem, b_sem) = refs[:n], refs[n:]
    core = me_ref[0] % 2
    depth = parts[0].shape[0]
    cols = b_ref.shape[1] // n_out // 2

    def column(i):
        if n == 1:
            return 0
        return pl.multiple_of((me_ref[0] ^ shifts[i]) * depth, depth)

    def copies():
        out = []
        pieces = max(1, depth // 1024)
        for i in range(n):
            for j in range(pieces):
                at = pl.ds(column(i) + j * (depth // pieces), depth // pieces)
                out.append(pltpu.make_async_copy(a_hbm.at[:, at], a_ref.at[:, at], a_sem.at[i * pieces + j]))
        wide = b_ref.shape[1] // n_out
        for i in range(n_out):
            at = pl.ds(i * wide, wide)
            out.append(pltpu.make_async_copy(b_hbm.at[:, at], b_ref.at[:, at], b_sem.at[i]))
        return out

    moves = copies()
    for move in moves:
        move.start()
    total = None
    pieces = max(1, depth // 1024)
    step = depth // pieces
    for i in range(n):
        for j in range(pieces):
            moves[i * pieces + j].wait()
            at = pl.ds(column(i) + j * step, step)
            weights = parts[i][j * step : j * step + step, :]
            term = jnp.dot(a_ref[:, at], weights, preferred_element_type=F32)
            total = term if total is None else total + term
    sketch = total.T.astype(BF16)
    for i in range(n_out):
        moves[n * pieces + i].wait()
        for rel, ref in ((0, keep_ref), (1, send_ref)):
            at = pl.multiple_of((2 * i + (core ^ rel)) * cols, cols)
            out = jnp.dot(sketch, b_ref[:, pl.ds(at, cols)], preferred_element_type=F32)
            ref[i] = out.T.reshape(ref.shape[1:])


def panel_call(me, a, b, parts, shifts, blocks, pieces, name):
    pairs, width = b.shape
    rank = parts[0].shape[-1]
    out = sds((blocks, pieces, width // blocks // pieces // 2, rank), F32)
    n_copies = len(parts) * max(1, parts[0].shape[0] // 1024)
    anywhere = pl.BlockSpec(memory_space=pl.ANY)
    return pl.pallas_call(
        functools.partial(panel_kernel, shifts, blocks),
        in_specs=[SMEM, anywhere, anywhere] + [VMEM] * len(parts),
        out_specs=[VMEM, VMEM],
        out_shape=[out, out],
        scratch_shapes=[
            pltpu.VMEM(a.shape, BF16),
            pltpu.VMEM(b.shape, BF16),
            pltpu.SemaphoreType.DMA((n_copies,)),
            pltpu.SemaphoreType.DMA((blocks,)),
        ],
        compiler_params=params(),
        cost_estimate=cost(2 * pairs * rank * (width + a.shape[1]), 2 * pairs * (width + a.shape[1])),
        name=name,
    )(me, a, b, *parts)


def sums_kernel(which, axis, shifts, n, me_ref, *refs):
    terms, (own_ref, *sends) = refs[:n], refs[n:]
    spot = me_ref[1] if which == "row" else me_ref[0] // 2

    def total(i):
        at = (slice(None),) * axis + (i,)
        value = terms[0][at]
        for term in terms[1:]:
            value = value + term[at].astype(F32)
        return value

    own_ref[...] = total(spot)
    for s, ref in zip(shifts, sends):
        ref[...] = total(spot ^ s).astype(BF16)


def sums_call(which, axis, shifts, me, terms, name):
    shape = list(terms[0].shape)
    size = terms[0].size
    del shape[axis]
    return pl.pallas_call(
        functools.partial(sums_kernel, which, axis, shifts, len(terms)),
        in_specs=[SMEM] + [VMEM] * len(terms),
        out_specs=[VMEM] * (1 + len(shifts)),
        out_shape=[sds(shape, F32)] + [sds(shape, BF16)] * len(shifts),
        compiler_params=params(),
        cost_estimate=cost(size, 4 * size * len(terms)),
        name=name,
    )(me, *terms)


def last_kernel(own_ref, *refs):
    *recv, out_ref = refs
    value = own_ref[...]
    for ref in recv:
        value = value + ref[...].astype(F32)
    out_ref[...] = value.astype(out_ref.dtype)


def last_call(own, recv, dtype, name):
    return pl.pallas_call(
        last_kernel,
        in_specs=[VMEM] * (1 + len(recv)),
        out_specs=VMEM,
        out_shape=sds(own.shape, dtype),
        compiler_params=params(),
        cost_estimate=cost(own.size, 12 * own.size),
        name=name,
    )(own, *recv)


def gram_kernel(which, order, me_ref, *refs):
    parts, (panel_ref, gram_ref) = refs[: len(order)], refs[len(order) :]
    for s, part in zip(order, parts):
        if which == "row":
            panel_ref[me_ref[1] ^ s] = part[...]
        else:
            spot = me_ref[0] ^ s
            panel_ref[spot % 2 * (len(order) // 2) + spot // 2] = part[...]
    panel = panel_ref[...].reshape(-1, gram_ref.shape[0])
    gram_ref[...] = lax.dot_general(
        panel, panel, (((0,), (0,)), ((), ())), preferred_element_type=F32
    )


def gram_call(which, order, me, parts, name):
    n = len(parts)
    rows, rank = parts[0].shape
    return pl.pallas_call(
        functools.partial(gram_kernel, which, order),
        in_specs=[SMEM] + [VMEM] * n,
        out_specs=[VMEM, VMEM],
        out_shape=[sds((n, rows, rank), BF16), sds((rank, rank), F32)],
        compiler_params=params(),
        cost_estimate=cost(2 * n * rows * rank * rank, 4 * n * rows * rank),
        name=name,
    )(me, *parts)


def tree_sum(values):
    while len(values) > 1:
        values = [x + y for x, y in zip(values[::2], values[1::2])]
    return values[0]


def text_gram_kernel(*refs):
    *parts, panel_ref, gram_ref = refs
    panel = tree_sum([part[...].astype(F32) for part in parts]).astype(BF16)
    panel_ref[0] = panel
    gram_ref[...] = lax.dot_general(
        panel, panel, (((0,), (0,)), ((), ())), preferred_element_type=F32
    )


def text_gram_call(parts):
    rows, rank = parts[0].shape
    return pl.pallas_call(
        text_gram_kernel,
        in_specs=[VMEM] * len(parts),
        out_specs=[VMEM, VMEM],
        out_shape=[sds((1, rows, rank), BF16), sds((rank, rank), F32)],
        compiler_params=params(),
        cost_estimate=cost(2 * rows * rank * rank, 4 * rows * rank),
        name="text_gram",
    )(*parts)


def inverse_factor(gram):
    n = gram.shape[0]
    lane = lax.broadcasted_iota(jnp.int32, (8, n), 1)
    sub = lax.broadcasted_iota(jnp.int32, (8, n), 0)
    rows = [gram[8 * i : 8 * i + 8, :] for i in range(n // 8)]
    for b in range(n // 8):
        cols = [
            [jnp.broadcast_to(rows[i][:, 8 * b + j : 8 * b + j + 1], (8, n)) for i in range(b, n // 8)]
            for j in range(8)
        ]
        scale = jnp.ones((8, n), F32)
        for j in range(8):
            k = 8 * b + j
            pivot = jnp.broadcast_to(cols[j][0][j : j + 1, :], (8, n))
            inv = 1.0 / pivot
            scale = jnp.where(sub == j, pivot, scale)
            pivot_row = jnp.where(lane == k, 1.0, jnp.broadcast_to(rows[b][j : j + 1, :], (8, n)))
            below = sub > j
            mult = [c * inv for c in cols[j]]
            mult[0] = jnp.where(below, mult[0], 0.0)
            for jj in range(j + 1, 8):
                entry = jnp.broadcast_to(cols[jj][0][j : j + 1, :], (8, n))
                cols[jj] = [c - m * entry for c, m in zip(cols[jj], mult)]
            for i in range(b, n // 8):
                here = lane == k
                if i == b:
                    here = jnp.logical_and(here, below)
                rows[i] = jnp.where(here, 0.0, rows[i]) - mult[i - b] * pivot_row
            yield None
        unit = jnp.where(lane == sub + 8 * b, 1.0, jnp.where(lane < sub + 8 * b, rows[b], 0.0))
        rows[b] = unit * lax.rsqrt(scale)
        yield None
    yield jnp.concatenate(rows, axis=0)


def finish_kernel(widths, n_image, ipanel, tpanel, *refs):
    *grams, iout, tout = refs

    def total(refs):
        value = refs[0][...]
        for ref in refs[1:]:
            value = value + ref[...]
        return value

    inverses = None
    for inverses in zip(inverse_factor(total(grams[:n_image])), inverse_factor(total(grams[n_image:]))):
        pass
    dims = (((1,), (1,)), ((), ()))
    for inverse, width, panel_ref, out_ref in zip(inverses, widths, (ipanel, tpanel), (iout, tout)):
        inverse = inverse * math.sqrt(width)
        high = inverse.astype(BF16)
        low = (inverse - high.astype(F32)).astype(BF16)
        panel = panel_ref[...].reshape(out_ref.shape)
        out_ref[...] = lax.dot_general(panel, high, dims, preferred_element_type=F32) + lax.dot_general(
            panel, low, dims, preferred_element_type=F32
        )


def finish_call(widths, ipanel, igrams, tpanel, tgrams):
    rank = ipanel.shape[-1]
    outs = [sds((math.prod(p.shape[:-1]), rank), F32) for p in (ipanel, tpanel)]
    return pl.pallas_call(
        functools.partial(finish_kernel, widths, len(igrams)),
        in_specs=[VMEM] * (2 + len(igrams) + len(tgrams)),
        out_specs=[VMEM] * 2,
        out_shape=outs,
        compiler_params=params(),
        cost_estimate=cost(10**10, 6 * ipanel.size),
        name="finish",
    )(ipanel, tpanel, *igrams, *tgrams)


def per_device(n_row, n_col, image_feats, text_feats, probe_image, probe_text):
    groups = n_col // 2
    me = jnp.stack([lax.axis_index("col"), lax.axis_index("row")]).astype(jnp.int32)
    col_swap = lambda x, s: lax.ppermute(x, "col", [(i, i ^ s) for i in range(n_col)])
    row_swap = lambda x, s: lax.ppermute(x, "row", [(i, i ^ s) for i in range(n_row)])
    chips, depths = list(range(1, groups)), list(range(1, n_row))
    over_chips = lambda xs: [col_swap(x, 2 * s) for x, s in zip(xs, chips)]
    over_depth = lambda xs: [row_swap(x, t) for x, t in zip(xs, depths)]

    def over_plane(x):
        got = {0: x}
        for s, block in zip(chips, over_chips([x] * len(chips))):
            got[2 * s] = block
        for s in list(got):
            got[s ^ 1] = col_swap(got[s], 1)
        return got

    text_parts = over_plane(probe_text)
    image_whole = lax.all_gather(probe_image, "row", axis=0, tiled=True)

    keep, send = panel_call(
        me,
        text_feats,
        image_feats,
        list(text_parts.values()),
        list(text_parts),
        n_row,
        groups,
        "image_panel",
    )
    own, *sends = sums_call("col", 1, chips, me, [keep, col_swap(send, 1)], "image_cores")
    own, *sends = sums_call("row", 0, depths, me, [own] + over_chips(sends), "image_plane")
    mine = last_call(own, over_depth(sends), BF16, "image_depth")
    parts = over_plane(mine)
    ipanel, gram = gram_call("col", list(parts), me, list(parts.values()), "image_gram")
    igrams = [gram] + over_depth([gram] * len(depths))

    keep, send = panel_call(
        me, image_feats, text_feats, [image_whole], [0], groups, 1, "text_panel"
    )
    own, *sends = sums_call("col", 0, chips, me, [keep, col_swap(send, 1)], "text_cores")
    own, sends = own[0], [x[0] for x in sends]
    mine = last_call(own, [x for x in over_chips(sends)], BF16, "text_plane")
    tpanel, gram = text_gram_call([mine] + over_depth([mine] * len(depths)))
    gram = last_call(gram, [col_swap(gram, 1)], F32, "text_gram_cores")
    tgrams = [gram] + over_chips([gram] * len(chips))

    widths = (image_feats.shape[1], text_feats.shape[1])
    return finish_call(widths, ipanel, igrams, tpanel, tgrams)


def solution(mesh):
    in_specs = (P(("row", "col"), None), P(("row", "col"), None), P("row", None), P("col", None))
    out_specs = (P("row", None), P("col", None))
    body = functools.partial(per_device, mesh.shape["row"], mesh.shape["col"])
    return jax.shard_map(body, mesh=mesh, in_specs=in_specs, out_specs=out_specs, check_vma=False)
```

```python
import functools
import math

import jax
import jax.numpy as jnp
from jax import lax
from jax.experimental import pallas as pl
from jax.experimental.pallas import tpu as pltpu
from jax.sharding import PartitionSpec as P

F32 = jnp.float32
BF16 = jnp.bfloat16
VMEM = pl.BlockSpec(memory_space=pltpu.VMEM)
SMEM = pl.BlockSpec(memory_space=pltpu.SMEM)
LIMIT = 32 * 1024 * 1024
PANEL_LIMIT = 46 * 1024 * 1024


def sds(shape, dtype):
    return jax.ShapeDtypeStruct(shape, dtype)


def params(**kw):
    return pltpu.CompilerParams(vmem_limit_bytes=LIMIT, **kw)


def cost(flops, nbytes):
    return pl.CostEstimate(flops=int(flops), bytes_accessed=int(nbytes), transcendentals=0)


def text_columns(shifts, depth):
    return lambda me_ref: [pl.multiple_of((me_ref[0] ^ s) * depth, depth) for s in shifts]


def image_columns(order, depth):
    def columns(me_ref):
        core = me_ref[0] % 2
        out = []
        for even, odd, half in order:
            at = (me_ref[1] ^ (even + core * (odd - even))) * depth
            if half is not None:
                at = pl.multiple_of(at + (core ^ half) * (depth // 2), depth // 2)
            else:
                at = pl.multiple_of(at, depth)
            out.append(at)
        return out

    return columns


def panel_kernel(columns, n, n_out, me_ref, a_hbm, b_hbm, *refs):
    parts, (keep_ref, send_ref, a_ref, b_ref, a_sem, b_sem) = refs[:n], refs[n:]
    core = me_ref[0] % 2
    cols = b_ref.shape[1] // n_out // 2
    moves = []
    spans = [pl.ds(at, part.shape[0]) for at, part in zip(columns(me_ref), parts)]
    for i, span in enumerate(spans):
        moves.append(pltpu.make_async_copy(a_hbm.at[:, span], a_ref.at[:, span], a_sem.at[i]))
    for i in range(n_out):
        span = pl.ds(2 * i * cols, 2 * cols)
        moves.append(pltpu.make_async_copy(b_hbm.at[:, span], b_ref.at[:, span], b_sem.at[i]))
    for move in moves:
        move.start()
    total = None
    for i, span in enumerate(spans):
        moves[i].wait()
        term = jnp.dot(a_ref[:, span], parts[i][...], preferred_element_type=F32)
        total = term if total is None else total + term
    sketch = total.T.astype(BF16)
    for i in range(n_out):
        moves[n + i].wait()
        for rel, ref in ((0, keep_ref), (1, send_ref)):
            at = pl.multiple_of((2 * i + (core ^ rel)) * cols, cols)
            out = jnp.dot(sketch, b_ref[:, pl.ds(at, cols)], preferred_element_type=F32)
            ref[i] = out.T.reshape(ref.shape[1:])


def panel_call(me, a, b, parts, columns, blocks, pieces, name):
    pairs, width = b.shape
    rank = parts[0].shape[-1]
    out = sds((blocks, pieces, width // blocks // pieces // 2, rank), F32)
    hbm = pl.BlockSpec(memory_space=pltpu.HBM)
    return pl.pallas_call(
        functools.partial(panel_kernel, columns, len(parts), blocks),
        in_specs=[SMEM, hbm, hbm] + [VMEM] * len(parts),
        out_specs=[VMEM, VMEM],
        out_shape=[out, out],
        scratch_shapes=[
            pltpu.VMEM(a.shape, BF16),
            pltpu.VMEM(b.shape, BF16),
            pltpu.SemaphoreType.DMA((len(parts),)),
            pltpu.SemaphoreType.DMA((blocks,)),
        ],
        compiler_params=pltpu.CompilerParams(vmem_limit_bytes=PANEL_LIMIT),
        cost_estimate=cost(2 * pairs * rank * (width + a.shape[1]), 2 * pairs * (width + a.shape[1])),
        name=name,
    )(me, a, b, *parts)


def sums_kernel(which, axis, shifts, n, me_ref, *refs):
    terms, (own_ref, *sends) = refs[:n], refs[n:]
    spot = me_ref[1] if which == "row" else me_ref[0] // 2

    def total(i):
        at = (slice(None),) * axis + (i,)
        value = terms[0][at]
        for term in terms[1:]:
            value = value + term[at].astype(F32)
        return value

    own_ref[...] = total(spot)
    for s, ref in zip(shifts, sends):
        ref[...] = total(spot ^ s).astype(BF16)


def sums_call(which, axis, shifts, me, terms, name):
    shape = list(terms[0].shape)
    size = terms[0].size
    del shape[axis]
    return pl.pallas_call(
        functools.partial(sums_kernel, which, axis, shifts, len(terms)),
        in_specs=[SMEM] + [VMEM] * len(terms),
        out_specs=[VMEM] * (1 + len(shifts)),
        out_shape=[sds(shape, F32)] + [sds(shape, BF16)] * len(shifts),
        compiler_params=params(),
        cost_estimate=cost(size, 4 * size * len(terms)),
        name=name,
    )(me, *terms)


def last_kernel(own_ref, *refs):
    *recv, out_ref = refs
    value = own_ref[...]
    for ref in recv:
        value = value + ref[...].astype(F32)
    out_ref[...] = value.astype(out_ref.dtype)


def last_call(own, recv, dtype, name):
    return pl.pallas_call(
        last_kernel,
        in_specs=[VMEM] * (1 + len(recv)),
        out_specs=VMEM,
        out_shape=sds(own.shape, dtype),
        compiler_params=params(),
        cost_estimate=cost(own.size, 12 * own.size),
        name=name,
    )(own, *recv)


def gram_kernel(which, order, me_ref, *refs):
    parts, (panel_ref, gram_ref) = refs[: len(order)], refs[len(order) :]
    for s, part in zip(order, parts):
        if which == "row":
            panel_ref[me_ref[1] ^ s] = part[...]
        else:
            spot = me_ref[0] ^ s
            panel_ref[spot % 2 * (len(order) // 2) + spot // 2] = part[...]
    panel = panel_ref[...].reshape(-1, gram_ref.shape[0])
    gram_ref[...] = lax.dot_general(
        panel, panel, (((0,), (0,)), ((), ())), preferred_element_type=F32
    )


def gram_call(which, order, me, parts, name):
    n = len(parts)
    rows, rank = parts[0].shape
    return pl.pallas_call(
        functools.partial(gram_kernel, which, order),
        in_specs=[SMEM] + [VMEM] * n,
        out_specs=[VMEM, VMEM],
        out_shape=[sds((n, rows, rank), BF16), sds((rank, rank), F32)],
        compiler_params=params(),
        cost_estimate=cost(2 * n * rows * rank * rank, 4 * n * rows * rank),
        name=name,
    )(me, *parts)


def tree_sum(values):
    while len(values) > 1:
        values = [x + y for x, y in zip(values[::2], values[1::2])]
    return values[0]


def text_gram_kernel(*refs):
    *parts, panel_ref, gram_ref = refs
    panel = tree_sum([part[...].astype(F32) for part in parts]).astype(BF16)
    panel_ref[0] = panel
    gram_ref[...] = lax.dot_general(
        panel, panel, (((0,), (0,)), ((), ())), preferred_element_type=F32
    )


def text_gram_call(parts):
    rows, rank = parts[0].shape
    return pl.pallas_call(
        text_gram_kernel,
        in_specs=[VMEM] * len(parts),
        out_specs=[VMEM, VMEM],
        out_shape=[sds((1, rows, rank), BF16), sds((rank, rank), F32)],
        compiler_params=params(),
        cost_estimate=cost(2 * rows * rank * rank, 4 * rows * rank),
        name="text_gram",
    )(*parts)


def inverse_factor(gram):
    n = gram.shape[0]
    lane = lax.broadcasted_iota(jnp.int32, (8, n), 1)
    sub = lax.broadcasted_iota(jnp.int32, (8, n), 0)
    rows = [gram[8 * i : 8 * i + 8, :] for i in range(n // 8)]
    for b in range(n // 8):
        cols = [
            [jnp.broadcast_to(rows[i][:, 8 * b + j : 8 * b + j + 1], (8, n)) for i in range(b, n // 8)]
            for j in range(8)
        ]
        scale = jnp.ones((8, n), F32)
        for j in range(8):
            k = 8 * b + j
            pivot = jnp.broadcast_to(cols[j][0][j : j + 1, :], (8, n))
            inv = 1.0 / pivot
            scale = jnp.where(sub == j, pivot, scale)
            pivot_row = jnp.where(lane == k, 1.0, jnp.broadcast_to(rows[b][j : j + 1, :], (8, n)))
            below = sub > j
            mult = [c * inv for c in cols[j]]
            mult[0] = jnp.where(below, mult[0], 0.0)
            for jj in range(j + 1, 8):
                entry = jnp.broadcast_to(cols[jj][0][j : j + 1, :], (8, n))
                cols[jj] = [c - m * entry for c, m in zip(cols[jj], mult)]
            for i in range(b, n // 8):
                here = lane == k
                if i == b:
                    here = jnp.logical_and(here, below)
                rows[i] = jnp.where(here, 0.0, rows[i]) - mult[i - b] * pivot_row
            yield None
        unit = jnp.where(lane == sub + 8 * b, 1.0, jnp.where(lane < sub + 8 * b, rows[b], 0.0))
        rows[b] = unit * lax.rsqrt(scale)
        yield None
    yield jnp.concatenate(rows, axis=0)


def finish_kernel(widths, n_image, ipanel, tpanel, *refs):
    *grams, iout, tout = refs

    def total(refs):
        value = refs[0][...]
        for ref in refs[1:]:
            value = value + ref[...]
        return value

    inverses = None
    for inverses in zip(inverse_factor(total(grams[:n_image])), inverse_factor(total(grams[n_image:]))):
        pass
    dims = (((1,), (1,)), ((), ()))
    for inverse, width, panel_ref, out_ref in zip(inverses, widths, (ipanel, tpanel), (iout, tout)):
        inverse = inverse * math.sqrt(width)
        high = inverse.astype(BF16)
        low = (inverse - high.astype(F32)).astype(BF16)
        panel = panel_ref[...].reshape(out_ref.shape)
        out_ref[...] = lax.dot_general(panel, high, dims, preferred_element_type=F32) + lax.dot_general(
            panel, low, dims, preferred_element_type=F32
        )


def finish_call(widths, ipanel, igrams, tpanel, tgrams):
    rank = ipanel.shape[-1]
    outs = [sds((math.prod(p.shape[:-1]), rank), F32) for p in (ipanel, tpanel)]
    return pl.pallas_call(
        functools.partial(finish_kernel, widths, len(igrams)),
        in_specs=[VMEM] * (2 + len(igrams) + len(tgrams)),
        out_specs=[VMEM] * 2,
        out_shape=outs,
        compiler_params=params(),
        cost_estimate=cost(10**10, 6 * ipanel.size),
        name="finish",
    )(ipanel, tpanel, *igrams, *tgrams)


def per_device(n_row, n_col, image_feats, text_feats, probe_image, probe_text):
    groups = n_col // 2
    me = jnp.stack([lax.axis_index("col"), lax.axis_index("row")]).astype(jnp.int32)
    col_swap = lambda x, s: lax.ppermute(x, "col", [(i, i ^ s) for i in range(n_col)])
    row_swap = lambda x, s: lax.ppermute(x, "row", [(i, i ^ s) for i in range(n_row)])
    chips, depths = list(range(1, groups)), list(range(1, n_row))
    over_chips = lambda xs: [col_swap(x, 2 * s) for x, s in zip(xs, chips)]
    over_depth = lambda xs: [row_swap(x, t) for x, t in zip(xs, depths)]

    def over_plane(x):
        got = {0: x}
        for s, block in zip(chips, over_chips([x] * len(chips))):
            got[2 * s] = block
        for s in list(got):
            got[s ^ 1] = col_swap(got[s], 1)
        return got

    def split_swap(x, even, odd):
        pairs = []
        for r in range(n_row):
            for c in range(n_col):
                pairs.append((r * n_col + c, (r ^ (odd if c % 2 else even)) * n_col + c))
        return lax.ppermute(x, ("row", "col"), pairs)

    fetched = [(t, t + 1, split_swap(probe_image, t, t + 1)) for t in depths[:-1:2]]
    text_parts = over_plane(probe_text)
    first, *blocks = lax.optimization_barrier((me, *[block for _, _, block in fetched]))
    half = probe_image.shape[0] // 2
    last = depths[-1]
    mine = row_swap(lax.dynamic_slice_in_dim(probe_image, me[0] % 2 * half, half, 0), last)
    image_order = [(0, 0, None)]
    image_parts = [probe_image]
    for (even, odd, _), block in zip(fetched, blocks):
        image_order += [(even, odd, None), (odd, even, None)]
        image_parts += [block, col_swap(block, 1)]
    image_order += [(last, last, 0), (last, last, 1)]

    columns = text_columns(list(text_parts), probe_text.shape[0])
    keep, send = panel_call(
        first, text_feats, image_feats, list(text_parts.values()), columns, n_row, groups, "image_panel"
    )
    own, *sends = sums_call("col", 1, chips, me, [keep, col_swap(send, 1)], "image_cores")
    own, mine = lax.optimization_barrier((own, mine))
    image_parts += [mine, col_swap(mine, 1)]
    received = over_chips(sends)
    columns = image_columns(image_order, probe_image.shape[0])
    keep, send = panel_call(
        me, image_feats, text_feats, image_parts, columns, groups, 1, "text_panel"
    )
    send, *received = lax.optimization_barrier((send, *received))
    own, *sends = sums_call("row", 0, depths, me, [own] + received, "image_plane")
    mine = last_call(own, over_depth(sends), BF16, "image_depth")
    parts = over_plane(mine)
    ipanel, gram = gram_call("col", list(parts), me, list(parts.values()), "image_gram")
    igrams = [gram] + over_depth([gram] * len(depths))

    own, *sends = sums_call("col", 0, chips, me, [keep, col_swap(send, 1)], "text_cores")
    own, sends = own[0], [x[0] for x in sends]
    mine = last_call(own, [x for x in over_chips(sends)], BF16, "text_plane")
    tpanel, gram = text_gram_call([mine] + over_depth([mine] * len(depths)))
    gram = last_call(gram, [col_swap(gram, 1)], F32, "text_gram_cores")
    tgrams = [gram] + over_chips([gram] * len(chips))

    widths = (image_feats.shape[1], text_feats.shape[1])
    return finish_call(widths, ipanel, igrams, tpanel, tgrams)


def solution(mesh):
    in_specs = (P(("row", "col"), None), P(("row", "col"), None), P("row", None), P("col", None))
    out_specs = (P("row", None), P("col", None))
    body = functools.partial(per_device, mesh.shape["row"], mesh.shape["col"])
    return jax.shard_map(body, mesh=mesh, in_specs=in_specs, out_specs=out_specs, check_vma=False)
```

```python
import functools
import math

import jax
import jax.numpy as jnp
from jax import lax
from jax.experimental import pallas as pl
from jax.experimental.pallas import tpu as pltpu
from jax.sharding import PartitionSpec as P

F32 = jnp.float32
BF16 = jnp.bfloat16
VMEM = pl.BlockSpec(memory_space=pltpu.VMEM)
SMEM = pl.BlockSpec(memory_space=pltpu.SMEM)
LIMIT = 16 * 1024 * 1024
LOAD_LIMITS = (42, 46)


def sds(shape, dtype):
    return jax.ShapeDtypeStruct(shape, dtype)


def params(**kw):
    return pltpu.CompilerParams(vmem_limit_bytes=LIMIT, **kw)


def cost(flops, nbytes):
    return pl.CostEstimate(flops=int(flops), bytes_accessed=int(nbytes), transcendentals=0)


def text_columns(shifts, depth):
    return lambda me_ref: [pl.multiple_of((me_ref[0] ^ s) * depth, depth) for s in shifts]


def image_columns(order, depth):
    def columns(me_ref):
        core = me_ref[0] % 2
        out = []
        for even, odd, half in order:
            at = (me_ref[1] ^ (even + core * (odd - even))) * depth
            if half is not None:
                at = pl.multiple_of(at + (core ^ half) * (depth // 2), depth // 2)
            else:
                at = pl.multiple_of(at, depth)
            out.append(at)
        return out

    return columns


def load_kernel(hbm_ref, out_ref, sem):
    move = pltpu.make_async_copy(hbm_ref, out_ref, sem)
    move.start()
    move.wait()


def load_call(x, limit):
    return pl.pallas_call(
        load_kernel,
        in_specs=[pl.BlockSpec(memory_space=pltpu.HBM)],
        out_specs=VMEM,
        out_shape=sds(x.shape, x.dtype),
        scratch_shapes=[pltpu.SemaphoreType.DMA],
        compiler_params=pltpu.CompilerParams(vmem_limit_bytes=limit * 1024 * 1024),
        cost_estimate=cost(1, 4 * x.size),
        name="load",
    )(x)


def panel_kernel(columns, n, n_out, me_ref, a_ref, b_ref, *refs):
    parts, (keep_ref, send_ref) = refs[:n], refs[n:]
    core = me_ref[0] % 2
    cols = b_ref.shape[1] // n_out // 2
    total = None
    for at, part in zip(columns(me_ref), parts):
        span = pl.ds(at, part.shape[0])
        term = jnp.dot(a_ref[:, span], part[...], preferred_element_type=F32)
        total = term if total is None else total + term
    sketch = total.T.astype(BF16)
    for i in range(n_out):
        for rel, ref in ((0, keep_ref), (1, send_ref)):
            at = pl.multiple_of((2 * i + (core ^ rel)) * cols, cols)
            out = jnp.dot(sketch, b_ref[:, pl.ds(at, cols)], preferred_element_type=F32)
            ref[i] = out.T.reshape(ref.shape[1:])


def panel_call(me, a, b, parts, columns, blocks, pieces, name):
    pairs, width = b.shape
    rank = parts[0].shape[-1]
    out = sds((blocks, pieces, width // blocks // pieces // 2, rank), F32)
    return pl.pallas_call(
        functools.partial(panel_kernel, columns, len(parts), blocks),
        in_specs=[SMEM] + [VMEM] * (2 + len(parts)),
        out_specs=[VMEM, VMEM],
        out_shape=[out, out],
        compiler_params=params(),
        cost_estimate=cost(2 * pairs * rank * (width + a.shape[1]), 2 * pairs * (width + a.shape[1])),
        name=name,
    )(me, a, b, *parts)


def sums_kernel(which, axis, shifts, n, me_ref, *refs):
    terms, (own_ref, *sends) = refs[:n], refs[n:]
    spot = me_ref[1] if which == "row" else me_ref[0] // 2

    def total(i):
        at = (slice(None),) * axis + (i,)
        value = terms[0][at]
        for term in terms[1:]:
            value = value + term[at].astype(F32)
        return value

    own_ref[...] = total(spot)
    for s, ref in zip(shifts, sends):
        ref[...] = total(spot ^ s).astype(BF16)


def sums_call(which, axis, shifts, me, terms, name):
    shape = list(terms[0].shape)
    size = terms[0].size
    del shape[axis]
    return pl.pallas_call(
        functools.partial(sums_kernel, which, axis, shifts, len(terms)),
        in_specs=[SMEM] + [VMEM] * len(terms),
        out_specs=[VMEM] * (1 + len(shifts)),
        out_shape=[sds(shape, F32)] + [sds(shape, BF16)] * len(shifts),
        compiler_params=params(),
        cost_estimate=cost(size, 4 * size * len(terms)),
        name=name,
    )(me, *terms)


def last_kernel(own_ref, *refs):
    *recv, out_ref = refs
    value = own_ref[...]
    for ref in recv:
        value = value + ref[...].astype(F32)
    out_ref[...] = value.astype(out_ref.dtype)


def last_call(own, recv, dtype, name):
    return pl.pallas_call(
        last_kernel,
        in_specs=[VMEM] * (1 + len(recv)),
        out_specs=VMEM,
        out_shape=sds(own.shape, dtype),
        compiler_params=params(),
        cost_estimate=cost(own.size, 12 * own.size),
        name=name,
    )(own, *recv)


def gram_kernel(which, order, me_ref, *refs):
    parts, (panel_ref, gram_ref) = refs[: len(order)], refs[len(order) :]
    for s, part in zip(order, parts):
        if which == "row":
            panel_ref[me_ref[1] ^ s] = part[...]
        else:
            spot = me_ref[0] ^ s
            panel_ref[spot % 2 * (len(order) // 2) + spot // 2] = part[...]
    panel = panel_ref[...].reshape(-1, gram_ref.shape[0])
    gram_ref[...] = lax.dot_general(
        panel, panel, (((0,), (0,)), ((), ())), preferred_element_type=F32
    )


def gram_call(which, order, me, parts, name):
    n = len(parts)
    rows, rank = parts[0].shape
    return pl.pallas_call(
        functools.partial(gram_kernel, which, order),
        in_specs=[SMEM] + [VMEM] * n,
        out_specs=[VMEM, VMEM],
        out_shape=[sds((n, rows, rank), BF16), sds((rank, rank), F32)],
        compiler_params=params(),
        cost_estimate=cost(2 * n * rows * rank * rank, 4 * n * rows * rank),
        name=name,
    )(me, *parts)


def tree_sum(values):
    while len(values) > 1:
        values = [x + y for x, y in zip(values[::2], values[1::2])]
    return values[0]


def text_gram_kernel(*refs):
    *parts, panel_ref, gram_ref = refs
    panel = tree_sum([part[...].astype(F32) for part in parts]).astype(BF16)
    panel_ref[0] = panel
    gram_ref[...] = lax.dot_general(
        panel, panel, (((0,), (0,)), ((), ())), preferred_element_type=F32
    )


def text_gram_call(parts):
    rows, rank = parts[0].shape
    return pl.pallas_call(
        text_gram_kernel,
        in_specs=[VMEM] * len(parts),
        out_specs=[VMEM, VMEM],
        out_shape=[sds((1, rows, rank), BF16), sds((rank, rank), F32)],
        compiler_params=params(),
        cost_estimate=cost(2 * rows * rank * rank, 4 * rows * rank),
        name="text_gram",
    )(*parts)


def reciprocal(x):
    guess = pl.reciprocal(x, approx=True)
    guess = guess * (2.0 - x * guess)
    return guess * (2.0 - x * guess)


def inverse_factor(gram):
    n = gram.shape[0]
    blocks = n // 8
    lane = lax.broadcasted_iota(jnp.int32, (8, n), 1)
    sub = lax.broadcasted_iota(jnp.int32, (8, n), 0)
    rows = [gram[8 * i : 8 * i + 8, :] for i in range(blocks)]

    def column(x, k):
        return jnp.broadcast_to(x[:, k : k + 1], (8, n))

    def row(x, j):
        return jnp.broadcast_to(x[j : j + 1, :], (8, n))

    for b in range(blocks):
        first = 8 * b
        diag = [column(rows[b], first + j) for j in range(8)]
        below = [[column(rows[i], first + j) for j in range(8)] for i in range(b + 1, blocks)]
        lower = full = rows[b]
        pivots = scales = jnp.ones((8, n), F32)
        for j in range(8):
            k = first + j
            pivot = row(diag[j], j)
            inv = reciprocal(pivot)
            others = jnp.where(sub == j, 0.0, diag[j] * inv)
            pivot_row = jnp.where(lane == k, 1.0, row(lower, j))
            for jj in range(j + 1, 8):
                diag[jj] = diag[jj] - others * row(diag[jj], j)
            full = jnp.where(lane == k, jnp.where(sub == j, 1.0, 0.0), full) - others * pivot_row
            lower = jnp.where(sub > j, full, lower)
            pivots = jnp.where(sub == j, pivot, pivots)
            scales = jnp.where(sub == j, inv, scales)
            yield None
        full = full * scales
        solved = [row(full, j) for j in range(8)]
        inside = jnp.logical_and(lane >= first, lane < first + 8)
        for i in range(b + 1, blocks):
            terms = [c * z for c, z in zip(below[i - b - 1], solved)]
            while len(terms) > 1:
                terms = [x + y for x, y in zip(terms[::2], terms[1::2])]
            rows[i] = jnp.where(inside, 0.0, rows[i]) - terms[0]
        diagonal = sub + first
        unit = jnp.where(lane == diagonal, 1.0, jnp.where(lane < diagonal, lower, 0.0))
        rows[b] = unit * lax.rsqrt(pivots)
        yield None
    yield jnp.concatenate(rows, axis=0)


def finish_kernel(widths, n_image, ipanel, tpanel, *refs):
    *grams, iout, tout = refs

    def total(refs):
        value = refs[0][...]
        for ref in refs[1:]:
            value = value + ref[...]
        return value

    inverses = None
    for inverses in zip(inverse_factor(total(grams[:n_image])), inverse_factor(total(grams[n_image:]))):
        pass
    dims = (((1,), (1,)), ((), ()))
    for inverse, width, panel_ref, out_ref in zip(inverses, widths, (ipanel, tpanel), (iout, tout)):
        inverse = inverse * math.sqrt(width)
        high = inverse.astype(BF16)
        low = (inverse - high.astype(F32)).astype(BF16)
        panel = panel_ref[...].reshape(out_ref.shape)
        out_ref[...] = lax.dot_general(panel, high, dims, preferred_element_type=F32) + lax.dot_general(
            panel, low, dims, preferred_element_type=F32
        )


def finish_call(widths, ipanel, igrams, tpanel, tgrams):
    rank = ipanel.shape[-1]
    outs = [sds((math.prod(p.shape[:-1]), rank), F32) for p in (ipanel, tpanel)]
    return pl.pallas_call(
        functools.partial(finish_kernel, widths, len(igrams)),
        in_specs=[VMEM] * (2 + len(igrams) + len(tgrams)),
        out_specs=[VMEM] * 2,
        out_shape=outs,
        compiler_params=params(),
        cost_estimate=cost(10**10, 6 * ipanel.size),
        name="finish",
    )(ipanel, tpanel, *igrams, *tgrams)


def per_device(n_row, n_col, image_feats, text_feats, probe_image, probe_text):
    groups = n_col // 2
    me = jnp.stack([lax.axis_index("col"), lax.axis_index("row")]).astype(jnp.int32)
    col_swap = lambda x, s: lax.ppermute(x, "col", [(i, i ^ s) for i in range(n_col)])
    row_swap = lambda x, s: lax.ppermute(x, "row", [(i, i ^ s) for i in range(n_row)])
    chips, depths = list(range(1, groups)), list(range(1, n_row))
    over_chips = lambda xs: [col_swap(x, 2 * s) for x, s in zip(xs, chips)]
    over_depth = lambda xs: [row_swap(x, t) for x, t in zip(xs, depths)]

    def over_plane(x, received=None):
        got = {0: x}
        for s, block in zip(chips, received or over_chips([x] * len(chips))):
            got[2 * s] = block
        for s in list(got):
            got[s ^ 1] = col_swap(got[s], 1)
        return got

    def split_swap(x, even, odd):
        pairs = []
        for r in range(n_row):
            for c in range(n_col):
                pairs.append((r * n_col + c, (r ^ (odd if c % 2 else even)) * n_col + c))
        return lax.ppermute(x, ("row", "col"), pairs)

    fetched = [(t, t + 1, split_swap(probe_image, t, t + 1)) for t in depths[:-1:2]]
    text_feats = load_call(text_feats, LOAD_LIMITS[0])
    image_feats = load_call(image_feats, LOAD_LIMITS[1])
    text_feats, image_feats, *received = lax.optimization_barrier(
        (text_feats, image_feats, *over_chips([probe_text] * len(chips)))
    )
    text_parts = over_plane(probe_text, received)
    first, *blocks = lax.optimization_barrier((me, *[block for _, _, block in fetched]))
    half = probe_image.shape[0] // 2
    last = depths[-1]
    mine = row_swap(lax.dynamic_slice_in_dim(probe_image, me[0] % 2 * half, half, 0), last)
    image_order = [(0, 0, None)]
    image_parts = [probe_image]
    for (even, odd, _), block in zip(fetched, blocks):
        image_order += [(even, odd, None), (odd, even, None)]
        image_parts += [block, col_swap(block, 1)]
    image_order += [(last, last, 0), (last, last, 1)]

    columns = text_columns(list(text_parts), probe_text.shape[0])
    keep, send = panel_call(
        first, text_feats, image_feats, list(text_parts.values()), columns, n_row, groups, "image_panel"
    )
    own, *sends = sums_call("col", 1, chips, me, [keep, col_swap(send, 1)], "image_cores")
    own, mine = lax.optimization_barrier((own, mine))
    image_parts += [mine, col_swap(mine, 1)]
    received = over_chips(sends)
    columns = image_columns(image_order, probe_image.shape[0])
    keep, send = panel_call(
        me, image_feats, text_feats, image_parts, columns, groups, 1, "text_panel"
    )
    send, *received = lax.optimization_barrier((send, *received))
    own, *sends = sums_call("row", 0, depths, me, [own] + received, "image_plane")
    text_recv, own = lax.optimization_barrier((col_swap(send, 1), own))
    mine = last_call(own, over_depth(sends), BF16, "image_depth")
    parts = over_plane(mine)
    ipanel, gram = gram_call("col", list(parts), me, list(parts.values()), "image_gram")
    igrams = [gram] + over_depth([gram] * len(depths))

    own, *sends = sums_call("col", 0, chips, me, [keep, text_recv], "text_cores")
    own, sends = own[0], [x[0] for x in sends]
    mine = last_call(own, [x for x in over_chips(sends)], BF16, "text_plane")
    tpanel, gram = text_gram_call([mine] + over_depth([mine] * len(depths)))
    gram = last_call(gram, [col_swap(gram, 1)], F32, "text_gram_cores")
    tgrams = [gram] + over_chips([gram] * len(chips))

    widths = (image_feats.shape[1], text_feats.shape[1])
    return finish_call(widths, ipanel, igrams, tpanel, tgrams)


def solution(mesh):
    in_specs = (P(("row", "col"), None), P(("row", "col"), None), P("row", None), P("col", None))
    out_specs = (P("row", None), P("col", None))
    body = functools.partial(per_device, mesh.shape["row"], mesh.shape["col"])
    return jax.shard_map(body, mesh=mesh, in_specs=in_specs, out_specs=out_specs, check_vma=False)
```

```python
import functools
import math

import jax
import jax.numpy as jnp
from jax import lax
from jax.experimental import pallas as pl
from jax.experimental.pallas import tpu as pltpu
from jax.sharding import PartitionSpec as P

F32 = jnp.float32
BF16 = jnp.bfloat16
VMEM = pl.BlockSpec(memory_space=pltpu.VMEM)
SMEM = pl.BlockSpec(memory_space=pltpu.SMEM)
LIMIT = 16 * 1024 * 1024
LOAD_LIMITS = (4, 4)


def sds(shape, dtype):
    return jax.ShapeDtypeStruct(shape, dtype)


def params(**kw):
    return pltpu.CompilerParams(vmem_limit_bytes=LIMIT, **kw)


def cost(flops, nbytes):
    return pl.CostEstimate(flops=int(flops), bytes_accessed=int(nbytes), transcendentals=0)


def text_columns(shifts, depth):
    return lambda me_ref: [pl.multiple_of((me_ref[0] ^ s) * depth, depth) for s in shifts]


def image_columns(order, depth):
    def columns(me_ref):
        core = me_ref[0] % 2
        out = []
        for even, odd, half in order:
            at = (me_ref[1] ^ (even + core * (odd - even))) * depth
            if half is not None:
                at = pl.multiple_of(at + (core ^ half) * (depth // 2), depth // 2)
            else:
                at = pl.multiple_of(at, depth)
            out.append(at)
        return out

    return columns


def load_kernel(hbm_ref, out_ref, sem):
    move = pltpu.make_async_copy(hbm_ref, out_ref, sem)
    move.start()
    move.wait()


def load_call(x, limit):
    return pl.pallas_call(
        load_kernel,
        in_specs=[pl.BlockSpec(memory_space=pltpu.HBM)],
        out_specs=VMEM,
        out_shape=sds(x.shape, x.dtype),
        scratch_shapes=[pltpu.SemaphoreType.DMA],
        compiler_params=pltpu.CompilerParams(vmem_limit_bytes=limit * 1024 * 1024),
        cost_estimate=cost(1, 4 * x.size),
        name="load",
    )(x)


def panel_kernel(columns, n, n_out, me_ref, a_ref, b_ref, *refs):
    parts, (keep_ref, send_ref) = refs[:n], refs[n:]
    core = me_ref[0] % 2
    cols = b_ref.shape[1] // n_out // 2
    total = None
    for at, part in zip(columns(me_ref), parts):
        span = pl.ds(at, part.shape[0])
        term = jnp.dot(a_ref[:, span], part[...], preferred_element_type=F32)
        total = term if total is None else total + term
    sketch = total.T.astype(BF16)
    for i in range(n_out):
        for rel, ref in ((0, keep_ref), (1, send_ref)):
            at = pl.multiple_of((2 * i + (core ^ rel)) * cols, cols)
            out = jnp.dot(sketch, b_ref[:, pl.ds(at, cols)], preferred_element_type=F32)
            ref[i] = out.T.reshape(ref.shape[1:])


def panel_call(me, a, b, parts, columns, blocks, pieces, name):
    pairs, width = b.shape
    rank = parts[0].shape[-1]
    out = sds((blocks, pieces, width // blocks // pieces // 2, rank), F32)
    return pl.pallas_call(
        functools.partial(panel_kernel, columns, len(parts), blocks),
        in_specs=[SMEM] + [VMEM] * (2 + len(parts)),
        out_specs=[VMEM, VMEM],
        out_shape=[out, out],
        compiler_params=params(),
        cost_estimate=cost(2 * pairs * rank * (width + a.shape[1]), 2 * pairs * (width + a.shape[1])),
        name=name,
    )(me, a, b, *parts)


def sums_kernel(which, axis, shifts, n, me_ref, *refs):
    terms, (own_ref, *sends) = refs[:n], refs[n:]
    spot = me_ref[1] if which == "row" else me_ref[0] // 2

    def total(i):
        at = (slice(None),) * axis + (i,)
        value = terms[0][at]
        for term in terms[1:]:
            value = value + term[at].astype(F32)
        return value

    own_ref[...] = total(spot)
    for s, ref in zip(shifts, sends):
        ref[...] = total(spot ^ s).astype(BF16)


def sums_call(which, axis, shifts, me, terms, name):
    shape = list(terms[0].shape)
    size = terms[0].size
    del shape[axis]
    return pl.pallas_call(
        functools.partial(sums_kernel, which, axis, shifts, len(terms)),
        in_specs=[SMEM] + [VMEM] * len(terms),
        out_specs=[VMEM] * (1 + len(shifts)),
        out_shape=[sds(shape, F32)] + [sds(shape, BF16)] * len(shifts),
        compiler_params=params(),
        cost_estimate=cost(size, 4 * size * len(terms)),
        name=name,
    )(me, *terms)


def last_kernel(own_ref, *refs):
    *recv, out_ref = refs
    value = own_ref[...]
    for ref in recv:
        value = value + ref[...].astype(F32)
    out_ref[...] = value.astype(out_ref.dtype)


def last_call(own, recv, dtype, name):
    return pl.pallas_call(
        last_kernel,
        in_specs=[VMEM] * (1 + len(recv)),
        out_specs=VMEM,
        out_shape=sds(own.shape, dtype),
        compiler_params=params(),
        cost_estimate=cost(own.size, 12 * own.size),
        name=name,
    )(own, *recv)


def gram_kernel(which, order, me_ref, *refs):
    parts, (panel_ref, gram_ref) = refs[: len(order)], refs[len(order) :]
    for s, part in zip(order, parts):
        if which == "row":
            panel_ref[me_ref[1] ^ s] = part[...]
        else:
            spot = me_ref[0] ^ s
            panel_ref[spot % 2 * (len(order) // 2) + spot // 2] = part[...]
    panel = panel_ref[...].reshape(-1, gram_ref.shape[0])
    gram_ref[...] = lax.dot_general(
        panel, panel, (((0,), (0,)), ((), ())), preferred_element_type=F32
    )


def gram_call(which, order, me, parts, name):
    n = len(parts)
    rows, rank = parts[0].shape
    return pl.pallas_call(
        functools.partial(gram_kernel, which, order),
        in_specs=[SMEM] + [VMEM] * n,
        out_specs=[VMEM, VMEM],
        out_shape=[sds((n, rows, rank), BF16), sds((rank, rank), F32)],
        compiler_params=params(),
        cost_estimate=cost(2 * n * rows * rank * rank, 4 * n * rows * rank),
        name=name,
    )(me, *parts)


def tree_sum(values):
    while len(values) > 1:
        values = [x + y for x, y in zip(values[::2], values[1::2])]
    return values[0]


def text_gram_kernel(*refs):
    *parts, panel_ref, gram_ref = refs
    panel = tree_sum([part[...].astype(F32) for part in parts]).astype(BF16)
    panel_ref[0] = panel
    gram_ref[...] = lax.dot_general(
        panel, panel, (((0,), (0,)), ((), ())), preferred_element_type=F32
    )


def text_gram_call(parts):
    rows, rank = parts[0].shape
    return pl.pallas_call(
        text_gram_kernel,
        in_specs=[VMEM] * len(parts),
        out_specs=[VMEM, VMEM],
        out_shape=[sds((1, rows, rank), BF16), sds((rank, rank), F32)],
        compiler_params=params(),
        cost_estimate=cost(2 * rows * rank * rank, 4 * rows * rank),
        name="text_gram",
    )(*parts)


def inverse_factor(gram):
    n = gram.shape[0]
    lane = lax.broadcasted_iota(jnp.int32, (8, n), 1)
    sub = lax.broadcasted_iota(jnp.int32, (8, n), 0)
    rows = [gram[8 * i : 8 * i + 8, :] for i in range(n // 8)]
    for b in range(n // 8):
        cols = [
            [jnp.broadcast_to(rows[i][:, 8 * b + j : 8 * b + j + 1], (8, n)) for i in range(b, n // 8)]
            for j in range(8)
        ]
        scale = jnp.ones((8, n), F32)
        for j in range(8):
            k = 8 * b + j
            pivot = jnp.broadcast_to(cols[j][0][j : j + 1, :], (8, n))
            inv = 1.0 / pivot
            scale = jnp.where(sub == j, pivot, scale)
            pivot_row = jnp.where(lane == k, 1.0, jnp.broadcast_to(rows[b][j : j + 1, :], (8, n)))
            below = sub > j
            mult = [c * inv for c in cols[j]]
            mult[0] = jnp.where(below, mult[0], 0.0)
            for jj in range(j + 1, 8):
                entry = jnp.broadcast_to(cols[jj][0][j : j + 1, :], (8, n))
                cols[jj] = [c - m * entry for c, m in zip(cols[jj], mult)]
            for i in range(b, n // 8):
                here = lane == k
                if i == b:
                    here = jnp.logical_and(here, below)
                rows[i] = jnp.where(here, 0.0, rows[i]) - mult[i - b] * pivot_row
            yield None
        unit = jnp.where(lane == sub + 8 * b, 1.0, jnp.where(lane < sub + 8 * b, rows[b], 0.0))
        rows[b] = unit * lax.rsqrt(scale)
        yield None
    yield jnp.concatenate(rows, axis=0)


def finish_kernel(widths, n_image, ipanel, tpanel, *refs):
    *grams, iout, tout = refs

    def total(refs):
        value = refs[0][...]
        for ref in refs[1:]:
            value = value + ref[...]
        return value

    inverses = None
    for inverses in zip(inverse_factor(total(grams[:n_image])), inverse_factor(total(grams[n_image:]))):
        pass
    dims = (((1,), (1,)), ((), ()))
    for inverse, width, panel_ref, out_ref in zip(inverses, widths, (ipanel, tpanel), (iout, tout)):
        inverse = inverse * math.sqrt(width)
        high = inverse.astype(BF16)
        low = (inverse - high.astype(F32)).astype(BF16)
        panel = panel_ref[...].reshape(out_ref.shape)
        out_ref[...] = lax.dot_general(panel, high, dims, preferred_element_type=F32) + lax.dot_general(
            panel, low, dims, preferred_element_type=F32
        )


def finish_call(widths, ipanel, igrams, tpanel, tgrams):
    rank = ipanel.shape[-1]
    outs = [sds((math.prod(p.shape[:-1]), rank), F32) for p in (ipanel, tpanel)]
    return pl.pallas_call(
        functools.partial(finish_kernel, widths, len(igrams)),
        in_specs=[VMEM] * (2 + len(igrams) + len(tgrams)),
        out_specs=[VMEM] * 2,
        out_shape=outs,
        compiler_params=params(),
        cost_estimate=cost(10**10, 6 * ipanel.size),
        name="finish",
    )(ipanel, tpanel, *igrams, *tgrams)


def per_device(n_row, n_col, image_feats, text_feats, probe_image, probe_text):
    groups = n_col // 2
    me = jnp.stack([lax.axis_index("col"), lax.axis_index("row")]).astype(jnp.int32)
    col_swap = lambda x, s: lax.ppermute(x, "col", [(i, i ^ s) for i in range(n_col)])
    row_swap = lambda x, s: lax.ppermute(x, "row", [(i, i ^ s) for i in range(n_row)])
    chips, depths = list(range(1, groups)), list(range(1, n_row))
    over_chips = lambda xs: [col_swap(x, 2 * s) for x, s in zip(xs, chips)]
    over_depth = lambda xs: [row_swap(x, t) for x, t in zip(xs, depths)]

    def over_plane(x, received=None):
        got = {0: x}
        for s, block in zip(chips, received or over_chips([x] * len(chips))):
            got[2 * s] = block
        for s in list(got):
            got[s ^ 1] = col_swap(got[s], 1)
        return got

    def split_swap(x, even, odd):
        pairs = []
        for r in range(n_row):
            for c in range(n_col):
                pairs.append((r * n_col + c, (r ^ (odd if c % 2 else even)) * n_col + c))
        return lax.ppermute(x, ("row", "col"), pairs)

    fetched = [(t, t + 1, split_swap(probe_image, t, t + 1)) for t in depths[:-1:2]]
    text_feats = load_call(text_feats, LOAD_LIMITS[0])
    image_feats = load_call(image_feats, LOAD_LIMITS[1])
    text_feats, image_feats, *received = lax.optimization_barrier(
        (text_feats, image_feats, *over_chips([probe_text] * len(chips)))
    )
    text_parts = over_plane(probe_text, received)
    first, *blocks = lax.optimization_barrier((me, *[block for _, _, block in fetched]))
    half = probe_image.shape[0] // 2
    last = depths[-1]
    mine = row_swap(lax.dynamic_slice_in_dim(probe_image, me[0] % 2 * half, half, 0), last)
    image_order = [(0, 0, None)]
    image_parts = [probe_image]
    for (even, odd, _), block in zip(fetched, blocks):
        image_order += [(even, odd, None), (odd, even, None)]
        image_parts += [block, col_swap(block, 1)]
    image_order += [(last, last, 0), (last, last, 1)]

    columns = text_columns(list(text_parts), probe_text.shape[0])
    keep, send = panel_call(
        first, text_feats, image_feats, list(text_parts.values()), columns, n_row, groups, "image_panel"
    )
    own, *sends = sums_call("col", 1, chips, me, [keep, col_swap(send, 1)], "image_cores")
    received = over_chips(sends)
    mine, *received = lax.optimization_barrier((mine, *received))
    image_parts += [mine, col_swap(mine, 1)]
    columns = image_columns(image_order, probe_image.shape[0])
    keep, send = panel_call(
        me, image_feats, text_feats, image_parts, columns, groups, 1, "text_panel"
    )
    send, *received = lax.optimization_barrier((send, *received))
    own, *sends = sums_call("row", 0, depths, me, [own] + received, "image_plane")
    text_recv, own = lax.optimization_barrier((col_swap(send, 1), own))
    mine = last_call(own, over_depth(sends), BF16, "image_depth")
    parts = over_plane(mine)
    ipanel, gram = gram_call("col", list(parts), me, list(parts.values()), "image_gram")
    igrams = [gram] + over_depth([gram] * len(depths))

    own, *sends = sums_call("col", 0, chips, me, [keep, text_recv], "text_cores")
    own, sends = own[0], [x[0] for x in sends]
    mine = last_call(own, [x for x in over_chips(sends)], BF16, "text_plane")
    tpanel, gram = text_gram_call([mine] + over_depth([mine] * len(depths)))
    gram = last_call(gram, [col_swap(gram, 1)], F32, "text_gram_cores")
    tgrams = [gram] + over_chips([gram] * len(chips))

    widths = (image_feats.shape[1], text_feats.shape[1])
    return finish_call(widths, ipanel, igrams, tpanel, tgrams)


def solution(mesh):
    in_specs = (P(("row", "col"), None), P(("row", "col"), None), P("row", None), P("col", None))
    out_specs = (P("row", None), P("col", None))
    body = functools.partial(per_device, mesh.shape["row"], mesh.shape["col"])
    return jax.shard_map(body, mesh=mesh, in_specs=in_specs, out_specs=out_specs, check_vma=False)
```

```python
import functools
import math

import jax
import jax.numpy as jnp
from jax import lax
from jax.experimental import pallas as pl
from jax.experimental.pallas import tpu as pltpu
from jax.sharding import PartitionSpec as P

F32 = jnp.float32
BF16 = jnp.bfloat16
VMEM = pl.BlockSpec(memory_space=pltpu.VMEM)
SMEM = pl.BlockSpec(memory_space=pltpu.SMEM)
LIMIT = 32 * 1024 * 1024
PANEL_LIMIT = 46 * 1024 * 1024


def sds(shape, dtype):
    return jax.ShapeDtypeStruct(shape, dtype)


def params(**kw):
    return pltpu.CompilerParams(vmem_limit_bytes=LIMIT, **kw)


def cost(flops, nbytes):
    return pl.CostEstimate(flops=int(flops), bytes_accessed=int(nbytes), transcendentals=0)


def text_rows(shifts, depth):
    return lambda me_ref: [pl.multiple_of((me_ref[0] ^ s) * depth, depth) for s in shifts]


def image_rows(order, depth):
    def rows(me_ref):
        core = me_ref[0] % 2
        out = []
        for even, odd, half in order:
            at = (me_ref[1] ^ (even + core * (odd - even))) * depth
            if half is not None:
                at = pl.multiple_of(at + (core ^ half) * (depth // 2), depth // 2)
            else:
                at = pl.multiple_of(at, depth)
            out.append(at)
        return out

    return rows


def panel_kernel(rows, n, n_in, n_out, me_ref, a_hbm, b_hbm, *refs):
    parts, (keep_ref, send_ref, a_ref, b_ref, probe, a_sem, b_sem) = refs[:n], refs[n:]
    core = me_ref[0] % 2
    tall = a_ref.shape[0] // n_in
    cols = b_ref.shape[1] // n_out // 2
    moves = []
    for i in range(n_in):
        span = pl.ds(i * tall, tall)
        moves.append(pltpu.make_async_copy(a_hbm.at[span], a_ref.at[span], a_sem.at[i]))
    for i in range(n_out):
        span = pl.ds(2 * i * cols, 2 * cols)
        moves.append(pltpu.make_async_copy(b_hbm.at[:, span], b_ref.at[:, span], b_sem.at[i]))
    for move in moves:
        move.start()
    for at, part in zip(rows(me_ref), parts):
        probe[pl.ds(at, part.shape[0]), :] = part[...]
    sketches = []
    for i in range(n_in):
        moves[i].wait()
        chunk = a_ref[i * tall : i * tall + tall, :]
        sketches.append(jnp.dot(chunk, probe[...], preferred_element_type=F32))
    sketch = jnp.concatenate(sketches, axis=0).T.astype(BF16)
    for i in range(n_out):
        moves[n_in + i].wait()
        for rel, ref in ((0, keep_ref), (1, send_ref)):
            at = pl.multiple_of((2 * i + (core ^ rel)) * cols, cols)
            out = jnp.dot(sketch, b_ref[:, pl.ds(at, cols)], preferred_element_type=F32)
            ref[i] = out.T.reshape(ref.shape[1:])


def panel_call(me, a, b, parts, rows, blocks, pieces, name):
    pairs, width = b.shape
    rank = parts[0].shape[-1]
    out = sds((blocks, pieces, width // blocks // pieces // 2, rank), F32)
    hbm = pl.BlockSpec(memory_space=pltpu.HBM)
    n_in = 3 if pairs % 48 == 0 else 1
    return pl.pallas_call(
        functools.partial(panel_kernel, rows, len(parts), n_in, blocks),
        in_specs=[SMEM, hbm, hbm] + [VMEM] * len(parts),
        out_specs=[VMEM, VMEM],
        out_shape=[out, out],
        scratch_shapes=[
            pltpu.VMEM(a.shape, BF16),
            pltpu.VMEM(b.shape, BF16),
            pltpu.VMEM((a.shape[1], rank), BF16),
            pltpu.SemaphoreType.DMA((n_in,)),
            pltpu.SemaphoreType.DMA((blocks,)),
        ],
        compiler_params=pltpu.CompilerParams(vmem_limit_bytes=PANEL_LIMIT),
        cost_estimate=cost(2 * pairs * rank * (width + a.shape[1]), 2 * pairs * (width + a.shape[1])),
        name=name,
    )(me, a, b, *parts)


def sums_kernel(which, axis, shifts, n, me_ref, *refs):
    terms, (own_ref, *sends) = refs[:n], refs[n:]
    spot = me_ref[1] if which == "row" else me_ref[0] // 2

    def total(i):
        at = (slice(None),) * axis + (i,)
        value = terms[0][at]
        for term in terms[1:]:
            value = value + term[at].astype(F32)
        return value

    own_ref[...] = total(spot)
    for s, ref in zip(shifts, sends):
        ref[...] = total(spot ^ s).astype(BF16)


def sums_call(which, axis, shifts, me, terms, name):
    shape = list(terms[0].shape)
    size = terms[0].size
    del shape[axis]
    return pl.pallas_call(
        functools.partial(sums_kernel, which, axis, shifts, len(terms)),
        in_specs=[SMEM] + [VMEM] * len(terms),
        out_specs=[VMEM] * (1 + len(shifts)),
        out_shape=[sds(shape, F32)] + [sds(shape, BF16)] * len(shifts),
        compiler_params=params(),
        cost_estimate=cost(size, 4 * size * len(terms)),
        name=name,
    )(me, *terms)


def last_kernel(own_ref, *refs):
    *recv, out_ref = refs
    value = own_ref[...]
    for ref in recv:
        value = value + ref[...].astype(F32)
    out_ref[...] = value.astype(out_ref.dtype)


def last_call(own, recv, dtype, name):
    return pl.pallas_call(
        last_kernel,
        in_specs=[VMEM] * (1 + len(recv)),
        out_specs=VMEM,
        out_shape=sds(own.shape, dtype),
        compiler_params=params(),
        cost_estimate=cost(own.size, 12 * own.size),
        name=name,
    )(own, *recv)


def gram_kernel(which, order, me_ref, *refs):
    parts, (panel_ref, gram_ref) = refs[: len(order)], refs[len(order) :]
    for s, part in zip(order, parts):
        if which == "row":
            panel_ref[me_ref[1] ^ s] = part[...]
        else:
            spot = me_ref[0] ^ s
            panel_ref[spot % 2 * (len(order) // 2) + spot // 2] = part[...]
    panel = panel_ref[...].reshape(-1, gram_ref.shape[0])
    gram_ref[...] = lax.dot_general(
        panel, panel, (((0,), (0,)), ((), ())), preferred_element_type=F32
    )


def gram_call(which, order, me, parts, name):
    n = len(parts)
    rows, rank = parts[0].shape
    return pl.pallas_call(
        functools.partial(gram_kernel, which, order),
        in_specs=[SMEM] + [VMEM] * n,
        out_specs=[VMEM, VMEM],
        out_shape=[sds((n, rows, rank), BF16), sds((rank, rank), F32)],
        compiler_params=params(),
        cost_estimate=cost(2 * n * rows * rank * rank, 4 * n * rows * rank),
        name=name,
    )(me, *parts)


def tree_sum(values):
    while len(values) > 1:
        values = [x + y for x, y in zip(values[::2], values[1::2])]
    return values[0]


def text_gram_kernel(*refs):
    *parts, panel_ref, gram_ref = refs
    panel = tree_sum([part[...].astype(F32) for part in parts]).astype(BF16)
    panel_ref[0] = panel
    gram_ref[...] = lax.dot_general(
        panel, panel, (((0,), (0,)), ((), ())), preferred_element_type=F32
    )


def text_gram_call(parts):
    rows, rank = parts[0].shape
    return pl.pallas_call(
        text_gram_kernel,
        in_specs=[VMEM] * len(parts),
        out_specs=[VMEM, VMEM],
        out_shape=[sds((1, rows, rank), BF16), sds((rank, rank), F32)],
        compiler_params=params(),
        cost_estimate=cost(2 * rows * rank * rank, 4 * rows * rank),
        name="text_gram",
    )(*parts)


def inverse_factor(gram):
    n = gram.shape[0]
    lane = lax.broadcasted_iota(jnp.int32, (8, n), 1)
    sub = lax.broadcasted_iota(jnp.int32, (8, n), 0)
    rows = [gram[8 * i : 8 * i + 8, :] for i in range(n // 8)]
    for b in range(n // 8):
        cols = [
            [jnp.broadcast_to(rows[i][:, 8 * b + j : 8 * b + j + 1], (8, n)) for i in range(b, n // 8)]
            for j in range(8)
        ]
        scale = jnp.ones((8, n), F32)
        for j in range(8):
            k = 8 * b + j
            pivot = jnp.broadcast_to(cols[j][0][j : j + 1, :], (8, n))
            guess = pl.reciprocal(pivot, approx=True)
            inv = guess * (2.0 - pivot * guess)
            scale = jnp.where(sub == j, pivot, scale)
            pivot_row = jnp.where(lane == k, 1.0, jnp.broadcast_to(rows[b][j : j + 1, :], (8, n)))
            below = sub > j
            mult = [c * inv for c in cols[j]]
            mult[0] = jnp.where(below, mult[0], 0.0)
            for jj in range(j + 1, 8):
                entry = jnp.broadcast_to(cols[jj][0][j : j + 1, :], (8, n))
                cols[jj] = [c - m * entry for c, m in zip(cols[jj], mult)]
            for i in range(b, n // 8):
                here = lane == k
                if i == b:
                    here = jnp.logical_and(here, below)
                rows[i] = jnp.where(here, 0.0, rows[i]) - mult[i - b] * pivot_row
            yield None
        unit = jnp.where(lane == sub + 8 * b, 1.0, jnp.where(lane < sub + 8 * b, rows[b], 0.0))
        rows[b] = unit * lax.rsqrt(scale)
        yield None
    yield jnp.concatenate(rows, axis=0)


def finish_kernel(widths, n_image, ipanel, tpanel, *refs):
    *grams, iout, tout = refs

    def total(refs):
        value = refs[0][...]
        for ref in refs[1:]:
            value = value + ref[...]
        return value

    inverses = None
    for inverses in zip(inverse_factor(total(grams[:n_image])), inverse_factor(total(grams[n_image:]))):
        pass
    dims = (((1,), (1,)), ((), ()))
    for inverse, width, panel_ref, out_ref in zip(inverses, widths, (ipanel, tpanel), (iout, tout)):
        inverse = inverse * math.sqrt(width)
        high = inverse.astype(BF16)
        low = (inverse - high.astype(F32)).astype(BF16)
        panel = panel_ref[...].reshape(out_ref.shape)
        out_ref[...] = lax.dot_general(panel, high, dims, preferred_element_type=F32) + lax.dot_general(
            panel, low, dims, preferred_element_type=F32
        )


def finish_call(widths, ipanel, igrams, tpanel, tgrams):
    rank = ipanel.shape[-1]
    outs = [sds((math.prod(p.shape[:-1]), rank), F32) for p in (ipanel, tpanel)]
    return pl.pallas_call(
        functools.partial(finish_kernel, widths, len(igrams)),
        in_specs=[VMEM] * (2 + len(igrams) + len(tgrams)),
        out_specs=[VMEM] * 2,
        out_shape=outs,
        compiler_params=params(),
        cost_estimate=cost(10**10, 6 * ipanel.size),
        name="finish",
    )(ipanel, tpanel, *igrams, *tgrams)


def per_device(n_row, n_col, image_feats, text_feats, probe_image, probe_text):
    groups = n_col // 2
    me = jnp.stack([lax.axis_index("col"), lax.axis_index("row")]).astype(jnp.int32)
    col_swap = lambda x, s: lax.ppermute(x, "col", [(i, i ^ s) for i in range(n_col)])
    row_swap = lambda x, s: lax.ppermute(x, "row", [(i, i ^ s) for i in range(n_row)])
    chips, depths = list(range(1, groups)), list(range(1, n_row))
    over_chips = lambda xs: [col_swap(x, 2 * s) for x, s in zip(xs, chips)]
    over_depth = lambda xs: [row_swap(x, t) for x, t in zip(xs, depths)]

    def over_plane(x):
        got = {0: x}
        for s, block in zip(chips, over_chips([x] * len(chips))):
            got[2 * s] = block
        for s in list(got):
            got[s ^ 1] = col_swap(got[s], 1)
        return got

    def split_swap(x, even, odd):
        pairs = []
        for r in range(n_row):
            for c in range(n_col):
                pairs.append((r * n_col + c, (r ^ (odd if c % 2 else even)) * n_col + c))
        return lax.ppermute(x, ("row", "col"), pairs)

    fetched = [(t, t + 1, split_swap(probe_image, t, t + 1)) for t in depths[:-1:2]]
    text_parts = over_plane(probe_text)
    first, *blocks = lax.optimization_barrier((me, *[block for _, _, block in fetched]))
    half = probe_image.shape[0] // 2
    last = depths[-1]
    mine = row_swap(lax.dynamic_slice_in_dim(probe_image, me[0] % 2 * half, half, 0), last)
    image_order = [(0, 0, None)]
    image_parts = [probe_image]
    for (even, odd, _), block in zip(fetched, blocks):
        image_order += [(even, odd, None), (odd, even, None)]
        image_parts += [block, col_swap(block, 1)]
    image_order += [(last, last, 0), (last, last, 1)]

    columns = text_rows(list(text_parts), probe_text.shape[0])
    keep, send = panel_call(
        first, text_feats, image_feats, list(text_parts.values()), columns, n_row, groups, "image_panel"
    )
    send, mine = lax.optimization_barrier((send, mine))
    image_parts += [mine, col_swap(mine, 1)]
    own, *image_sends = sums_call("col", 1, chips, me, [keep, col_swap(send, 1)], "image_cores")
    own, *sends = sums_call("row", 0, depths, me, [own] + over_chips(image_sends), "image_plane")
    after_plane = sends[0]
    mine = last_call(own, over_depth(sends), BF16, "image_depth")
    parts = over_plane(mine)
    ipanel, gram = gram_call("col", list(parts), me, list(parts.values()), "image_gram")
    igrams = [gram] + over_depth([gram] * len(depths))

    columns = image_rows(image_order, probe_image.shape[0])
    keep, send = panel_call(
        me, image_feats, text_feats, image_parts, columns, groups, 1, "text_panel"
    )
    swapped, _ = lax.optimization_barrier((col_swap(send, 1), image_sends[0]))
    own, *sends = sums_call("col", 0, chips, me, [keep, swapped], "text_cores")
    own, sends = own[0], [x[0] for x in sends]
    own, _ = lax.optimization_barrier((own, after_plane))
    mine = last_call(own, over_chips(sends), BF16, "text_plane")
    tpanel, gram = text_gram_call([mine] + over_depth([mine] * len(depths)))
    gram = last_call(gram, [col_swap(gram, 1)], F32, "text_gram_cores")
    tgrams = [gram] + over_chips([gram] * len(chips))

    widths = (image_feats.shape[1], text_feats.shape[1])
    return finish_call(widths, ipanel, igrams, tpanel, tgrams)


def solution(mesh):
    in_specs = (P(("row", "col"), None), P(("row", "col"), None), P("row", None), P("col", None))
    out_specs = (P("row", None), P("col", None))
    body = functools.partial(per_device, mesh.shape["row"], mesh.shape["col"])
    return jax.shard_map(body, mesh=mesh, in_specs=in_specs, out_specs=out_specs, check_vma=False)
```

```python
import functools
import math

import jax
import jax.numpy as jnp
from jax import lax
from jax.experimental import pallas as pl
from jax.experimental.pallas import tpu as pltpu
from jax.sharding import PartitionSpec as P

F32 = jnp.float32
BF16 = jnp.bfloat16
VMEM = pl.BlockSpec(memory_space=pltpu.VMEM)
SMEM = pl.BlockSpec(memory_space=pltpu.SMEM)
LIMIT = 32 * 1024 * 1024
PANEL_LIMIT = 46 * 1024 * 1024


def sds(shape, dtype):
    return jax.ShapeDtypeStruct(shape, dtype)


def params(**kw):
    return pltpu.CompilerParams(vmem_limit_bytes=LIMIT, **kw)


def cost(flops, nbytes):
    return pl.CostEstimate(flops=int(flops), bytes_accessed=int(nbytes), transcendentals=0)


def text_rows(shifts, depth):
    return lambda me_ref: [pl.multiple_of((me_ref[0] ^ s) * depth, depth) for s in shifts]


def image_rows(order, depth):
    def rows(me_ref):
        core = me_ref[0] % 2
        out = []
        for even, odd, half in order:
            at = (me_ref[1] ^ (even + core * (odd - even))) * depth
            if half is not None:
                at = pl.multiple_of(at + (core ^ half) * (depth // 2), depth // 2)
            else:
                at = pl.multiple_of(at, depth)
            out.append(at)
        return out

    return rows


def panel_kernel(rows, n, n_in, n_out, me_ref, a_hbm, b_hbm, *refs):
    parts, (keep_ref, send_ref, a_ref, b_ref, probe, a_sem, b_sem, own_sem) = refs[:n], refs[n:]
    core = me_ref[0] % 2
    tall = a_ref.shape[0] // n_in
    cols = b_ref.shape[1] // n_out // 2
    moves = []
    for i in range(n_in):
        span = pl.ds(i * tall, tall)
        moves.append(pltpu.make_async_copy(a_hbm.at[span], a_ref.at[span], a_sem.at[i]))
    for i in range(n_out):
        span = pl.ds(2 * i * cols, 2 * cols)
        moves.append(pltpu.make_async_copy(b_hbm.at[:, span], b_ref.at[:, span], b_sem.at[i]))
    places = rows(me_ref)
    own = pltpu.make_async_copy(parts[0], probe.at[pl.ds(places[0], parts[0].shape[0])], own_sem)
    own.start()
    for move in moves:
        move.start()
    for at, part in zip(places[1:], parts[1:]):
        probe[pl.ds(at, part.shape[0]), :] = part[...]
    own.wait()
    sketches = []
    for i in range(n_in):
        moves[i].wait()
        chunk = a_ref[i * tall : i * tall + tall, :]
        sketches.append(jnp.dot(chunk, probe[...], preferred_element_type=F32))
    sketch = jnp.concatenate(sketches, axis=0).T.astype(BF16)
    for i in range(n_out):
        moves[n_in + i].wait()
        for rel, ref in ((0, keep_ref), (1, send_ref)):
            at = pl.multiple_of((2 * i + (core ^ rel)) * cols, cols)
            out = jnp.dot(sketch, b_ref[:, pl.ds(at, cols)], preferred_element_type=F32)
            ref[i] = out.T.reshape(ref.shape[1:])


def panel_call(me, a, b, parts, rows, blocks, pieces, name):
    pairs, width = b.shape
    rank = parts[0].shape[-1]
    out = sds((blocks, pieces, width // blocks // pieces // 2, rank), F32)
    hbm = pl.BlockSpec(memory_space=pltpu.HBM)
    n_in = 3 if pairs % 48 == 0 else 1
    return pl.pallas_call(
        functools.partial(panel_kernel, rows, len(parts), n_in, blocks),
        in_specs=[SMEM, hbm, hbm, hbm] + [VMEM] * (len(parts) - 1),
        out_specs=[VMEM, VMEM],
        out_shape=[out, out],
        scratch_shapes=[
            pltpu.VMEM(a.shape, BF16),
            pltpu.VMEM(b.shape, BF16),
            pltpu.VMEM((a.shape[1], rank), BF16),
            pltpu.SemaphoreType.DMA((n_in,)),
            pltpu.SemaphoreType.DMA((blocks,)),
            pltpu.SemaphoreType.DMA,
        ],
        compiler_params=pltpu.CompilerParams(vmem_limit_bytes=PANEL_LIMIT),
        cost_estimate=cost(2 * pairs * rank * (width + a.shape[1]), 2 * pairs * (width + a.shape[1])),
        name=name,
    )(me, a, b, *parts)


def sums_kernel(which, axis, shifts, n, me_ref, *refs):
    terms, (own_ref, *sends) = refs[:n], refs[n:]
    spot = me_ref[1] if which == "row" else me_ref[0] // 2

    def total(i):
        at = (slice(None),) * axis + (i,)
        value = terms[0][at]
        for term in terms[1:]:
            value = value + term[at].astype(F32)
        return value

    own_ref[...] = total(spot)
    for s, ref in zip(shifts, sends):
        ref[...] = total(spot ^ s).astype(BF16)


def sums_call(which, axis, shifts, me, terms, name):
    shape = list(terms[0].shape)
    size = terms[0].size
    del shape[axis]
    return pl.pallas_call(
        functools.partial(sums_kernel, which, axis, shifts, len(terms)),
        in_specs=[SMEM] + [VMEM] * len(terms),
        out_specs=[VMEM] * (1 + len(shifts)),
        out_shape=[sds(shape, F32)] + [sds(shape, BF16)] * len(shifts),
        compiler_params=params(),
        cost_estimate=cost(size, 4 * size * len(terms)),
        name=name,
    )(me, *terms)


def last_kernel(own_ref, *refs):
    *recv, out_ref = refs
    value = own_ref[...]
    for ref in recv:
        value = value + ref[...].astype(F32)
    out_ref[...] = value.astype(out_ref.dtype)


def last_call(own, recv, dtype, name):
    return pl.pallas_call(
        last_kernel,
        in_specs=[VMEM] * (1 + len(recv)),
        out_specs=VMEM,
        out_shape=sds(own.shape, dtype),
        compiler_params=params(),
        cost_estimate=cost(own.size, 12 * own.size),
        name=name,
    )(own, *recv)


def gram_kernel(which, order, me_ref, *refs):
    parts, (panel_ref, gram_ref) = refs[: len(order)], refs[len(order) :]
    for s, part in zip(order, parts):
        if which == "row":
            panel_ref[me_ref[1] ^ s] = part[...]
        else:
            spot = me_ref[0] ^ s
            panel_ref[spot % 2 * (len(order) // 2) + spot // 2] = part[...]
    panel = panel_ref[...].reshape(-1, gram_ref.shape[0])
    gram_ref[...] = lax.dot_general(
        panel, panel, (((0,), (0,)), ((), ())), preferred_element_type=F32
    )


def gram_call(which, order, me, parts, name):
    n = len(parts)
    rows, rank = parts[0].shape
    return pl.pallas_call(
        functools.partial(gram_kernel, which, order),
        in_specs=[SMEM] + [VMEM] * n,
        out_specs=[VMEM, VMEM],
        out_shape=[sds((n, rows, rank), BF16), sds((rank, rank), F32)],
        compiler_params=params(),
        cost_estimate=cost(2 * n * rows * rank * rank, 4 * n * rows * rank),
        name=name,
    )(me, *parts)


def inverse_factor(gram):
    n = gram.shape[0]
    lane = lax.broadcasted_iota(jnp.int32, (8, n), 1)
    sub = lax.broadcasted_iota(jnp.int32, (8, n), 0)
    rows = [gram[8 * i : 8 * i + 8, :] for i in range(n // 8)]
    for b in range(n // 8):
        cols = [
            [jnp.broadcast_to(rows[i][:, 8 * b + j : 8 * b + j + 1], (8, n)) for i in range(b, n // 8)]
            for j in range(8)
        ]
        scale = jnp.ones((8, n), F32)
        for j in range(8):
            k = 8 * b + j
            pivot = jnp.broadcast_to(cols[j][0][j : j + 1, :], (8, n))
            guess = pl.reciprocal(pivot, approx=True)
            inv = guess * (2.0 - pivot * guess)
            scale = jnp.where(sub == j, pivot, scale)
            pivot_row = jnp.where(lane == k, 1.0, jnp.broadcast_to(rows[b][j : j + 1, :], (8, n)))
            below = sub > j
            mult = [c * inv for c in cols[j]]
            mult[0] = jnp.where(below, mult[0], 0.0)
            for jj in range(j + 1, 8):
                entry = jnp.broadcast_to(cols[jj][0][j : j + 1, :], (8, n))
                cols[jj] = [c - m * entry for c, m in zip(cols[jj], mult)]
            for i in range(b, n // 8):
                here = lane == k
                if i == b:
                    here = jnp.logical_and(here, below)
                rows[i] = jnp.where(here, 0.0, rows[i]) - mult[i - b] * pivot_row
            yield None
        unit = jnp.where(lane == sub + 8 * b, 1.0, jnp.where(lane < sub + 8 * b, rows[b], 0.0))
        rows[b] = unit * lax.rsqrt(scale)
        yield None
    yield jnp.concatenate(rows, axis=0)


def finish_kernel(widths, n_image, ipanel, tpanel, *refs):
    *grams, iout, tout = refs

    def total(refs):
        value = refs[0][...]
        for ref in refs[1:]:
            value = value + ref[...]
        return value

    inverses = None
    for inverses in zip(inverse_factor(total(grams[:n_image])), inverse_factor(total(grams[n_image:]))):
        pass
    dims = (((1,), (1,)), ((), ()))
    for inverse, width, panel_ref, out_ref in zip(inverses, widths, (ipanel, tpanel), (iout, tout)):
        inverse = inverse * math.sqrt(width)
        high = inverse.astype(BF16)
        low = (inverse - high.astype(F32)).astype(BF16)
        panel = panel_ref[...].reshape(out_ref.shape)
        out_ref[...] = lax.dot_general(panel, high, dims, preferred_element_type=F32) + lax.dot_general(
            panel, low, dims, preferred_element_type=F32
        )


def finish_call(widths, ipanel, igrams, tpanel, tgrams):
    rank = ipanel.shape[-1]
    outs = [sds((math.prod(p.shape[:-1]), rank), F32) for p in (ipanel, tpanel)]
    return pl.pallas_call(
        functools.partial(finish_kernel, widths, len(igrams)),
        in_specs=[VMEM] * (2 + len(igrams) + len(tgrams)),
        out_specs=[VMEM] * 2,
        out_shape=outs,
        compiler_params=params(),
        cost_estimate=cost(10**10, 6 * ipanel.size),
        name="finish",
    )(ipanel, tpanel, *igrams, *tgrams)


def per_device(n_row, n_col, image_feats, text_feats, probe_image, probe_text):
    groups = n_col // 2
    me = jnp.stack([lax.axis_index("col"), lax.axis_index("row")]).astype(jnp.int32)
    col_swap = lambda x, s: lax.ppermute(x, "col", [(i, i ^ s) for i in range(n_col)])
    row_swap = lambda x, s: lax.ppermute(x, "row", [(i, i ^ s) for i in range(n_row)])
    chips, depths = list(range(1, groups)), list(range(1, n_row))
    over_chips = lambda xs: [col_swap(x, 2 * s) for x, s in zip(xs, chips)]
    over_depth = lambda xs: [row_swap(x, t) for x, t in zip(xs, depths)]

    def over_plane(x, received=None):
        got = {0: x}
        for s, block in zip(chips, received or over_chips([x] * len(chips))):
            got[2 * s] = block
        for s in list(got):
            got[s ^ 1] = col_swap(got[s], 1)
        return got

    def split_swap(x, even, odd):
        pairs = []
        for r in range(n_row):
            for c in range(n_col):
                pairs.append((r * n_col + c, (r ^ (odd if c % 2 else even)) * n_col + c))
        return lax.ppermute(x, ("row", "col"), pairs)

    fetched = [(t, t + 1, split_swap(probe_image, t, t + 1)) for t in depths[:-1:2]]
    half = probe_image.shape[0] // 2
    mine = lax.dynamic_slice_in_dim(probe_image, me[0] % 2 * half, half, 0)
    received = over_chips([probe_text] * len(chips))
    mine, received[-1] = lax.optimization_barrier((mine, received[-1]))
    text_parts = over_plane(probe_text, received)
    first, *blocks = lax.optimization_barrier((me, *[block for _, _, block in fetched]))
    last = depths[-1]
    mine = row_swap(mine, last)
    image_order = [(0, 0, None)]
    image_parts = [probe_image]

    columns = text_rows(list(text_parts), probe_text.shape[0])
    keep, send = panel_call(
        first, text_feats, image_feats, list(text_parts.values()), columns, n_row, groups, "image_panel"
    )
    send, mine, *blocks = lax.optimization_barrier((send, mine, *blocks))
    swapped = [col_swap(block, 1) for block in blocks]
    send, other, *swapped = lax.optimization_barrier((send, col_swap(mine, 1), *swapped))
    for (even, odd, _), block, twin in zip(fetched, blocks, swapped):
        image_order += [(even, odd, None), (odd, even, None)]
        image_parts += [block, twin]
    image_order += [(last, last, 0), (last, last, 1)]
    image_parts += [mine, other]
    own, *image_sends = sums_call("col", 1, chips, me, [keep, col_swap(send, 1)], "image_cores")
    own, *sends = sums_call("row", 0, depths, me, [own] + over_chips(image_sends), "image_plane")
    after_plane = sends[0]
    mine = last_call(own, over_depth(sends), BF16, "image_depth")
    after_depth = mine
    parts = over_plane(mine)
    ipanel, gram = gram_call("col", list(parts), me, list(parts.values()), "image_gram")
    igrams = [gram] + over_depth([gram] * len(depths))

    columns = image_rows(image_order, probe_image.shape[0])
    keep, send = panel_call(
        me, image_feats, text_feats, image_parts, columns, groups, n_row, "text_panel"
    )
    swapped, _ = lax.optimization_barrier((col_swap(send, 1), image_sends[0]))
    own, *sends = sums_call("row", 1, depths, me, [keep, swapped], "text_cores")
    own, _ = lax.optimization_barrier((own, after_plane))
    own, *sends = sums_call("col", 0, chips, me, [own] + over_depth(sends), "text_depth")
    own, _ = lax.optimization_barrier((own, after_depth))
    mine = last_call(own, over_chips(sends), BF16, "text_plane")
    parts = [mine] + over_depth([mine] * len(depths))
    tpanel, gram = gram_call("row", [0] + depths, me, parts, "text_gram")
    gram = last_call(gram, [col_swap(gram, 1)], F32, "text_gram_cores")
    tgrams = [gram] + over_chips([gram] * len(chips))

    widths = (image_feats.shape[1], text_feats.shape[1])
    return finish_call(widths, ipanel, igrams, tpanel, tgrams)


def solution(mesh):
    in_specs = (P(("row", "col"), None), P(("row", "col"), None), P("row", None), P("col", None))
    out_specs = (P("row", None), P("col", None))
    body = functools.partial(per_device, mesh.shape["row"], mesh.shape["col"])
    return jax.shard_map(body, mesh=mesh, in_specs=in_specs, out_specs=out_specs, check_vma=False)
```

```python
import functools
import math

import jax
import jax.numpy as jnp
from jax import lax
from jax.experimental import pallas as pl
from jax.experimental.pallas import tpu as pltpu
from jax.sharding import PartitionSpec as P

F32 = jnp.float32
BF16 = jnp.bfloat16
VMEM = pl.BlockSpec(memory_space=pltpu.VMEM)
SMEM = pl.BlockSpec(memory_space=pltpu.SMEM)
LIMIT = 32 * 1024 * 1024
PANEL_LIMIT = 46 * 1024 * 1024


def sds(shape, dtype):
    return jax.ShapeDtypeStruct(shape, dtype)


def params(**kw):
    return pltpu.CompilerParams(vmem_limit_bytes=LIMIT, **kw)


def cost(flops, nbytes):
    return pl.CostEstimate(flops=int(flops), bytes_accessed=int(nbytes), transcendentals=0)


def text_rows(shifts, depth):
    return lambda me_ref: [pl.multiple_of((me_ref[0] ^ s) * depth, depth) for s in shifts]


def image_rows(order, depth):
    def rows(me_ref):
        core = me_ref[0] % 2
        out = []
        for even, odd, half in order:
            at = (me_ref[1] ^ (even + core * (odd - even))) * depth
            if half is not None:
                at = pl.multiple_of(at + (core ^ half) * (depth // 2), depth // 2)
            else:
                at = pl.multiple_of(at, depth)
            out.append(at)
        return out

    return rows


def panel_kernel(rows, n, n_in, n_out, me_ref, a_hbm, b_hbm, *refs):
    parts, (keep_ref, send_ref, a_ref, b_ref, probe, a_sem, b_sem, own_sem) = refs[:n], refs[n:]
    core = me_ref[0] % 2
    tall = a_ref.shape[0] // n_in
    cols = b_ref.shape[1] // n_out // 2
    moves = []
    for i in range(n_in):
        span = pl.ds(i * tall, tall)
        moves.append(pltpu.make_async_copy(a_hbm.at[span], a_ref.at[span], a_sem.at[i]))
    for i in range(n_out):
        span = pl.ds(2 * i * cols, 2 * cols)
        moves.append(pltpu.make_async_copy(b_hbm.at[:, span], b_ref.at[:, span], b_sem.at[i]))
    places = rows(me_ref)
    own = pltpu.make_async_copy(parts[0], probe.at[pl.ds(places[0], parts[0].shape[0])], own_sem)
    own.start()
    for move in moves:
        move.start()
    for at, part in zip(places[1:], parts[1:]):
        probe[pl.ds(at, part.shape[0]), :] = part[...]
    own.wait()
    sketches = []
    for i in range(n_in):
        moves[i].wait()
        chunk = a_ref[i * tall : i * tall + tall, :]
        sketches.append(jnp.dot(chunk, probe[...], preferred_element_type=F32))
    sketch = jnp.concatenate(sketches, axis=0).T.astype(BF16)
    for i in range(n_out):
        moves[n_in + i].wait()
        for rel, ref in ((0, keep_ref), (1, send_ref)):
            at = pl.multiple_of((2 * i + (core ^ rel)) * cols, cols)
            out = jnp.dot(sketch, b_ref[:, pl.ds(at, cols)], preferred_element_type=F32)
            ref[i] = out.T.reshape(ref.shape[1:])


def panel_call(me, a, b, parts, rows, blocks, pieces, name):
    pairs, width = b.shape
    rank = parts[0].shape[-1]
    out = sds((blocks, pieces, width // blocks // pieces // 2, rank), F32)
    hbm = pl.BlockSpec(memory_space=pltpu.HBM)
    n_in = 3 if pairs % 48 == 0 else 1
    return pl.pallas_call(
        functools.partial(panel_kernel, rows, len(parts), n_in, blocks),
        in_specs=[SMEM, hbm, hbm, hbm] + [VMEM] * (len(parts) - 1),
        out_specs=[VMEM, VMEM],
        out_shape=[out, out],
        scratch_shapes=[
            pltpu.VMEM(a.shape, BF16),
            pltpu.VMEM(b.shape, BF16),
            pltpu.VMEM((a.shape[1], rank), BF16),
            pltpu.SemaphoreType.DMA((n_in,)),
            pltpu.SemaphoreType.DMA((blocks,)),
            pltpu.SemaphoreType.DMA,
        ],
        compiler_params=pltpu.CompilerParams(vmem_limit_bytes=PANEL_LIMIT),
        cost_estimate=cost(2 * pairs * rank * (width + a.shape[1]), 2 * pairs * (width + a.shape[1])),
        name=name,
    )(me, a, b, *parts)


def sums_kernel(which, axis, shifts, n, me_ref, *refs):
    terms, (own_ref, *sends) = refs[:n], refs[n:]
    spot = me_ref[1] if which == "row" else me_ref[0] // 2

    def total(i):
        at = (slice(None),) * axis + (i,)
        value = terms[0][at]
        for term in terms[1:]:
            value = value + term[at].astype(F32)
        return value

    own_ref[...] = total(spot)
    for s, ref in zip(shifts, sends):
        ref[...] = total(spot ^ s).astype(BF16)


def sums_call(which, axis, shifts, me, terms, name):
    shape = list(terms[0].shape)
    size = terms[0].size
    del shape[axis]
    return pl.pallas_call(
        functools.partial(sums_kernel, which, axis, shifts, len(terms)),
        in_specs=[SMEM] + [VMEM] * len(terms),
        out_specs=[VMEM] * (1 + len(shifts)),
        out_shape=[sds(shape, F32)] + [sds(shape, BF16)] * len(shifts),
        compiler_params=params(),
        cost_estimate=cost(size, 4 * size * len(terms)),
        name=name,
    )(me, *terms)


def last_kernel(own_ref, *refs):
    *recv, out_ref = refs
    value = own_ref[...]
    for ref in recv:
        value = value + ref[...].astype(F32)
    out_ref[...] = value.astype(out_ref.dtype)


def last_call(own, recv, dtype, name):
    return pl.pallas_call(
        last_kernel,
        in_specs=[VMEM] * (1 + len(recv)),
        out_specs=VMEM,
        out_shape=sds(own.shape, dtype),
        compiler_params=params(),
        cost_estimate=cost(own.size, 12 * own.size),
        name=name,
    )(own, *recv)


def gram_kernel(which, order, me_ref, *refs):
    parts, (panel_ref, gram_ref) = refs[: len(order)], refs[len(order) :]
    for s, part in zip(order, parts):
        if which == "row":
            panel_ref[me_ref[1] ^ s] = part[...]
        else:
            spot = me_ref[0] ^ s
            panel_ref[spot % 2 * (len(order) // 2) + spot // 2] = part[...]
    panel = panel_ref[...].reshape(-1, gram_ref.shape[0])
    gram_ref[...] = lax.dot_general(
        panel, panel, (((0,), (0,)), ((), ())), preferred_element_type=F32
    )


def gram_call(which, order, me, parts, name):
    n = len(parts)
    rows, rank = parts[0].shape
    return pl.pallas_call(
        functools.partial(gram_kernel, which, order),
        in_specs=[SMEM] + [VMEM] * n,
        out_specs=[VMEM, VMEM],
        out_shape=[sds((n, rows, rank), BF16), sds((rank, rank), F32)],
        compiler_params=params(),
        cost_estimate=cost(2 * n * rows * rank * rank, 4 * n * rows * rank),
        name=name,
    )(me, *parts)


def tree_sum(values):
    while len(values) > 1:
        values = [x + y for x, y in zip(values[::2], values[1::2])]
    return values[0]


def text_gram_kernel(*refs):
    *parts, panel_ref, gram_ref = refs
    panel = tree_sum([part[...].astype(F32) for part in parts]).astype(BF16)
    panel_ref[0] = panel
    gram_ref[...] = lax.dot_general(
        panel, panel, (((0,), (0,)), ((), ())), preferred_element_type=F32
    )


def text_gram_call(parts):
    rows, rank = parts[0].shape
    return pl.pallas_call(
        text_gram_kernel,
        in_specs=[VMEM] * len(parts),
        out_specs=[VMEM, VMEM],
        out_shape=[sds((1, rows, rank), BF16), sds((rank, rank), F32)],
        compiler_params=params(),
        cost_estimate=cost(2 * rows * rank * rank, 4 * rows * rank),
        name="text_gram",
    )(*parts)


def inverse_factor(gram):
    n = gram.shape[0]
    lane = lax.broadcasted_iota(jnp.int32, (8, n), 1)
    sub = lax.broadcasted_iota(jnp.int32, (8, n), 0)
    rows = [gram[8 * i : 8 * i + 8, :] for i in range(n // 8)]
    for b in range(n // 8):
        cols = [
            [jnp.broadcast_to(rows[i][:, 8 * b + j : 8 * b + j + 1], (8, n)) for i in range(b, n // 8)]
            for j in range(8)
        ]
        scale = jnp.ones((8, n), F32)
        for j in range(8):
            k = 8 * b + j
            pivot = jnp.broadcast_to(cols[j][0][j : j + 1, :], (8, n))
            guess = pl.reciprocal(pivot, approx=True)
            inv = guess * (2.0 - pivot * guess)
            scale = jnp.where(sub == j, pivot, scale)
            pivot_row = jnp.where(lane == k, 1.0, jnp.broadcast_to(rows[b][j : j + 1, :], (8, n)))
            below = sub > j
            mult = [c * inv for c in cols[j]]
            mult[0] = jnp.where(below, mult[0], 0.0)
            for jj in range(j + 1, 8):
                entry = jnp.broadcast_to(cols[jj][0][j : j + 1, :], (8, n))
                cols[jj] = [c - m * entry for c, m in zip(cols[jj], mult)]
            for i in range(b, n // 8):
                here = lane == k
                if i == b:
                    here = jnp.logical_and(here, below)
                rows[i] = jnp.where(here, 0.0, rows[i]) - mult[i - b] * pivot_row
            yield None
        unit = jnp.where(lane == sub + 8 * b, 1.0, jnp.where(lane < sub + 8 * b, rows[b], 0.0))
        rows[b] = unit * lax.rsqrt(scale)
        yield None
    yield jnp.concatenate(rows, axis=0)


def finish_kernel(widths, n_image, ipanel, tpanel, *refs):
    *grams, iout, tout = refs

    def total(refs):
        value = refs[0][...]
        for even, odd in zip(refs[1::2], refs[2::2]):
            value = value + (even[...] + odd[...])
        return value

    inverses = None
    for inverses in zip(inverse_factor(total(grams[:n_image])), inverse_factor(total(grams[n_image:]))):
        pass
    dims = (((1,), (1,)), ((), ()))
    for inverse, width, panel_ref, out_ref in zip(inverses, widths, (ipanel, tpanel), (iout, tout)):
        inverse = inverse * math.sqrt(width)
        high = inverse.astype(BF16)
        low = (inverse - high.astype(F32)).astype(BF16)
        panel = panel_ref[...].reshape(out_ref.shape)
        out_ref[...] = lax.dot_general(panel, high, dims, preferred_element_type=F32) + lax.dot_general(
            panel, low, dims, preferred_element_type=F32
        )


def finish_call(widths, ipanel, igrams, tpanel, tgrams):
    rank = ipanel.shape[-1]
    outs = [sds((math.prod(p.shape[:-1]), rank), F32) for p in (ipanel, tpanel)]
    return pl.pallas_call(
        functools.partial(finish_kernel, widths, len(igrams)),
        in_specs=[VMEM] * (2 + len(igrams) + len(tgrams)),
        out_specs=[VMEM] * 2,
        out_shape=outs,
        compiler_params=params(),
        cost_estimate=cost(10**10, 6 * ipanel.size),
        name="finish",
    )(ipanel, tpanel, *igrams, *tgrams)


def per_device(n_row, n_col, image_feats, text_feats, probe_image, probe_text):
    groups = n_col // 2
    me = jnp.stack([lax.axis_index("col"), lax.axis_index("row")]).astype(jnp.int32)
    col_swap = lambda x, s: lax.ppermute(x, "col", [(i, i ^ s) for i in range(n_col)])
    row_swap = lambda x, s: lax.ppermute(x, "row", [(i, i ^ s) for i in range(n_row)])
    chips, depths = list(range(1, groups)), list(range(1, n_row))
    over_chips = lambda xs: [col_swap(x, 2 * s) for x, s in zip(xs, chips)]
    over_depth = lambda xs: [row_swap(x, t) for x, t in zip(xs, depths)]

    def over_plane(x, received=None):
        got = {0: x}
        for s, block in zip(chips, received or over_chips([x] * len(chips))):
            got[2 * s] = block
        for s in list(got):
            got[s ^ 1] = col_swap(got[s], 1)
        return got

    def split_swap(x, even, odd):
        pairs = []
        for r in range(n_row):
            for c in range(n_col):
                shift = odd if c % 2 else even
                if shift is not None:
                    pairs.append((r * n_col + c, (r ^ shift[0]) * n_col + (c ^ shift[1])))
        return lax.ppermute(x, ("row", "col"), pairs)

    def shared_sums(x, shifts):
        got = [split_swap(x, *pair) for pair in zip(shifts[::2], shifts[1::2] + [None])]
        return [term for block in got for term in (block, col_swap(block, 1))]

    fetched = [(t, t + 1, split_swap(probe_image, (t, 0), (t + 1, 0))) for t in depths[:-1:2]]
    half = probe_image.shape[0] // 2
    mine = lax.dynamic_slice_in_dim(probe_image, me[0] % 2 * half, half, 0)
    received = over_chips([probe_text] * len(chips))
    mine, received[-1] = lax.optimization_barrier((mine, received[-1]))
    text_parts = over_plane(probe_text, received)
    first, *blocks = lax.optimization_barrier((me, *[block for _, _, block in fetched]))
    last = depths[-1]
    mine = row_swap(mine, last)
    image_order = [(0, 0, None)]
    image_parts = [probe_image]

    columns = text_rows(list(text_parts), probe_text.shape[0])
    keep, send = panel_call(
        first, text_feats, image_feats, list(text_parts.values()), columns, n_row, groups, "image_panel"
    )
    send, mine, *blocks = lax.optimization_barrier((send, mine, *blocks))
    swapped = [col_swap(block, 1) for block in blocks]
    send, other, *swapped = lax.optimization_barrier((send, col_swap(mine, 1), *swapped))
    for (even, odd, _), block, twin in zip(fetched, blocks, swapped):
        image_order += [(even, odd, None), (odd, even, None)]
        image_parts += [block, twin]
    image_order += [(last, last, 0), (last, last, 1)]
    image_parts += [mine, other]
    own, *image_sends = sums_call("col", 1, chips, me, [keep, col_swap(send, 1)], "image_cores")
    own, *sends = sums_call("row", 0, depths, me, [own] + over_chips(image_sends), "image_plane")
    after_plane = sends[0]
    mine = last_call(own, over_depth(sends), BF16, "image_depth")
    parts = over_plane(mine)
    ipanel, gram = gram_call("col", list(parts), me, list(parts.values()), "image_gram")
    igrams = [gram] + shared_sums(gram, [(t, 0) for t in depths])

    rows = image_rows(image_order, probe_image.shape[0])
    keep, send = panel_call(me, image_feats, text_feats, image_parts, rows, groups, 1, "text_panel")
    swapped, _ = lax.optimization_barrier((col_swap(send, 1), image_sends[0]))
    own, *sends = sums_call("col", 0, chips, me, [keep, swapped], "text_cores")
    own, sends = own[0], [x[0] for x in sends]
    own, _ = lax.optimization_barrier((own, after_plane))
    mine = last_call(own, over_chips(sends), BF16, "text_plane")
    tpanel, gram = text_gram_call([mine] + over_depth([mine] * len(depths)))
    gram = last_call(gram, [col_swap(gram, 1)], F32, "text_gram_cores")
    tgrams = [gram] + shared_sums(gram, [(0, 2 * s) for s in chips])

    widths = (image_feats.shape[1], text_feats.shape[1])
    return finish_call(widths, ipanel, igrams, tpanel, tgrams)


def solution(mesh):
    in_specs = (P(("row", "col"), None), P(("row", "col"), None), P("row", None), P("col", None))
    out_specs = (P("row", None), P("col", None))
    body = functools.partial(per_device, mesh.shape["row"], mesh.shape["col"])
    return jax.shard_map(body, mesh=mesh, in_specs=in_specs, out_specs=out_specs, check_vma=False)
```

```python
import functools
import math

import jax
import jax.numpy as jnp
from jax import lax
from jax.experimental import pallas as pl
from jax.experimental.pallas import tpu as pltpu
from jax.sharding import PartitionSpec as P

F32 = jnp.float32
BF16 = jnp.bfloat16
VMEM = pl.BlockSpec(memory_space=pltpu.VMEM)
SMEM = pl.BlockSpec(memory_space=pltpu.SMEM)
LIMIT = 32 * 1024 * 1024
PANEL_LIMIT = 46 * 1024 * 1024


def sds(shape, dtype):
    return jax.ShapeDtypeStruct(shape, dtype)


def params(**kw):
    return pltpu.CompilerParams(vmem_limit_bytes=LIMIT, **kw)


def cost(flops, nbytes):
    return pl.CostEstimate(flops=int(flops), bytes_accessed=int(nbytes), transcendentals=0)


def text_rows(shifts, depth):
    return lambda me_ref: [pl.multiple_of((me_ref[0] ^ s) * depth, depth) for s in shifts]


def image_rows(order, depth):
    def rows(me_ref):
        core = me_ref[0] % 2
        out = []
        for even, odd, half in order:
            at = (me_ref[1] ^ (even + core * (odd - even))) * depth
            if half is not None:
                at = pl.multiple_of(at + (core ^ half) * (depth // 2), depth // 2)
            else:
                at = pl.multiple_of(at, depth)
            out.append(at)
        return out

    return rows


def load_kernel(hbm_ref, out_ref, sem):
    move = pltpu.make_async_copy(hbm_ref, out_ref, sem)
    move.start()
    move.wait()


def load_call(x):
    return pl.pallas_call(
        load_kernel,
        in_specs=[pl.BlockSpec(memory_space=pltpu.HBM)],
        out_specs=VMEM,
        out_shape=sds(x.shape, x.dtype),
        scratch_shapes=[pltpu.SemaphoreType.DMA],
        compiler_params=params(),
        cost_estimate=cost(1, 4 * x.size),
        name="load",
    )(x)


def panel_kernel(rows, n, n_in, n_out, me_ref, a_hbm, b_hbm, *refs):
    parts, (keep_ref, send_ref, a_ref, b_ref, probe, a_sem, b_sem) = refs[:n], refs[n:]
    core = me_ref[0] % 2
    tall = a_ref.shape[0] // n_in
    cols = b_ref.shape[1] // n_out // 2
    moves = []
    for i in range(n_in):
        span = pl.ds(i * tall, tall)
        moves.append(pltpu.make_async_copy(a_hbm.at[span], a_ref.at[span], a_sem.at[i]))
    for i in range(n_out):
        span = pl.ds(2 * i * cols, 2 * cols)
        moves.append(pltpu.make_async_copy(b_hbm.at[:, span], b_ref.at[:, span], b_sem.at[i]))
    places = rows(me_ref)
    for move in moves:
        move.start()
    for at, part in zip(places, parts):
        probe[pl.ds(at, part.shape[0]), :] = part[...]
    sketches = []
    for i in range(n_in):
        moves[i].wait()
        chunk = a_ref[i * tall : i * tall + tall, :]
        sketches.append(jnp.dot(chunk, probe[...], preferred_element_type=F32))
    sketch = jnp.concatenate(sketches, axis=0).T.astype(BF16)
    for i in range(n_out):
        moves[n_in + i].wait()
        for rel, ref in ((0, keep_ref), (1, send_ref)):
            at = pl.multiple_of((2 * i + (core ^ rel)) * cols, cols)
            out = jnp.dot(sketch, b_ref[:, pl.ds(at, cols)], preferred_element_type=F32)
            ref[i] = out.T.reshape(ref.shape[1:])


def panel_call(me, a, b, parts, rows, blocks, pieces, name):
    pairs, width = b.shape
    rank = parts[0].shape[-1]
    out = sds((blocks, pieces, width // blocks // pieces // 2, rank), F32)
    hbm = pl.BlockSpec(memory_space=pltpu.HBM)
    n_in = 3 if pairs % 48 == 0 else 1
    return pl.pallas_call(
        functools.partial(panel_kernel, rows, len(parts), n_in, blocks),
        in_specs=[SMEM, hbm, hbm] + [VMEM] * len(parts),
        out_specs=[VMEM, VMEM],
        out_shape=[out, out],
        scratch_shapes=[
            pltpu.VMEM(a.shape, BF16),
            pltpu.VMEM(b.shape, BF16),
            pltpu.VMEM((a.shape[1], rank), BF16),
            pltpu.SemaphoreType.DMA((n_in,)),
            pltpu.SemaphoreType.DMA((blocks,)),
        ],
        compiler_params=pltpu.CompilerParams(vmem_limit_bytes=PANEL_LIMIT),
        cost_estimate=cost(2 * pairs * rank * (width + a.shape[1]), 2 * pairs * (width + a.shape[1])),
        name=name,
    )(me, a, b, *parts)


def sums_kernel(which, axis, shifts, n, me_ref, *refs):
    terms, (own_ref, *sends) = refs[:n], refs[n:]
    spot = me_ref[1] if which == "row" else me_ref[0] // 2

    def total(i):
        at = (slice(None),) * axis + (i,)
        value = terms[0][at]
        for term in terms[1:]:
            value = value + term[at].astype(F32)
        return value

    own_ref[...] = total(spot)
    for s, ref in zip(shifts, sends):
        ref[...] = total(spot ^ s).astype(BF16)


def sums_call(which, axis, shifts, me, terms, name):
    shape = list(terms[0].shape)
    size = terms[0].size
    del shape[axis]
    return pl.pallas_call(
        functools.partial(sums_kernel, which, axis, shifts, len(terms)),
        in_specs=[SMEM] + [VMEM] * len(terms),
        out_specs=[VMEM] * (1 + len(shifts)),
        out_shape=[sds(shape, F32)] + [sds(shape, BF16)] * len(shifts),
        compiler_params=params(),
        cost_estimate=cost(size, 4 * size * len(terms)),
        name=name,
    )(me, *terms)


def last_kernel(own_ref, *refs):
    *recv, out_ref = refs
    value = own_ref[...]
    for ref in recv:
        value = value + ref[...].astype(F32)
    out_ref[...] = value.astype(out_ref.dtype)


def last_call(own, recv, dtype, name):
    return pl.pallas_call(
        last_kernel,
        in_specs=[VMEM] * (1 + len(recv)),
        out_specs=VMEM,
        out_shape=sds(own.shape, dtype),
        compiler_params=params(),
        cost_estimate=cost(own.size, 12 * own.size),
        name=name,
    )(own, *recv)


def pack(gram):
    half = gram.shape[0] // 2
    top, low = gram[:half], gram[half:]
    row = lax.broadcasted_iota(jnp.int32, top.shape, 0)
    lane = lax.broadcasted_iota(jnp.int32, top.shape, 1)
    body = jnp.where(row + half >= lane, low, pltpu.roll(top, half, 1))
    diagonal = jnp.sum(jnp.where(row == lane, top, 0.0), axis=0, keepdims=True)
    return jnp.concatenate([body, jnp.broadcast_to(diagonal, (8, gram.shape[1]))], axis=0)


def unpack(packed):
    half = packed.shape[0] - 8
    body, diagonal = packed[:half], packed[half : half + 1]
    row = lax.broadcasted_iota(jnp.int32, body.shape, 0)
    lane = lax.broadcasted_iota(jnp.int32, body.shape, 1)
    upper = jnp.where(jnp.logical_and(lane < half, row < lane), pltpu.roll(body, half, 1), 0.0)
    lower = jnp.where(row + half > lane, body, 0.0)
    strict = jnp.concatenate([upper, lower], axis=0)
    first = jnp.where(row == lane, jnp.broadcast_to(diagonal, body.shape), 0.0)
    last = jnp.where(row + half == lane, body, 0.0)
    return strict + strict.T + jnp.concatenate([first, last], axis=0)


def gram_kernel(which, order, me_ref, *refs):
    parts, (panel_ref, gram_ref) = refs[: len(order)], refs[len(order) :]
    for s, part in zip(order, parts):
        if which == "row":
            panel_ref[me_ref[1] ^ s] = part[...]
        else:
            spot = me_ref[0] ^ s
            panel_ref[spot % 2 * (len(order) // 2) + spot // 2] = part[...]
    panel = panel_ref[...].reshape(-1, gram_ref.shape[1])
    gram = lax.dot_general(panel, panel, (((0,), (0,)), ((), ())), preferred_element_type=F32)
    gram_ref[...] = pack(gram)


def gram_call(which, order, me, parts, name):
    n = len(parts)
    rows, rank = parts[0].shape
    return pl.pallas_call(
        functools.partial(gram_kernel, which, order),
        in_specs=[SMEM] + [VMEM] * n,
        out_specs=[VMEM, VMEM],
        out_shape=[sds((n, rows, rank), BF16), sds((rank // 2 + 8, rank), F32)],
        compiler_params=params(),
        cost_estimate=cost(2 * n * rows * rank * rank, 4 * n * rows * rank),
        name=name,
    )(me, *parts)


def tree_sum(values):
    while len(values) > 1:
        values = [x + y for x, y in zip(values[::2], values[1::2])]
    return values[0]


def text_gram_kernel(*refs):
    *parts, panel_ref, gram_ref = refs
    panel = tree_sum([part[...].astype(F32) for part in parts]).astype(BF16)
    panel_ref[0] = panel
    gram = lax.dot_general(panel, panel, (((0,), (0,)), ((), ())), preferred_element_type=F32)
    gram_ref[...] = pack(gram)


def text_gram_call(parts):
    rows, rank = parts[0].shape
    return pl.pallas_call(
        text_gram_kernel,
        in_specs=[VMEM] * len(parts),
        out_specs=[VMEM, VMEM],
        out_shape=[sds((1, rows, rank), BF16), sds((rank // 2 + 8, rank), F32)],
        compiler_params=params(),
        cost_estimate=cost(2 * rows * rank * rank, 4 * rows * rank),
        name="text_gram",
    )(*parts)


def inverse_factor(gram):
    n = gram.shape[0]
    lane = lax.broadcasted_iota(jnp.int32, (8, n), 1)
    sub = lax.broadcasted_iota(jnp.int32, (8, n), 0)
    rows = [gram[8 * i : 8 * i + 8, :] for i in range(n // 8)]
    for b in range(n // 8):
        cols = [
            [jnp.broadcast_to(rows[i][:, 8 * b + j : 8 * b + j + 1], (8, n)) for i in range(b, n // 8)]
            for j in range(8)
        ]
        scale = jnp.ones((8, n), F32)
        for j in range(8):
            k = 8 * b + j
            pivot = jnp.broadcast_to(cols[j][0][j : j + 1, :], (8, n))
            guess = pl.reciprocal(pivot, approx=True)
            inv = guess * (2.0 - pivot * guess)
            scale = jnp.where(sub == j, pivot, scale)
            pivot_row = jnp.where(lane == k, 1.0, jnp.broadcast_to(rows[b][j : j + 1, :], (8, n)))
            below = sub > j
            mult = [c * inv for c in cols[j]]
            mult[0] = jnp.where(below, mult[0], 0.0)
            for jj in range(j + 1, 8):
                entry = jnp.broadcast_to(cols[jj][0][j : j + 1, :], (8, n))
                cols[jj] = [c - m * entry for c, m in zip(cols[jj], mult)]
            for i in range(b, n // 8):
                here = lane == k
                if i == b:
                    here = jnp.logical_and(here, below)
                rows[i] = jnp.where(here, 0.0, rows[i]) - mult[i - b] * pivot_row
            yield None
        unit = jnp.where(lane == sub + 8 * b, 1.0, jnp.where(lane < sub + 8 * b, rows[b], 0.0))
        rows[b] = unit * lax.rsqrt(scale)
        yield None
    yield jnp.concatenate(rows, axis=0)


def finish_kernel(widths, n_image, ipanel, tpanel, *refs):
    *grams, iout, tout = refs

    def total(refs):
        value = refs[0][...]
        for ref in refs[1:]:
            value = value + ref[...]
        return unpack(value)

    inverses = None
    for inverses in zip(inverse_factor(total(grams[:n_image])), inverse_factor(total(grams[n_image:]))):
        pass
    dims = (((1,), (1,)), ((), ()))
    for inverse, width, panel_ref, out_ref in zip(inverses, widths, (ipanel, tpanel), (iout, tout)):
        inverse = inverse * math.sqrt(width)
        high = inverse.astype(BF16)
        low = (inverse - high.astype(F32)).astype(BF16)
        panel = panel_ref[...].reshape(out_ref.shape)
        out_ref[...] = lax.dot_general(panel, high, dims, preferred_element_type=F32) + lax.dot_general(
            panel, low, dims, preferred_element_type=F32
        )


def finish_call(widths, ipanel, igrams, tpanel, tgrams):
    rank = ipanel.shape[-1]
    outs = [sds((math.prod(p.shape[:-1]), rank), F32) for p in (ipanel, tpanel)]
    return pl.pallas_call(
        functools.partial(finish_kernel, widths, len(igrams)),
        in_specs=[VMEM] * (2 + len(igrams) + len(tgrams)),
        out_specs=[VMEM] * 2,
        out_shape=outs,
        compiler_params=params(),
        cost_estimate=cost(10**10, 6 * ipanel.size),
        name="finish",
    )(ipanel, tpanel, *igrams, *tgrams)


def per_device(n_row, n_col, image_feats, text_feats, probe_image, probe_text):
    groups = n_col // 2
    me = jnp.stack([lax.axis_index("col"), lax.axis_index("row")]).astype(jnp.int32)
    col_swap = lambda x, s: lax.ppermute(x, "col", [(i, i ^ s) for i in range(n_col)])
    row_swap = lambda x, s: lax.ppermute(x, "row", [(i, i ^ s) for i in range(n_row)])
    chips, depths = list(range(1, groups)), list(range(1, n_row))
    over_chips = lambda xs: [col_swap(x, 2 * s) for x, s in zip(xs, chips)]
    over_depth = lambda xs: [row_swap(x, t) for x, t in zip(xs, depths)]

    def over_plane(x, received=None):
        got = {0: x}
        for s, block in zip(chips, received or over_chips([x] * len(chips))):
            got[2 * s] = block
        for s in list(got):
            got[s ^ 1] = col_swap(got[s], 1)
        return got

    def split_swap(x, even, odd):
        pairs = []
        for r in range(n_row):
            for c in range(n_col):
                pairs.append((r * n_col + c, (r ^ (odd if c % 2 else even)) * n_col + c))
        return lax.ppermute(x, ("row", "col"), pairs)

    fetched = [(t, t + 1, split_swap(probe_image, t, t + 1)) for t in depths[:-1:2]]
    half = probe_image.shape[0] // 2
    mine = lax.dynamic_slice_in_dim(probe_image, me[0] % 2 * half, half, 0)
    received = over_chips([probe_text] * len(chips))
    own = load_call(probe_text)
    mine, own, received[-1] = lax.optimization_barrier((mine, own, received[-1]))
    text_parts = over_plane(probe_text, received)
    text_parts[0] = own
    first, *blocks = lax.optimization_barrier((me, *[block for _, _, block in fetched]))
    last = depths[-1]
    mine = row_swap(mine, last)
    image_order = [(0, 0, None)]
    image_parts = [probe_image]

    columns = text_rows(list(text_parts), probe_text.shape[0])
    keep, send = panel_call(
        first, text_feats, image_feats, list(text_parts.values()), columns, n_row, groups, "image_panel"
    )
    send, mine, *blocks = lax.optimization_barrier((send, mine, *blocks))
    swapped = [col_swap(block, 1) for block in blocks]
    send, other, *swapped = lax.optimization_barrier((send, col_swap(mine, 1), *swapped))
    for (even, odd, _), block, twin in zip(fetched, blocks, swapped):
        image_order += [(even, odd, None), (odd, even, None)]
        image_parts += [block, twin]
    image_order += [(last, last, 0), (last, last, 1)]
    image_parts += [mine, other]
    own, *image_sends = sums_call("col", 1, chips, me, [keep, col_swap(send, 1)], "image_cores")
    own, *sends = sums_call("row", 0, depths, me, [own] + over_chips(image_sends), "image_plane")
    received = over_depth(sends)
    after_depth = received
    mine = last_call(own, received, BF16, "image_depth")
    parts = over_plane(mine)
    ipanel, gram = gram_call("col", list(parts), me, list(parts.values()), "image_gram")
    igrams = [gram] + over_depth([gram] * len(depths))

    rows = image_rows(image_order, probe_image.shape[0])
    keep, send = panel_call(me, image_feats, text_feats, image_parts, rows, groups, 1, "text_panel")
    swapped, _ = lax.optimization_barrier((col_swap(send, 1), image_sends[0]))
    own, *sends = sums_call("col", 0, chips, me, [keep, swapped], "text_cores")
    own, sends = own[0], [x[0] for x in sends]
    own, *_ = lax.optimization_barrier((own, *after_depth))
    mine = last_call(own, over_chips(sends), BF16, "text_plane")
    tpanel, gram = text_gram_call([mine] + over_depth([mine] * len(depths)))
    gram = last_call(gram, [col_swap(gram, 1)], F32, "text_gram_cores")
    tgrams = [gram] + over_chips([gram] * len(chips))

    widths = (image_feats.shape[1], text_feats.shape[1])
    return finish_call(widths, ipanel, igrams, tpanel, tgrams)


def solution(mesh):
    in_specs = (P(("row", "col"), None), P(("row", "col"), None), P("row", None), P("col", None))
    out_specs = (P("row", None), P("col", None))
    body = functools.partial(per_device, mesh.shape["row"], mesh.shape["col"])
    return jax.shard_map(body, mesh=mesh, in_specs=in_specs, out_specs=out_specs, check_vma=False)
```

```python
import functools
import math

import jax
import jax.numpy as jnp
from jax import lax
from jax.experimental import pallas as pl
from jax.experimental.pallas import tpu as pltpu
from jax.sharding import PartitionSpec as P

F32 = jnp.float32
BF16 = jnp.bfloat16
VMEM = pl.BlockSpec(memory_space=pltpu.VMEM)
SMEM = pl.BlockSpec(memory_space=pltpu.SMEM)
LIMIT = 32 * 1024 * 1024
PANEL_LIMIT = 46 * 1024 * 1024


def sds(shape, dtype):
    return jax.ShapeDtypeStruct(shape, dtype)


def params(**kw):
    return pltpu.CompilerParams(vmem_limit_bytes=LIMIT, **kw)


def cost(flops, nbytes):
    return pl.CostEstimate(flops=int(flops), bytes_accessed=int(nbytes), transcendentals=0)


def text_rows(shifts, depth):
    return lambda me_ref: [pl.multiple_of((me_ref[0] ^ s) * depth, depth) for s in shifts]


def image_rows(order, depth):
    def rows(me_ref):
        core = me_ref[0] % 2
        out = []
        for even, odd, half in order:
            at = (me_ref[1] ^ (even + core * (odd - even))) * depth
            if half is not None:
                at = pl.multiple_of(at + (core ^ half) * (depth // 2), depth // 2)
            else:
                at = pl.multiple_of(at, depth)
            out.append(at)
        return out

    return rows


def load_kernel(hbm_ref, out_ref, sem):
    move = pltpu.make_async_copy(hbm_ref, out_ref, sem)
    move.start()
    move.wait()


def load_call(x):
    return pl.pallas_call(
        load_kernel,
        in_specs=[pl.BlockSpec(memory_space=pltpu.HBM)],
        out_specs=VMEM,
        out_shape=sds(x.shape, x.dtype),
        scratch_shapes=[pltpu.SemaphoreType.DMA],
        compiler_params=params(),
        cost_estimate=cost(1, 4 * x.size),
        name="load",
    )(x)


def panel_kernel(rows, n, n_in, n_out, me_ref, a_hbm, b_hbm, *refs):
    parts, (keep_ref, send_ref, a_ref, b_ref, probe, a_sem, b_sem) = refs[:n], refs[n:]
    core = me_ref[0] % 2
    tall = a_ref.shape[0] // n_in
    cols = b_ref.shape[1] // n_out // 2
    moves = []
    for i in range(n_in):
        span = pl.ds(i * tall, tall)
        moves.append(pltpu.make_async_copy(a_hbm.at[span], a_ref.at[span], a_sem.at[i]))
    for i in range(n_out):
        span = pl.ds(2 * i * cols, 2 * cols)
        moves.append(pltpu.make_async_copy(b_hbm.at[:, span], b_ref.at[:, span], b_sem.at[i]))
    places = rows(me_ref)
    for move in moves:
        move.start()
    for at, part in zip(places, parts):
        probe[pl.ds(at, part.shape[0]), :] = part[...]
    sketches = []
    for i in range(n_in):
        moves[i].wait()
        chunk = a_ref[i * tall : i * tall + tall, :]
        sketches.append(jnp.dot(chunk, probe[...], preferred_element_type=F32))
    sketch = jnp.concatenate(sketches, axis=0).T.astype(BF16)
    for i in range(n_out):
        moves[n_in + i].wait()
        for rel, ref in ((0, keep_ref), (1, send_ref)):
            at = pl.multiple_of((2 * i + (core ^ rel)) * cols, cols)
            out = jnp.dot(sketch, b_ref[:, pl.ds(at, cols)], preferred_element_type=F32)
            ref[i] = out.T.reshape(ref.shape[1:])


def panel_call(me, a, b, parts, rows, blocks, pieces, name):
    pairs, width = b.shape
    rank = parts[0].shape[-1]
    out = sds((blocks, pieces, width // blocks // pieces // 2, rank), F32)
    hbm = pl.BlockSpec(memory_space=pltpu.HBM)
    n_in = 3 if pairs % 48 == 0 else 1
    return pl.pallas_call(
        functools.partial(panel_kernel, rows, len(parts), n_in, blocks),
        in_specs=[SMEM, hbm, hbm] + [VMEM] * len(parts),
        out_specs=[VMEM, VMEM],
        out_shape=[out, out],
        scratch_shapes=[
            pltpu.VMEM(a.shape, BF16),
            pltpu.VMEM(b.shape, BF16),
            pltpu.VMEM((a.shape[1], rank), BF16),
            pltpu.SemaphoreType.DMA((n_in,)),
            pltpu.SemaphoreType.DMA((blocks,)),
        ],
        compiler_params=pltpu.CompilerParams(vmem_limit_bytes=PANEL_LIMIT),
        cost_estimate=cost(1, 1),
        name=name,
    )(me, a, b, *parts)


def sums_kernel(which, axis, shifts, n, me_ref, *refs):
    terms, (own_ref, *sends) = refs[:n], refs[n:]
    spot = me_ref[1] if which == "row" else me_ref[0] // 2

    def total(i):
        at = (slice(None),) * axis + (i,)
        value = terms[0][at]
        for term in terms[1:]:
            value = value + term[at].astype(F32)
        return value

    own_ref[...] = total(spot)
    for s, ref in zip(shifts, sends):
        ref[...] = total(spot ^ s).astype(BF16)


def sums_call(which, axis, shifts, me, terms, name):
    shape = list(terms[0].shape)
    size = terms[0].size
    del shape[axis]
    return pl.pallas_call(
        functools.partial(sums_kernel, which, axis, shifts, len(terms)),
        in_specs=[SMEM] + [VMEM] * len(terms),
        out_specs=[VMEM] * (1 + len(shifts)),
        out_shape=[sds(shape, F32)] + [sds(shape, BF16)] * len(shifts),
        compiler_params=params(),
        cost_estimate=cost(size, 4 * size * len(terms)),
        name=name,
    )(me, *terms)


def last_kernel(own_ref, *refs):
    *recv, out_ref = refs
    value = own_ref[...]
    for ref in recv:
        value = value + ref[...].astype(F32)
    out_ref[...] = value.astype(out_ref.dtype)


def last_call(own, recv, dtype, name):
    return pl.pallas_call(
        last_kernel,
        in_specs=[VMEM] * (1 + len(recv)),
        out_specs=VMEM,
        out_shape=sds(own.shape, dtype),
        compiler_params=params(),
        cost_estimate=cost(own.size, 12 * own.size),
        name=name,
    )(own, *recv)


def pack(gram):
    half = gram.shape[0] // 2
    top, low = gram[:half], gram[half:]
    row = lax.broadcasted_iota(jnp.int32, top.shape, 0)
    lane = lax.broadcasted_iota(jnp.int32, top.shape, 1)
    body = jnp.where(row + half >= lane, low, pltpu.roll(top, half, 1))
    diagonal = jnp.sum(jnp.where(row == lane, top, 0.0), axis=0, keepdims=True)
    return jnp.concatenate([body, jnp.broadcast_to(diagonal, (8, gram.shape[1]))], axis=0)


def unpack(packed):
    half = packed.shape[0] - 8
    body, diagonal = packed[:half], packed[half : half + 1]
    row = lax.broadcasted_iota(jnp.int32, body.shape, 0)
    lane = lax.broadcasted_iota(jnp.int32, body.shape, 1)
    upper = jnp.where(jnp.logical_and(lane < half, row < lane), pltpu.roll(body, half, 1), 0.0)
    lower = jnp.where(row + half > lane, body, 0.0)
    strict = jnp.concatenate([upper, lower], axis=0)
    first = jnp.where(row == lane, jnp.broadcast_to(diagonal, body.shape), 0.0)
    last = jnp.where(row + half == lane, body, 0.0)
    return strict + strict.T + jnp.concatenate([first, last], axis=0)


def gram_kernel(which, order, me_ref, *refs):
    parts, (panel_ref, gram_ref) = refs[: len(order)], refs[len(order) :]
    for s, part in zip(order, parts):
        if which == "row":
            panel_ref[me_ref[1] ^ s] = part[...]
        else:
            spot = me_ref[0] ^ s
            panel_ref[spot % 2 * (len(order) // 2) + spot // 2] = part[...]
    panel = panel_ref[...].reshape(-1, gram_ref.shape[1])
    gram = lax.dot_general(panel, panel, (((0,), (0,)), ((), ())), preferred_element_type=F32)
    gram_ref[...] = pack(gram)


def gram_call(which, order, me, parts, name):
    n = len(parts)
    rows, rank = parts[0].shape
    return pl.pallas_call(
        functools.partial(gram_kernel, which, order),
        in_specs=[SMEM] + [VMEM] * n,
        out_specs=[VMEM, VMEM],
        out_shape=[sds((n, rows, rank), BF16), sds((rank // 2 + 8, rank), F32)],
        compiler_params=params(),
        cost_estimate=cost(2 * n * rows * rank * rank, 4 * n * rows * rank),
        name=name,
    )(me, *parts)


def tree_sum(values):
    while len(values) > 1:
        values = [x + y for x, y in zip(values[::2], values[1::2])]
    return values[0]


def text_gram_kernel(*refs):
    *parts, panel_ref, gram_ref = refs
    panel = tree_sum([part[...].astype(F32) for part in parts]).astype(BF16)
    panel_ref[0] = panel
    gram = lax.dot_general(panel, panel, (((0,), (0,)), ((), ())), preferred_element_type=F32)
    gram_ref[...] = pack(gram)


def text_gram_call(parts):
    rows, rank = parts[0].shape
    return pl.pallas_call(
        text_gram_kernel,
        in_specs=[VMEM] * len(parts),
        out_specs=[VMEM, VMEM],
        out_shape=[sds((1, rows, rank), BF16), sds((rank // 2 + 8, rank), F32)],
        compiler_params=params(),
        cost_estimate=cost(2 * rows * rank * rank, 4 * rows * rank),
        name="text_gram",
    )(*parts)


def inverse_factor(gram):
    n = gram.shape[0]
    lane = lax.broadcasted_iota(jnp.int32, (8, n), 1)
    sub = lax.broadcasted_iota(jnp.int32, (8, n), 0)
    rows = [gram[8 * i : 8 * i + 8, :] for i in range(n // 8)]
    for b in range(n // 8):
        cols = [
            [jnp.broadcast_to(rows[i][:, 8 * b + j : 8 * b + j + 1], (8, n)) for i in range(b, n // 8)]
            for j in range(8)
        ]
        scale = jnp.ones((8, n), F32)
        for j in range(8):
            k = 8 * b + j
            pivot = jnp.broadcast_to(cols[j][0][j : j + 1, :], (8, n))
            guess = pl.reciprocal(pivot, approx=True)
            inv = guess * (2.0 - pivot * guess)
            scale = jnp.where(sub == j, pivot, scale)
            pivot_row = jnp.where(lane == k, 1.0, jnp.broadcast_to(rows[b][j : j + 1, :], (8, n)))
            below = sub > j
            mult = [c * inv for c in cols[j]]
            mult[0] = jnp.where(below, mult[0], 0.0)
            for jj in range(j + 1, 8):
                entry = jnp.broadcast_to(cols[jj][0][j : j + 1, :], (8, n))
                cols[jj] = [c - m * entry for c, m in zip(cols[jj], mult)]
            for i in range(b, n // 8):
                here = lane == k
                if i == b:
                    here = jnp.logical_and(here, below)
                rows[i] = jnp.where(here, 0.0, rows[i]) - mult[i - b] * pivot_row
            yield None
        unit = jnp.where(lane == sub + 8 * b, 1.0, jnp.where(lane < sub + 8 * b, rows[b], 0.0))
        rows[b] = unit * lax.rsqrt(scale)
        yield None
    yield jnp.concatenate(rows, axis=0)


def finish_kernel(widths, n_image, ipanel, tpanel, *refs):
    *grams, iout, tout = refs

    def total(refs):
        value = refs[0][...]
        for ref in refs[1:]:
            value = value + ref[...]
        return unpack(value)

    inverses = None
    for inverses in zip(inverse_factor(total(grams[:n_image])), inverse_factor(total(grams[n_image:]))):
        pass
    dims = (((1,), (1,)), ((), ()))
    for inverse, width, panel_ref, out_ref in zip(inverses, widths, (ipanel, tpanel), (iout, tout)):
        inverse = inverse * math.sqrt(width)
        high = inverse.astype(BF16)
        low = (inverse - high.astype(F32)).astype(BF16)
        panel = panel_ref[...].reshape(out_ref.shape)
        out_ref[...] = lax.dot_general(panel, high, dims, preferred_element_type=F32) + lax.dot_general(
            panel, low, dims, preferred_element_type=F32
        )


def finish_call(widths, ipanel, igrams, tpanel, tgrams):
    rank = ipanel.shape[-1]
    outs = [sds((math.prod(p.shape[:-1]), rank), F32) for p in (ipanel, tpanel)]
    return pl.pallas_call(
        functools.partial(finish_kernel, widths, len(igrams)),
        in_specs=[VMEM] * (2 + len(igrams) + len(tgrams)),
        out_specs=[VMEM] * 2,
        out_shape=outs,
        compiler_params=params(),
        cost_estimate=cost(10**10, 6 * ipanel.size),
        name="finish",
    )(ipanel, tpanel, *igrams, *tgrams)


def per_device(n_row, n_col, image_feats, text_feats, probe_image, probe_text):
    groups = n_col // 2
    me = jnp.stack([lax.axis_index("col"), lax.axis_index("row")]).astype(jnp.int32)
    col_swap = lambda x, s: lax.ppermute(x, "col", [(i, i ^ s) for i in range(n_col)])
    row_swap = lambda x, s: lax.ppermute(x, "row", [(i, i ^ s) for i in range(n_row)])
    chips, depths = list(range(1, groups)), list(range(1, n_row))
    over_chips = lambda xs: [col_swap(x, 2 * s) for x, s in zip(xs, chips)]
    over_depth = lambda xs: [row_swap(x, t) for x, t in zip(xs, depths)]

    def over_plane(x, received=None):
        got = {0: x}
        for s, block in zip(chips, received or over_chips([x] * len(chips))):
            got[2 * s] = block
        for s in list(got):
            got[s ^ 1] = col_swap(got[s], 1)
        return got

    def split_swap(x, even, odd):
        pairs = []
        for r in range(n_row):
            for c in range(n_col):
                pairs.append((r * n_col + c, (r ^ (odd if c % 2 else even)) * n_col + c))
        return lax.ppermute(x, ("row", "col"), pairs)

    fetched = [(t, t + 1, split_swap(probe_image, t, t + 1)) for t in depths[:-1:2]]
    half = probe_image.shape[0] // 2
    mine = lax.dynamic_slice_in_dim(probe_image, me[0] % 2 * half, half, 0)
    received = over_chips([probe_text] * len(chips))
    own = load_call(probe_text)
    mine, own, received[-1] = lax.optimization_barrier((mine, own, received[-1]))
    text_parts = over_plane(probe_text, received)
    text_parts[0] = own
    blocks = [block for _, _, block in fetched]
    last = depths[-1]
    mine = row_swap(mine, last)
    image_order = [(0, 0, None)]
    image_parts = [probe_image]

    columns = text_rows(list(text_parts), probe_text.shape[0])
    keep, send = panel_call(
        me, text_feats, image_feats, list(text_parts.values()), columns, n_row, groups, "image_panel"
    )
    send, mine, *blocks = lax.optimization_barrier((send, mine, *blocks))
    swapped = [col_swap(block, 1) for block in blocks]
    send, other, *swapped = lax.optimization_barrier((send, col_swap(mine, 1), *swapped))
    for (even, odd, _), block, twin in zip(fetched, blocks, swapped):
        image_order += [(even, odd, None), (odd, even, None)]
        image_parts += [block, twin]
    image_order += [(last, last, 0), (last, last, 1)]
    image_parts += [mine, other]
    own, *image_sends = sums_call("col", 1, chips, me, [keep, col_swap(send, 1)], "image_cores")
    own, *sends = sums_call("row", 0, depths, me, [own] + over_chips(image_sends), "image_plane")
    after_plane = sends[0]
    received = over_depth(sends)
    mine = last_call(own, received, BF16, "image_depth")
    parts = over_plane(mine)
    ipanel, gram = gram_call("col", list(parts), me, list(parts.values()), "image_gram")
    igrams = [gram] + over_depth([gram] * len(depths))

    rows = image_rows(image_order, probe_image.shape[0])
    keep, send = panel_call(me, image_feats, text_feats, image_parts, rows, groups, 1, "text_panel")
    swapped, _ = lax.optimization_barrier((col_swap(send, 1), image_sends[0]))
    own, *sends = sums_call("col", 0, chips, me, [keep, swapped], "text_cores")
    own, sends = own[0], [x[0] for x in sends]
    own, _ = lax.optimization_barrier((own, after_plane))
    mine = last_call(own, over_chips(sends), BF16, "text_plane")
    tpanel, gram = text_gram_call([mine] + over_depth([mine] * len(depths)))
    gram = last_call(gram, [col_swap(gram, 1)], F32, "text_gram_cores")
    tgrams = [gram] + over_chips([gram] * len(chips))

    widths = (image_feats.shape[1], text_feats.shape[1])
    return finish_call(widths, ipanel, igrams, tpanel, tgrams)


def solution(mesh):
    in_specs = (P(("row", "col"), None), P(("row", "col"), None), P("row", None), P("col", None))
    out_specs = (P("row", None), P("col", None))
    body = functools.partial(per_device, mesh.shape["row"], mesh.shape["col"])
    return jax.shard_map(body, mesh=mesh, in_specs=in_specs, out_specs=out_specs, check_vma=False)
```

```python
import functools
import math

import jax
import jax.numpy as jnp
from jax import lax
from jax.experimental import pallas as pl
from jax.experimental.pallas import tpu as pltpu
from jax.sharding import PartitionSpec as P

F32 = jnp.float32
BF16 = jnp.bfloat16
VMEM = pl.BlockSpec(memory_space=pltpu.VMEM)
SMEM = pl.BlockSpec(memory_space=pltpu.SMEM)
LIMIT = 32 * 1024 * 1024
PANEL_LIMIT = 46 * 1024 * 1024


def sds(shape, dtype):
    return jax.ShapeDtypeStruct(shape, dtype)


def params(**kw):
    return pltpu.CompilerParams(vmem_limit_bytes=LIMIT, **kw)


def cost(flops, nbytes):
    return pl.CostEstimate(flops=int(flops), bytes_accessed=int(nbytes), transcendentals=0)


def text_rows(shifts, depth):
    return lambda me_ref: [pl.multiple_of((me_ref[0] ^ s) * depth, depth) for s in shifts]


def image_rows(order, depth):
    def rows(me_ref):
        core = me_ref[0] % 2
        out = []
        for even, odd, half in order:
            at = (me_ref[1] ^ (even + core * (odd - even))) * depth
            if half is not None:
                at = pl.multiple_of(at + (core ^ half) * (depth // 2), depth // 2)
            else:
                at = pl.multiple_of(at, depth)
            out.append(at)
        return out

    return rows


def load_kernel(hbm_ref, out_ref, sem):
    move = pltpu.make_async_copy(hbm_ref, out_ref, sem)
    move.start()
    move.wait()


def load_call(x):
    return pl.pallas_call(
        load_kernel,
        in_specs=[pl.BlockSpec(memory_space=pltpu.HBM)],
        out_specs=VMEM,
        out_shape=sds(x.shape, x.dtype),
        scratch_shapes=[pltpu.SemaphoreType.DMA],
        compiler_params=params(),
        cost_estimate=cost(1, 4 * x.size),
        name="load",
    )(x)


def panel_kernel(rows, n, n_in, n_out, me_ref, a_hbm, b_hbm, *refs):
    parts, (keep_ref, send_ref, a_ref, b_ref, probe, a_sem, b_sem) = refs[:n], refs[n:]
    core = me_ref[0] % 2
    tall = a_ref.shape[0] // n_in
    cols = b_ref.shape[1] // n_out // 2
    moves = []
    for i in range(n_in):
        span = pl.ds(i * tall, tall)
        moves.append(pltpu.make_async_copy(a_hbm.at[span], a_ref.at[span], a_sem.at[i]))
    for i in range(n_out):
        span = pl.ds(2 * i * cols, 2 * cols)
        moves.append(pltpu.make_async_copy(b_hbm.at[:, span], b_ref.at[:, span], b_sem.at[i]))
    places = rows(me_ref)
    for move in moves:
        move.start()
    for at, part in zip(places, parts):
        probe[pl.ds(at, part.shape[0]), :] = part[...]
    sketches = []
    for i in range(n_in):
        moves[i].wait()
        chunk = a_ref[i * tall : i * tall + tall, :]
        sketches.append(jnp.dot(chunk, probe[...], preferred_element_type=F32))
    sketch = jnp.concatenate(sketches, axis=0).T.astype(BF16)
    for i in range(n_out):
        moves[n_in + i].wait()
        for rel, ref in ((0, keep_ref), (1, send_ref)):
            at = pl.multiple_of((2 * i + (core ^ rel)) * cols, cols)
            out = jnp.dot(sketch, b_ref[:, pl.ds(at, cols)], preferred_element_type=F32)
            ref[i] = out.T.reshape(ref.shape[1:])


def panel_call(me, a, b, parts, rows, blocks, pieces, name):
    pairs, width = b.shape
    rank = parts[0].shape[-1]
    out = sds((blocks, pieces, width // blocks // pieces // 2, rank), F32)
    hbm = pl.BlockSpec(memory_space=pltpu.HBM)
    n_in = 3 if pairs % 48 == 0 else 1
    return pl.pallas_call(
        functools.partial(panel_kernel, rows, len(parts), n_in, blocks),
        in_specs=[SMEM, hbm, hbm] + [VMEM] * len(parts),
        out_specs=[VMEM, VMEM],
        out_shape=[out, out],
        scratch_shapes=[
            pltpu.VMEM(a.shape, BF16),
            pltpu.VMEM(b.shape, BF16),
            pltpu.VMEM((a.shape[1], rank), BF16),
            pltpu.SemaphoreType.DMA((n_in,)),
            pltpu.SemaphoreType.DMA((blocks,)),
        ],
        compiler_params=pltpu.CompilerParams(vmem_limit_bytes=PANEL_LIMIT),
        cost_estimate=cost(1, 1),
        name=name,
    )(me, a, b, *parts)


def sums_kernel(which, axis, shifts, n, me_ref, *refs):
    terms, (own_ref, *sends) = refs[:n], refs[n:]
    spot = me_ref[1] if which == "row" else me_ref[0] // 2

    def total(i):
        at = (slice(None),) * axis + (i,)
        value = terms[0][at]
        for term in terms[1:]:
            value = value + term[at].astype(F32)
        return value

    own_ref[...] = total(spot)
    for s, ref in zip(shifts, sends):
        ref[...] = total(spot ^ s).astype(BF16)


def sums_call(which, axis, shifts, me, terms, name):
    shape = list(terms[0].shape)
    size = terms[0].size
    del shape[axis]
    return pl.pallas_call(
        functools.partial(sums_kernel, which, axis, shifts, len(terms)),
        in_specs=[SMEM] + [VMEM] * len(terms),
        out_specs=[VMEM] * (1 + len(shifts)),
        out_shape=[sds(shape, F32)] + [sds(shape, BF16)] * len(shifts),
        compiler_params=params(),
        cost_estimate=cost(size, 4 * size * len(terms)),
        name=name,
    )(me, *terms)


def last_kernel(own_ref, *refs):
    *recv, out_ref = refs
    value = own_ref[...]
    for ref in recv:
        value = value + ref[...].astype(F32)
    out_ref[...] = value.astype(out_ref.dtype)


def last_call(own, recv, dtype, name):
    return pl.pallas_call(
        last_kernel,
        in_specs=[VMEM] * (1 + len(recv)),
        out_specs=VMEM,
        out_shape=sds(own.shape, dtype),
        compiler_params=params(),
        cost_estimate=cost(own.size, 12 * own.size),
        name=name,
    )(own, *recv)


def pack(gram):
    half = gram.shape[0] // 2
    top, low = gram[:half], gram[half:]
    row = lax.broadcasted_iota(jnp.int32, top.shape, 0)
    lane = lax.broadcasted_iota(jnp.int32, top.shape, 1)
    body = jnp.where(row + half >= lane, low, pltpu.roll(top, half, 1))
    diagonal = jnp.sum(jnp.where(row == lane, top, 0.0), axis=0, keepdims=True)
    return jnp.concatenate([body, jnp.broadcast_to(diagonal, (8, gram.shape[1]))], axis=0)


def unpack(packed):
    half = packed.shape[0] - 8
    body, diagonal = packed[:half], packed[half : half + 1]
    row = lax.broadcasted_iota(jnp.int32, body.shape, 0)
    lane = lax.broadcasted_iota(jnp.int32, body.shape, 1)
    upper = jnp.where(jnp.logical_and(lane < half, row < lane), pltpu.roll(body, half, 1), 0.0)
    lower = jnp.where(row + half > lane, body, 0.0)
    strict = jnp.concatenate([upper, lower], axis=0)
    first = jnp.where(row == lane, jnp.broadcast_to(diagonal, body.shape), 0.0)
    last = jnp.where(row + half == lane, body, 0.0)
    return strict + strict.T + jnp.concatenate([first, last], axis=0)


def gram_kernel(which, order, me_ref, *refs):
    parts, (panel_ref, gram_ref) = refs[: len(order)], refs[len(order) :]
    for s, part in zip(order, parts):
        if which == "row":
            panel_ref[me_ref[1] ^ s] = part[...]
        else:
            spot = me_ref[0] ^ s
            panel_ref[spot % 2 * (len(order) // 2) + spot // 2] = part[...]
    panel = panel_ref[...].reshape(-1, gram_ref.shape[1])
    gram = lax.dot_general(panel, panel, (((0,), (0,)), ((), ())), preferred_element_type=F32)
    gram_ref[...] = pack(gram)


def gram_call(which, order, me, parts, name):
    n = len(parts)
    rows, rank = parts[0].shape
    return pl.pallas_call(
        functools.partial(gram_kernel, which, order),
        in_specs=[SMEM] + [VMEM] * n,
        out_specs=[VMEM, VMEM],
        out_shape=[sds((n, rows, rank), BF16), sds((rank // 2 + 8, rank), F32)],
        compiler_params=params(),
        cost_estimate=cost(2 * n * rows * rank * rank, 4 * n * rows * rank),
        name=name,
    )(me, *parts)


def tree_sum(values):
    while len(values) > 1:
        values = [x + y for x, y in zip(values[::2], values[1::2])]
    return values[0]


def text_gram_kernel(*refs):
    *parts, panel_ref, gram_ref = refs
    panel = tree_sum([part[...].astype(F32) for part in parts]).astype(BF16)
    panel_ref[0] = panel
    gram = lax.dot_general(panel, panel, (((0,), (0,)), ((), ())), preferred_element_type=F32)
    gram_ref[...] = pack(gram)


def text_gram_call(parts):
    rows, rank = parts[0].shape
    return pl.pallas_call(
        text_gram_kernel,
        in_specs=[VMEM] * len(parts),
        out_specs=[VMEM, VMEM],
        out_shape=[sds((1, rows, rank), BF16), sds((rank // 2 + 8, rank), F32)],
        compiler_params=params(),
        cost_estimate=cost(2 * rows * rank * rank, 4 * rows * rank),
        name="text_gram",
    )(*parts)


def inverse_factor(gram):
    n = gram.shape[0]
    lane = lax.broadcasted_iota(jnp.int32, (8, n), 1)
    sub = lax.broadcasted_iota(jnp.int32, (8, n), 0)
    rows = [gram[8 * i : 8 * i + 8, :] for i in range(n // 8)]
    for b in range(n // 8):
        cols = [
            [jnp.broadcast_to(rows[i][:, 8 * b + j : 8 * b + j + 1], (8, n)) for i in range(b, n // 8)]
            for j in range(8)
        ]
        scale = jnp.ones((8, n), F32)
        for j in range(8):
            k = 8 * b + j
            pivot = jnp.broadcast_to(cols[j][0][j : j + 1, :], (8, n))
            guess = pl.reciprocal(pivot, approx=True)
            inv = guess * (2.0 - pivot * guess)
            scale = jnp.where(sub == j, pivot, scale)
            pivot_row = jnp.where(lane == k, 1.0, jnp.broadcast_to(rows[b][j : j + 1, :], (8, n)))
            below = sub > j
            mult = [c * inv for c in cols[j]]
            mult[0] = jnp.where(below, mult[0], 0.0)
            for jj in range(j + 1, 8):
                entry = jnp.broadcast_to(cols[jj][0][j : j + 1, :], (8, n))
                cols[jj] = [c - m * entry for c, m in zip(cols[jj], mult)]
            for i in range(b, n // 8):
                here = lane == k
                if i == b:
                    here = jnp.logical_and(here, below)
                rows[i] = jnp.where(here, 0.0, rows[i]) - mult[i - b] * pivot_row
            yield None
        unit = jnp.where(lane == sub + 8 * b, 1.0, jnp.where(lane < sub + 8 * b, rows[b], 0.0))
        rows[b] = unit * lax.rsqrt(scale)
        yield None
    yield jnp.concatenate(rows, axis=0)


def finish_kernel(width, panel_ref, *refs):
    *grams, out_ref = refs
    total = grams[0][...]
    for ref in grams[1:]:
        total = total + ref[...]
    inverse = None
    for inverse in inverse_factor(unpack(total)):
        pass
    inverse = inverse * math.sqrt(width)
    high = inverse.astype(BF16)
    low = (inverse - high.astype(F32)).astype(BF16)
    dims = (((1,), (1,)), ((), ()))
    panel = panel_ref[...].reshape(out_ref.shape)
    out_ref[...] = lax.dot_general(panel, high, dims, preferred_element_type=F32) + lax.dot_general(
        panel, low, dims, preferred_element_type=F32
    )


def finish_call(width, panel, grams, name):
    n, rows, rank = panel.shape
    return pl.pallas_call(
        functools.partial(finish_kernel, width),
        in_specs=[VMEM] * (1 + len(grams)),
        out_specs=VMEM,
        out_shape=sds((n * rows, rank), F32),
        compiler_params=params(),
        cost_estimate=cost(5 * 10**9, 6 * n * rows * rank),
        name=name,
    )(panel, *grams)


def per_device(n_row, n_col, image_feats, text_feats, probe_image, probe_text):
    groups = n_col // 2
    me = jnp.stack([lax.axis_index("col"), lax.axis_index("row")]).astype(jnp.int32)
    col_swap = lambda x, s: lax.ppermute(x, "col", [(i, i ^ s) for i in range(n_col)])
    row_swap = lambda x, s: lax.ppermute(x, "row", [(i, i ^ s) for i in range(n_row)])
    chips, depths = list(range(1, groups)), list(range(1, n_row))
    over_chips = lambda xs: [col_swap(x, 2 * s) for x, s in zip(xs, chips)]
    over_depth = lambda xs: [row_swap(x, t) for x, t in zip(xs, depths)]

    def over_plane(x, received=None):
        got = {0: x}
        for s, block in zip(chips, received or over_chips([x] * len(chips))):
            got[2 * s] = block
        for s in list(got):
            got[s ^ 1] = col_swap(got[s], 1)
        return got

    def split_swap(x, even, odd):
        pairs = []
        for r in range(n_row):
            for c in range(n_col):
                pairs.append((r * n_col + c, (r ^ (odd if c % 2 else even)) * n_col + c))
        return lax.ppermute(x, ("row", "col"), pairs)

    fetched = [(t, t + 1, split_swap(probe_image, t, t + 1)) for t in depths[:-1:2]]
    half = probe_image.shape[0] // 2
    mine = lax.dynamic_slice_in_dim(probe_image, me[0] % 2 * half, half, 0)
    received = over_chips([probe_text] * len(chips))
    own = load_call(probe_text)
    mine, own, received[-1] = lax.optimization_barrier((mine, own, received[-1]))
    text_parts = over_plane(probe_text, received)
    text_parts[0] = own
    blocks = [block for _, _, block in fetched]
    last = depths[-1]
    mine = row_swap(mine, last)
    image_order = [(0, 0, None)]
    image_parts = [probe_image]

    columns = text_rows(list(text_parts), probe_text.shape[0])
    keep, send = panel_call(
        me, text_feats, image_feats, list(text_parts.values()), columns, n_row, groups, "image_panel"
    )
    send, mine, *blocks = lax.optimization_barrier((send, mine, *blocks))
    swapped = [col_swap(block, 1) for block in blocks]
    send, other, *swapped = lax.optimization_barrier((send, col_swap(mine, 1), *swapped))
    for (even, odd, _), block, twin in zip(fetched, blocks, swapped):
        image_order += [(even, odd, None), (odd, even, None)]
        image_parts += [block, twin]
    image_order += [(last, last, 0), (last, last, 1)]
    image_parts += [mine, other]
    own, *image_sends = sums_call("col", 1, chips, me, [keep, col_swap(send, 1)], "image_cores")
    own, *sends = sums_call("row", 0, depths, me, [own] + over_chips(image_sends), "image_plane")
    after_plane = sends[0]
    received = over_depth(sends)
    mine = last_call(own, received, BF16, "image_depth")
    parts = over_plane(mine)
    ipanel, gram = gram_call("col", list(parts), me, list(parts.values()), "image_gram")
    igrams = [gram] + over_depth([gram] * len(depths))

    rows = image_rows(image_order, probe_image.shape[0])
    keep, send = panel_call(me, image_feats, text_feats, image_parts, rows, groups, 1, "text_panel")
    swapped, _ = lax.optimization_barrier((col_swap(send, 1), image_sends[0]))
    own, *sends = sums_call("col", 0, chips, me, [keep, swapped], "text_cores")
    own, sends = own[0], [x[0] for x in sends]
    own, _ = lax.optimization_barrier((own, after_plane))
    mine = last_call(own, over_chips(sends), BF16, "text_plane")
    tpanel, gram = text_gram_call([mine] + over_depth([mine] * len(depths)))
    gram = last_call(gram, [col_swap(gram, 1)], F32, "text_gram_cores")
    tgrams = [gram] + over_chips([gram] * len(chips))

    return (
        finish_call(image_feats.shape[1], ipanel, igrams, "image_finish"),
        finish_call(text_feats.shape[1], tpanel, tgrams, "text_finish"),
    )


def solution(mesh):
    in_specs = (P(("row", "col"), None), P(("row", "col"), None), P("row", None), P("col", None))
    out_specs = (P("row", None), P("col", None))
    body = functools.partial(per_device, mesh.shape["row"], mesh.shape["col"])
    return jax.shard_map(body, mesh=mesh, in_specs=in_specs, out_specs=out_specs, check_vma=False)
```

```python
import functools
import math

import jax
import jax.numpy as jnp
from jax import lax
from jax.experimental import pallas as pl
from jax.experimental.pallas import tpu as pltpu
from jax.sharding import PartitionSpec as P

F32 = jnp.float32
BF16 = jnp.bfloat16
VMEM = pl.BlockSpec(memory_space=pltpu.VMEM)
SMEM = pl.BlockSpec(memory_space=pltpu.SMEM)
LIMIT = 32 * 1024 * 1024
PANEL_LIMIT = 46 * 1024 * 1024


def sds(shape, dtype):
    return jax.ShapeDtypeStruct(shape, dtype)


def params(**kw):
    return pltpu.CompilerParams(vmem_limit_bytes=LIMIT, **kw)


def cost(flops, nbytes):
    return pl.CostEstimate(flops=int(flops), bytes_accessed=int(nbytes), transcendentals=0)


def text_rows(shifts, depth):
    return lambda me_ref: [pl.multiple_of((me_ref[0] ^ s) * depth, depth) for s in shifts]


def image_rows(order, depth):
    def rows(me_ref):
        core = me_ref[0] % 2
        out = []
        for even, odd, half in order:
            at = (me_ref[1] ^ (even + core * (odd - even))) * depth
            if half is not None:
                at = pl.multiple_of(at + (core ^ half) * (depth // 2), depth // 2)
            else:
                at = pl.multiple_of(at, depth)
            out.append(at)
        return out

    return rows


def load_kernel(hbm_ref, out_ref, sem):
    move = pltpu.make_async_copy(hbm_ref, out_ref, sem)
    move.start()
    move.wait()


def load_call(x):
    return pl.pallas_call(
        load_kernel,
        in_specs=[pl.BlockSpec(memory_space=pltpu.HBM)],
        out_specs=VMEM,
        out_shape=sds(x.shape, x.dtype),
        scratch_shapes=[pltpu.SemaphoreType.DMA],
        compiler_params=params(),
        cost_estimate=cost(1, 4 * x.size),
        name="load",
    )(x)


def panel_kernel(rows, n, n_in, n_out, me_ref, a_hbm, b_hbm, *refs):
    parts, (keep_ref, send_ref, a_ref, b_ref, probe, a_sem, b_sem) = refs[:n], refs[n:]
    core = me_ref[0] % 2
    tall = a_ref.shape[0] // n_in
    cols = b_ref.shape[1] // n_out // 2
    moves = []
    for i in range(n_in):
        span = pl.ds(i * tall, tall)
        moves.append(pltpu.make_async_copy(a_hbm.at[span], a_ref.at[span], a_sem.at[i]))
    for i in range(n_out):
        span = pl.ds(2 * i * cols, 2 * cols)
        moves.append(pltpu.make_async_copy(b_hbm.at[:, span], b_ref.at[:, span], b_sem.at[i]))
    places = rows(me_ref)
    for move in moves:
        move.start()
    for at, part in zip(places, parts):
        probe[pl.ds(at, part.shape[0]), :] = part[...]
    sketches = []
    for i in range(n_in):
        moves[i].wait()
        chunk = a_ref[i * tall : i * tall + tall, :]
        sketches.append(jnp.dot(chunk, probe[...], preferred_element_type=F32))
    sketch = jnp.concatenate(sketches, axis=0).T.astype(BF16)
    for i in range(n_out):
        moves[n_in + i].wait()
        for rel, ref in ((0, keep_ref), (1, send_ref)):
            at = pl.multiple_of((2 * i + (core ^ rel)) * cols, cols)
            out = jnp.dot(sketch, b_ref[:, pl.ds(at, cols)], preferred_element_type=F32)
            ref[i] = out.T.reshape(ref.shape[1:])


def panel_call(me, a, b, parts, rows, blocks, pieces, name):
    pairs, width = b.shape
    rank = parts[0].shape[-1]
    out = sds((blocks, pieces, width // blocks // pieces // 2, rank), F32)
    hbm = pl.BlockSpec(memory_space=pltpu.HBM)
    n_in = 3 if pairs % 48 == 0 else 1
    return pl.pallas_call(
        functools.partial(panel_kernel, rows, len(parts), n_in, blocks),
        in_specs=[SMEM, hbm, hbm] + [VMEM] * len(parts),
        out_specs=[VMEM, VMEM],
        out_shape=[out, out],
        scratch_shapes=[
            pltpu.VMEM(a.shape, BF16),
            pltpu.VMEM(b.shape, BF16),
            pltpu.VMEM((a.shape[1], rank), BF16),
            pltpu.SemaphoreType.DMA((n_in,)),
            pltpu.SemaphoreType.DMA((blocks,)),
        ],
        compiler_params=pltpu.CompilerParams(vmem_limit_bytes=PANEL_LIMIT),
        cost_estimate=cost(1, 1),
        name=name,
    )(me, a, b, *parts)


def sums_kernel(which, axis, shifts, n, me_ref, *refs):
    terms, (own_ref, *sends) = refs[:n], refs[n:]
    spot = me_ref[1] if which == "row" else me_ref[0] // 2

    def total(i):
        at = (slice(None),) * axis + (i,)
        value = terms[0][at]
        for term in terms[1:]:
            value = value + term[at].astype(F32)
        return value

    own_ref[...] = total(spot)
    for s, ref in zip(shifts, sends):
        ref[...] = total(spot ^ s).astype(BF16)


def sums_call(which, axis, shifts, me, terms, name):
    shape = list(terms[0].shape)
    size = terms[0].size
    del shape[axis]
    return pl.pallas_call(
        functools.partial(sums_kernel, which, axis, shifts, len(terms)),
        in_specs=[SMEM] + [VMEM] * len(terms),
        out_specs=[VMEM] * (1 + len(shifts)),
        out_shape=[sds(shape, F32)] + [sds(shape, BF16)] * len(shifts),
        compiler_params=params(),
        cost_estimate=cost(size, 4 * size * len(terms)),
        name=name,
    )(me, *terms)


def last_kernel(own_ref, *refs):
    *recv, out_ref = refs
    value = own_ref[...]
    for ref in recv:
        value = value + ref[...].astype(F32)
    out_ref[...] = value.astype(out_ref.dtype)


def last_call(own, recv, dtype, name):
    return pl.pallas_call(
        last_kernel,
        in_specs=[VMEM] * (1 + len(recv)),
        out_specs=VMEM,
        out_shape=sds(own.shape, dtype),
        compiler_params=params(),
        cost_estimate=cost(own.size, 12 * own.size),
        name=name,
    )(own, *recv)


def pack(gram):
    half = gram.shape[0] // 2
    top, low = gram[:half], gram[half:]
    row = lax.broadcasted_iota(jnp.int32, top.shape, 0)
    lane = lax.broadcasted_iota(jnp.int32, top.shape, 1)
    body = jnp.where(row + half >= lane, low, pltpu.roll(top, half, 1))
    diagonal = jnp.sum(jnp.where(row == lane, top, 0.0), axis=0, keepdims=True)
    return jnp.concatenate([body, jnp.broadcast_to(diagonal, (8, gram.shape[1]))], axis=0)


def unpack(packed):
    half = packed.shape[0] - 8
    body, diagonal = packed[:half], packed[half : half + 1]
    row = lax.broadcasted_iota(jnp.int32, body.shape, 0)
    lane = lax.broadcasted_iota(jnp.int32, body.shape, 1)
    upper = jnp.where(jnp.logical_and(lane < half, row < lane), pltpu.roll(body, half, 1), 0.0)
    lower = jnp.where(row + half > lane, body, 0.0)
    strict = jnp.concatenate([upper, lower], axis=0)
    first = jnp.where(row == lane, jnp.broadcast_to(diagonal, body.shape), 0.0)
    last = jnp.where(row + half == lane, body, 0.0)
    return strict + strict.T + jnp.concatenate([first, last], axis=0)


def gram_kernel(which, order, me_ref, *refs):
    parts, (panel_ref, gram_ref) = refs[: len(order)], refs[len(order) :]
    for s, part in zip(order, parts):
        if which == "row":
            panel_ref[me_ref[1] ^ s] = part[...]
        else:
            spot = me_ref[0] ^ s
            panel_ref[spot % 2 * (len(order) // 2) + spot // 2] = part[...]
    panel = panel_ref[...].reshape(-1, gram_ref.shape[1])
    gram = lax.dot_general(panel, panel, (((0,), (0,)), ((), ())), preferred_element_type=F32)
    gram_ref[...] = pack(gram)


def gram_call(which, order, me, parts, name):
    n = len(parts)
    rows, rank = parts[0].shape
    return pl.pallas_call(
        functools.partial(gram_kernel, which, order),
        in_specs=[SMEM] + [VMEM] * n,
        out_specs=[VMEM, VMEM],
        out_shape=[sds((n, rows, rank), BF16), sds((rank // 2 + 8, rank), F32)],
        compiler_params=params(),
        cost_estimate=cost(2 * n * rows * rank * rank, 4 * n * rows * rank),
        name=name,
    )(me, *parts)


def tree_sum(values):
    while len(values) > 1:
        values = [x + y for x, y in zip(values[::2], values[1::2])]
    return values[0]


def text_gram_kernel(*refs):
    *parts, panel_ref, gram_ref = refs
    panel = tree_sum([part[...].astype(F32) for part in parts]).astype(BF16)
    panel_ref[0] = panel
    gram = lax.dot_general(panel, panel, (((0,), (0,)), ((), ())), preferred_element_type=F32)
    gram_ref[...] = pack(gram)


def text_gram_call(parts):
    rows, rank = parts[0].shape
    return pl.pallas_call(
        text_gram_kernel,
        in_specs=[VMEM] * len(parts),
        out_specs=[VMEM, VMEM],
        out_shape=[sds((1, rows, rank), BF16), sds((rank // 2 + 8, rank), F32)],
        compiler_params=params(),
        cost_estimate=cost(2 * rows * rank * rank, 4 * rows * rank),
        name="text_gram",
    )(*parts)


def inverse_factor(gram):
    n = gram.shape[0]
    lane = lax.broadcasted_iota(jnp.int32, (8, n), 1)
    sub = lax.broadcasted_iota(jnp.int32, (8, n), 0)
    rows = [gram[8 * i : 8 * i + 8, :] for i in range(n // 8)]
    for b in range(n // 8):
        cols = [
            [jnp.broadcast_to(rows[i][:, 8 * b + j : 8 * b + j + 1], (8, n)) for i in range(b, n // 8)]
            for j in range(8)
        ]
        scale = jnp.ones((8, n), F32)
        for j in range(8):
            k = 8 * b + j
            pivot = jnp.broadcast_to(cols[j][0][j : j + 1, :], (8, n))
            guess = pl.reciprocal(pivot, approx=True)
            inv = guess * (2.0 - pivot * guess)
            scale = jnp.where(sub == j, pivot, scale)
            pivot_row = jnp.where(lane == k, 1.0, jnp.broadcast_to(rows[b][j : j + 1, :], (8, n)))
            below = sub > j
            mult = [c * inv for c in cols[j]]
            mult[0] = jnp.where(below, mult[0], 0.0)
            for jj in range(j + 1, 8):
                entry = jnp.broadcast_to(cols[jj][0][j : j + 1, :], (8, n))
                cols[jj] = [c - m * entry for c, m in zip(cols[jj], mult)]
            for i in range(b, n // 8):
                here = lane == k
                if i == b:
                    here = jnp.logical_and(here, below)
                rows[i] = jnp.where(here, 0.0, rows[i]) - mult[i - b] * pivot_row
            yield None
        unit = jnp.where(lane == sub + 8 * b, 1.0, jnp.where(lane < sub + 8 * b, rows[b], 0.0))
        rows[b] = unit * lax.rsqrt(scale)
        yield None
    yield jnp.concatenate(rows, axis=0)


def finish_kernel(widths, n_image, ipanel, tpanel, *refs):
    *grams, iout, tout = refs

    def total(refs):
        value = refs[0][...]
        for ref in refs[1:]:
            value = value + ref[...]
        return unpack(value)

    inverses = None
    for inverses in zip(inverse_factor(total(grams[:n_image])), inverse_factor(total(grams[n_image:]))):
        pass
    dims = (((1,), (1,)), ((), ()))
    for inverse, width, panel_ref, out_ref in zip(inverses, widths, (ipanel, tpanel), (iout, tout)):
        inverse = inverse * math.sqrt(width)
        high = inverse.astype(BF16)
        low = (inverse - high.astype(F32)).astype(BF16)
        panel = panel_ref[...].reshape(out_ref.shape)
        panel = jnp.concatenate([panel, panel], axis=1)
        both = jnp.concatenate([high, low], axis=1)
        out_ref[...] = lax.dot_general(panel, both, dims, preferred_element_type=F32)


def finish_call(widths, ipanel, igrams, tpanel, tgrams):
    rank = ipanel.shape[-1]
    outs = [sds((math.prod(p.shape[:-1]), rank), F32) for p in (ipanel, tpanel)]
    return pl.pallas_call(
        functools.partial(finish_kernel, widths, len(igrams)),
        in_specs=[VMEM] * (2 + len(igrams) + len(tgrams)),
        out_specs=[VMEM] * 2,
        out_shape=outs,
        compiler_params=params(),
        cost_estimate=cost(10**10, 6 * ipanel.size),
        name="finish",
    )(ipanel, tpanel, *igrams, *tgrams)


def per_device(n_row, n_col, image_feats, text_feats, probe_image, probe_text):
    groups = n_col // 2
    me = jnp.stack([lax.axis_index("col"), lax.axis_index("row")]).astype(jnp.int32)
    col_swap = lambda x, s: lax.ppermute(x, "col", [(i, i ^ s) for i in range(n_col)])
    row_swap = lambda x, s: lax.ppermute(x, "row", [(i, i ^ s) for i in range(n_row)])
    chips, depths = list(range(1, groups)), list(range(1, n_row))
    over_chips = lambda xs: [col_swap(x, 2 * s) for x, s in zip(xs, chips)]
    over_depth = lambda xs: [row_swap(x, t) for x, t in zip(xs, depths)]

    def over_plane(x, received=None):
        got = {0: x}
        for s, block in zip(chips, received or over_chips([x] * len(chips))):
            got[2 * s] = block
        for s in list(got):
            got[s ^ 1] = col_swap(got[s], 1)
        return got

    def split_swap(x, even, odd):
        pairs = []
        for r in range(n_row):
            for c in range(n_col):
                pairs.append((r * n_col + c, (r ^ (odd if c % 2 else even)) * n_col + c))
        return lax.ppermute(x, ("row", "col"), pairs)

    fetched = [(t, t + 1, split_swap(probe_image, t, t + 1)) for t in depths[:-1:2]]
    half = probe_image.shape[0] // 2
    mine = lax.dynamic_slice_in_dim(probe_image, me[0] % 2 * half, half, 0)
    received = over_chips([probe_text] * len(chips))
    own = load_call(probe_text)
    mine, own, received[-1] = lax.optimization_barrier((mine, own, received[-1]))
    text_parts = over_plane(probe_text, received)
    text_parts[0] = own
    blocks = [block for _, _, block in fetched]
    last = depths[-1]
    mine = row_swap(mine, last)
    image_order = [(0, 0, None)]
    image_parts = [probe_image]

    columns = text_rows(list(text_parts), probe_text.shape[0])
    keep, send = panel_call(
        me, text_feats, image_feats, list(text_parts.values()), columns, n_row, groups, "image_panel"
    )
    send, mine, *blocks = lax.optimization_barrier((send, mine, *blocks))
    swapped = [col_swap(block, 1) for block in blocks]
    send, other, *swapped = lax.optimization_barrier((send, col_swap(mine, 1), *swapped))
    for (even, odd, _), block, twin in zip(fetched, blocks, swapped):
        image_order += [(even, odd, None), (odd, even, None)]
        image_parts += [block, twin]
    image_order += [(last, last, 0), (last, last, 1)]
    image_parts += [mine, other]
    own, *image_sends = sums_call("col", 1, chips, me, [keep, col_swap(send, 1)], "image_cores")
    own, *sends = sums_call("row", 0, depths, me, [own] + over_chips(image_sends), "image_plane")
    after_plane = sends[0]
    received = over_depth(sends)
    mine = last_call(own, received, BF16, "image_depth")
    parts = over_plane(mine)
    ipanel, gram = gram_call("col", list(parts), me, list(parts.values()), "image_gram")
    igrams = [gram] + over_depth([gram] * len(depths))

    rows = image_rows(image_order, probe_image.shape[0])
    keep, send = panel_call(me, image_feats, text_feats, image_parts, rows, groups, 1, "text_panel")
    swapped, _ = lax.optimization_barrier((col_swap(send, 1), image_sends[0]))
    own, *sends = sums_call("col", 0, chips, me, [keep, swapped], "text_cores")
    own, sends = own[0], [x[0] for x in sends]
    own, _ = lax.optimization_barrier((own, after_plane))
    mine = last_call(own, over_chips(sends), BF16, "text_plane")
    tpanel, gram = text_gram_call([mine] + over_depth([mine] * len(depths)))
    gram = last_call(gram, [col_swap(gram, 1)], F32, "text_gram_cores")
    tgrams = [gram] + over_chips([gram] * len(chips))

    widths = (image_feats.shape[1], text_feats.shape[1])
    return finish_call(widths, ipanel, igrams, tpanel, tgrams)


def solution(mesh):
    in_specs = (P(("row", "col"), None), P(("row", "col"), None), P("row", None), P("col", None))
    out_specs = (P("row", None), P("col", None))
    body = functools.partial(per_device, mesh.shape["row"], mesh.shape["col"])
    return jax.shard_map(body, mesh=mesh, in_specs=in_specs, out_specs=out_specs, check_vma=False)
```
